32 devices in a mesh: macro: 16 (over z, x, core), vox: 2 (over y).
Axes of the slice: x: 2, y: 2, z: 4, core: 2. Of those that a mesh axis runs over, the one named last changes fastest.
Arguments:
- nodal_disp: float32 [16, 3], P('macro'), may hold values from -6 to 6
- weighted_shape_gradients: float32 [16, 3, 8], P('macro'), may hold values from -2 to 2
- rve_element: int32 [16], replicated, may hold values from 0 to 1, as said below
- connectivity: int32 [2, 8], replicated, may hold values from 0 to 15, as said below
- block_slot: int32 [2, 8, 8], replicated, may hold values from 0 to 11, as said below
- stiffness: float32 [16, 64, 4096], P('macro', 'vox'), may hold values from 0.2 to 1
- yielded_mask: int32 [16, 64, 4096], P('macro', 'vox'), may hold values 0 or 1
Outputs:
- voxel_stress: float32 [16, 6, 64, 4096], P('macro', None, 'vox')
- homogenized_stress: float32 [16, 6], P('macro')
- macro_strain: float32 [16, 6], P('macro')
- internal_node_force: float32 [16, 3], P('macro')
- tangent: float32 [16, 108], P('macro')
The draws below stay inside these ranges and needn't reach their ends.
Inputs may be any that keep to these rules, and one draw needn't show every extreme that they name: `rve_element`: each element number is named by exactly 8 RVEs. `connectivity`: the elements form a strip of hexahedra: element e and e + 1 share four corner nodes; distinct mesh nodes have distinct numbers. `block_slot`: a node pair gets the same slot wherever it appears; the neighbours of one node get distinct slots.
All inputs are finite; a program needn't handle non-finite values. No bound on the sum of `yielded_mask` on one device may be relied on, other than what follows from the above.
Results may differ from the reference program's by a relative error of at most 0.0003.
Values sent between devices are 32-bit elements; how exact they have to be, the bound alone decides.
No kernel may reach another device: no remote copies, remote signals or barrier semaphores. Data moves between devices by JAX's collectives and lax.ppermute only.
A program may use at most 64 MiB of HBM per device.

```python
import math
import jax
import jax.numpy as jnp
import numpy as np
from jax import lax

EDGE = 64
SWEEPS = 3
NEIGHBOUR_SLOTS = 12
POINTS = 16
ELEMS = 2
MACRO_NODE_COUNT = 16


def strip_positions():
    corner_x = np.array([0, 1, 1, 0, 0, 1, 1, 0])
    corner_c = np.array([0, 0, 1, 1, 2, 2, 3, 3])
    return (corner_x, corner_c)


def draw_rve_element(key, part):
    key = jax.random.fold_in(key, 11)
    return (jax.random.permutation(key, POINTS) // 8).astype(jnp.int32)


def draw_connectivity(key, part):
    key = jax.random.fold_in(key, 12)
    count = 4 * (ELEMS + 1)
    corner_x, corner_c = strip_positions()
    order = jax.random.permutation(key, count)
    numbers = order * (MACRO_NODE_COUNT - 1) // (count - 1)
    places = 4 * (jnp.arange(ELEMS)[:, None] + jnp.array(corner_x)[None, :]) + jnp.array(corner_c)[None, :]
    return numbers[places].astype(jnp.int32)


def draw_block_slot(key, part):
    key = jax.random.fold_in(key, 13)
    count = 4 * (ELEMS + 1)
    corner_x, corner_c = strip_positions()
    keys = jax.random.split(key, count)
    orders = jax.vmap(lambda single: jax.random.permutation(single, NEIGHBOUR_SLOTS))(keys)
    places = 4 * (jnp.arange(ELEMS)[:, None] + jnp.array(corner_x)[None, :]) + jnp.array(corner_c)[None, :]
    codes = 4 * (corner_x[None, :] - corner_x[:, None] + 1) + corner_c[None, :]
    return orders[places[:, :, None], jnp.array(codes)[None, :, :]].astype(jnp.int32)


def set_ends(result, rng, least, high):
    extent = result.shape
    place = [jax.random.randint(jax.random.fold_in(rng, axis), (), 0, extent[axis]) for axis in range(len(extent))]
    result = result.at[tuple(place)].set(least)
    longest = extent.index(max(extent))
    place[longest] = (place[longest] + 1) % extent[longest]
    return result.at[tuple(place)].set(high)


def steps_of(key, dims, cuts, least, top_value):
    loudness, own = 1.0, jax.random.fold_in(key, 6)
    for axis_at, blocks in cuts:
        draws = jnp.exp(jax.random.uniform(jax.random.fold_in(own, axis_at), (blocks,), jnp.float32, least / len(cuts), top_value / len(cuts)))
        loudness = loudness * jnp.repeat(draws, dims[axis_at] // blocks).reshape([-1 if axis == axis_at else 1 for axis in range(len(dims))])
    return loudness


def normal_values(stream_key, shape, width, most, cuts=(), kind=jnp.bfloat16):
    level = steps_of(stream_key, shape, cuts, -0.22, 0.18) if cuts else 1.0
    entries = jax.random.normal(stream_key, shape, jnp.float32) * width * level
    return jnp.minimum(jnp.maximum(entries, -most), most).astype(kind)


def setup_inputs(seed: int = 0) -> dict:
    seeds = jax.random.split(jax.random.key(seed), 8)
    return {
        "nodal_disp": normal_values(seeds[0], (MACRO_NODE_COUNT, 3), 1.0, 6.0, ((0, 16),), jnp.float32),
        "weighted_shape_gradients": normal_values(seeds[1], (POINTS, 3, 8), 8 ** -0.5, 2.0, ((0, 16),), jnp.float32),
        "rve_element": draw_rve_element(jax.random.fold_in(seeds[7], 71), 0),
        "connectivity": draw_connectivity(jax.random.fold_in(seeds[7], 71), 0),
        "block_slot": draw_block_slot(jax.random.fold_in(seeds[7], 71), 0),
        "stiffness": jnp.clip(jnp.exp(math.log(1.0) - 1.609438 * jax.random.uniform(seeds[5], (POINTS, EDGE, EDGE * EDGE), jnp.float32) ** steps_of(seeds[5], (POINTS, EDGE, EDGE * EDGE), ((0, 16), (1, 2)), -0.2, 0.2)), 0.2, 1.0),
        "yielded_mask": set_ends((jax.random.randint(seeds[6], (POINTS, EDGE, EDGE * EDGE), 0, 3) < 1).astype(jnp.int32), jax.random.fold_in(seeds[6], 1), 0, 1),
    }


lame_base = 1.5
shear_base = 1.0
yield_ratio = 0.2
precond = 1.0 / 42.0
lower_bound = 0.05
upper_bound = 2.0
largest_value = lax.Precision.HIGHEST


def chebyshev_terms(count):
    centre = 0.5 * (upper_bound + lower_bound)
    half_width = 0.5 * (upper_bound - lower_bound)
    ratio_bound = centre / half_width
    rho_prev = 1.0 / ratio_bound
    weights = []
    for number in range(count):
        rho_next = 1.0 / (2.0 * ratio_bound - rho_prev)
        weights.append((rho_next * rho_prev, 2.0 * rho_next / half_width))
        rho_prev = rho_next
    return centre, weights


def ahead(field, axis):
    return jnp.roll(field, -1, axis=axis) - field


def behind(field, axis):
    return field - jnp.roll(field, 1, axis=axis)


def plane_diff(field):
    return field[..., 1:, :, :] - field[..., :-1, :, :]


def head_planes(field):
    return field[..., :-1, :, :]


def tail_diff(field, axis):
    return behind(field[..., 1:, :, :], axis)


def stress_field(displace, lame_win, shear_win, strain_tensor):
    disp_x = displace[..., 0, :, :, :]
    disp_y = displace[..., 1, :, :, :]
    disp_z = displace[..., 2, :, :, :]
    macro = [strain_tensor[..., k, None, None, None] for k in range(6)]
    normal_xx = macro[0] + plane_diff(disp_x)
    normal_yy = macro[1] + ahead(head_planes(disp_y), -2)
    normal_zz = macro[2] + ahead(head_planes(disp_z), -1)
    shear_yz = macro[3] + ahead(head_planes(disp_y), -1) + ahead(head_planes(disp_z), -2)
    shear_xz = macro[4] + ahead(head_planes(disp_x), -1) + plane_diff(disp_z)
    shear_xy = macro[5] + ahead(head_planes(disp_x), -2) + plane_diff(disp_y)
    volume = normal_xx + normal_yy + normal_zz
    return jnp.stack([lame_win * volume + 2.0 * shear_win * normal_xx,
                      lame_win * volume + 2.0 * shear_win * normal_yy,
                      lame_win * volume + 2.0 * shear_win * normal_zz,
                      shear_win * shear_yz, shear_win * shear_xz, shear_win * shear_xy], axis=-4)


def divergence(stress):
    stress_xx = stress[..., 0, :, :, :]
    stress_yy = stress[..., 1, :, :, :]
    stress_zz = stress[..., 2, :, :, :]
    stress_yz = stress[..., 3, :, :, :]
    stress_xz = stress[..., 4, :, :, :]
    stress_xy = stress[..., 5, :, :, :]
    force_x = plane_diff(stress_xx) + tail_diff(stress_xy, -2) + tail_diff(stress_xz, -1)
    force_y = plane_diff(stress_xy) + tail_diff(stress_yy, -2) + tail_diff(stress_yz, -1)
    force_z = plane_diff(stress_xz) + tail_diff(stress_yz, -2) + tail_diff(stress_zz, -1)
    return jnp.stack([force_x, force_y, force_z], axis=-4)


def macro_strain_of(shape_gradient, element_disp):
    grad_x = shape_gradient[:, 0]
    grad_y = shape_gradient[:, 1]
    grad_z = shape_gradient[:, 2]
    move_x = element_disp[:, :, 0]
    move_y = element_disp[:, :, 1]
    move_z = element_disp[:, :, 2]
    return jnp.stack([jnp.sum(grad_x * move_x, axis=1), jnp.sum(grad_y * move_y, axis=1),
                      jnp.sum(grad_z * move_z, axis=1),
                      jnp.sum(grad_z * move_y + grad_y * move_z, axis=1),
                      jnp.sum(grad_z * move_x + grad_x * move_z, axis=1),
                      jnp.sum(grad_y * move_x + grad_x * move_y, axis=1)], axis=1)


def strain_matrix(shape_gradient):
    grad_x = shape_gradient[:, 0]
    grad_y = shape_gradient[:, 1]
    grad_z = shape_gradient[:, 2]
    blank = jnp.zeros_like(grad_x)
    layout = [[grad_x, blank, blank], [blank, grad_y, blank], [blank, blank, grad_z],
              [blank, grad_z, grad_y], [grad_z, blank, grad_x], [grad_y, grad_x, blank]]
    return jnp.stack([jnp.stack(entry, axis=-1) for entry in layout], axis=-2)


def tangent_matrix(average_lame, average_shear):
    normal_mask = jnp.concatenate([jnp.ones((3,), jnp.float32), jnp.zeros((3,), jnp.float32)])
    eye_full = jnp.eye(6, dtype=jnp.float32)
    return (average_lame[:, None, None] * (normal_mask[:, None] * normal_mask[None, :])[None]
            + average_shear[:, None, None] * (eye_full * (1.0 + normal_mask)[None, :])[None])


def element_contrib(shape_gradient, homogenized, average_lame, average_shear):
    strain_operator = strain_matrix(shape_gradient)
    moduli = tangent_matrix(average_lame, average_shear)
    node_forces = jnp.einsum('dufh,df->duh', strain_operator, homogenized, precision=largest_value)
    inner_prod = jnp.einsum('pvw,plwb->plvb', moduli, strain_operator, precision=largest_value)
    tangent_blocks = jnp.einsum('pkva,plvb->pklab', strain_operator, inner_prod, precision=largest_value)
    return node_forces, tangent_blocks.reshape(tangent_blocks.shape[0], 8, 8, 9)


def solve_unit_cell(items):
    stiff_block, plastic_block, strain_tensor = items
    stiff_cube = stiff_block.reshape(EDGE, EDGE, EDGE)
    yielded = plastic_block.reshape(EDGE, EDGE, EDGE)
    lame_field = lame_base * stiff_cube
    shear_field = shear_base * stiff_cube * jnp.where(yielded == 1, yield_ratio, 1.0)
    lame_win = jnp.concatenate([lame_field[-1:], lame_field], axis=0)
    shear_win = jnp.concatenate([shear_field[-1:], shear_field], axis=0)
    centre, weights = chebyshev_terms(SWEEPS - 1)

    def residual(displace):
        window = jnp.concatenate([displace[:, -1:], displace, displace[:, :1]], axis=1)
        return divergence(stress_field(window, lame_win, shear_win, strain_tensor))

    zero_disp = jnp.zeros((3, EDGE, EDGE, EDGE), jnp.float32)
    direction = residual(zero_disp) * (precond / centre)
    displace = direction
    for keep_coef, push_coef in weights:
        direction = keep_coef * direction + push_coef * (precond * residual(displace))
        displace = displace + direction
    window = jnp.concatenate([displace, displace[:, :1]], axis=1)
    stress = stress_field(window, lame_field, shear_field, strain_tensor)
    return (stress.reshape(6, EDGE, EDGE * EDGE), jnp.mean(stress, axis=(1, 2, 3)),
            jnp.mean(lame_field), jnp.mean(shear_field))


def reference(nodal_disp, weighted_shape_gradients, rve_element, connectivity, block_slot, stiffness, yielded_mask):
    point_nodes = connectivity[rve_element]
    strain_tensor = macro_strain_of(weighted_shape_gradients, nodal_disp[point_nodes])
    voxel_stress, homogenized_stress, average_lame, average_shear = lax.map(solve_unit_cell, (stiffness, yielded_mask, strain_tensor))
    node_forces, tangent_blocks = element_contrib(weighted_shape_gradients, homogenized_stress, average_lame, average_shear)
    point_slots = block_slot[rve_element]
    tangent = jnp.zeros((MACRO_NODE_COUNT, NEIGHBOUR_SLOTS, 9), jnp.float32).at[point_nodes[:, :, None], point_slots].add(tangent_blocks)
    internal_node_force = jnp.zeros((MACRO_NODE_COUNT, 3), jnp.float32).at[point_nodes].add(node_forces)
    return voxel_stress, homogenized_stress, strain_tensor, internal_node_force, tangent.reshape(MACRO_NODE_COUNT, NEIGHBOUR_SLOTS * 9)
```

```python
import functools

import jax
import jax.numpy as jnp
from jax import lax
from jax.experimental import pallas as pl
from jax.experimental.pallas import tpu as pltpu
from jax.sharding import PartitionSpec as P

EDGE = 64
SWEEPS = 3
NEIGHBOUR_SLOTS = 12
BLOCK = NEIGHBOUR_SLOTS * 9

lame_base = 1.5
shear_base = 1.0
yield_ratio = 0.2
precond = 1.0 / 42.0
lower_bound = 0.05
upper_bound = 2.0

ROWS = EDGE * EDGE // 128
HALO = 3


def chebyshev_terms(count):
    centre = 0.5 * (upper_bound + lower_bound)
    half_width = 0.5 * (upper_bound - lower_bound)
    ratio_bound = centre / half_width
    rho_prev = 1.0 / ratio_bound
    weights = []
    for number in range(count):
        rho_next = 1.0 / (2.0 * ratio_bound - rho_prev)
        weights.append((rho_next * rho_prev, 2.0 * rho_next / half_width))
        rho_prev = rho_next
    return (centre, weights)


centre, ((keep1, push1), (keep2, push2)) = chebyshev_terms(SWEEPS - 1)
gain1 = push1 * precond
gain2 = push2 * precond


def lanes():
    return lax.broadcasted_iota(jnp.int32, (ROWS, 128), 1)


def swap(x):
    return pltpu.roll(x, 64, 1)


def next_row(y):
    after = jnp.concatenate([y[8:], pltpu.roll(y[:8], 7, 0)], axis=0)
    return jnp.where(lanes() < 64, y, after)


def prev_row(y):
    before = jnp.concatenate([pltpu.roll(y[24:], 1, 0), y[:24]], axis=0)
    return jnp.where(lanes() < 64, before, y)


def next_lane(x, y):
    return pltpu.roll(jnp.where((lanes() & 63) == 0, y, x), 127, 1)


def prev_lane(x, y):
    return pltpu.roll(jnp.where((lanes() & 63) == 63, y, x), 1, 1)


def plane_stress(w, above, lame, shear, strain):
    w0, w1, w2 = w
    n0, n1, n2 = above
    y0, y1, y2 = swap(w0), swap(w1), swap(w2)
    e0 = (n0 - w0) + strain[0]
    e1 = (next_row(y1) - w1) + strain[1]
    e2 = (next_lane(w2, y2) - w2) + strain[2]
    g3 = (next_lane(w1, y1) + next_row(y2)) - (w1 + w2) + strain[3]
    g4 = (next_lane(w0, y0) + n2) - (w0 + w2) + strain[4]
    g5 = (next_row(y0) + n1) - (w0 + w1) + strain[5]
    bulk = lame * (e0 + e1 + e2)
    twice = shear + shear
    return (
        bulk + twice * e0,
        bulk + twice * e1,
        bulk + twice * e2,
        shear * g3,
        shear * g4,
        shear * g5,
    )


def uniform_stress(lame, shear, strain):
    bulk = lame * (strain[0] + strain[1] + strain[2])
    return (
        bulk + shear * (2.0 * strain[0]),
        bulk + shear * (2.0 * strain[1]),
        bulk + shear * (2.0 * strain[2]),
        shear * strain[3],
        shear * strain[4],
        shear * strain[5],
    )


def plane_divergence(stress, below):
    xx, yy, zz, yz, xz, xy = stress
    pxx, pxz, pxy = below
    yyz = swap(yz)
    r0 = (xx - pxx) + (xy - prev_row(swap(xy))) + (xz - prev_lane(xz, swap(xz)))
    r1 = (xy - pxy) + (yy - prev_row(swap(yy))) + (yz - prev_lane(yz, yyz))
    r2 = (xz - pxz) + (yz - prev_row(yyz)) + (zz - prev_lane(zz, swap(zz)))
    return r0, r1, r2


def slab_kernel(
    step,
    gathered,
    rve_element,
    connectivity,
    stiff_ref,
    mask_ref,
    halo_ref,
    stress_ref,
    strain_ref,
    sums_ref,
    lame_v,
    shear_v,
    w1_v,
    w2_v,
    w3_v,
    carry_v,
    out_v,
    sem,
):
    planes = stiff_ref.shape[0] // ROWS
    point = lax.axis_index("macro")
    elem = rve_element[point]

    grads = [[gathered[point, 3 + c * 8 + k] for k in range(8)] for c in range(3)]
    nodes = [connectivity[elem, k] for k in range(8)]
    moves = [[gathered[n, a] for n in nodes] for a in range(3)]

    def dot(c, a):
        total = grads[c][0] * moves[a][0]
        for k in range(1, 8):
            total = total + grads[c][k] * moves[a][k]
        return total

    strain = [
        dot(0, 0),
        dot(1, 1),
        dot(2, 2),
        dot(2, 1) + dot(1, 2),
        dot(2, 0) + dot(0, 2),
        dot(1, 0) + dot(0, 1),
    ]
    for c in range(6):
        strain_ref[0, c] = strain[c]

    def native(p8, s, q):
        return pl.ds(p8 * (8 * ROWS) + s + 8 * q, 8, stride=ROWS)

    def load_material(g, acc):
        acc_s, acc_m = acc
        for s in range(8):
            stiff = jnp.concatenate([stiff_ref[native(g, s, q), :] for q in range(4)], axis=0)
            mask = jnp.concatenate([mask_ref[native(g, s, q), :] for q in range(4)], axis=0)
            shear = stiff * jnp.where(mask == 1, shear_base * yield_ratio, shear_base)
            lame = lame_base * stiff
            lame_v[g * 8 + s + HALO] = lame
            shear_v[g * 8 + s + HALO] = shear
            acc_s = acc_s + lame
            acc_m = acc_m + shear
        return acc_s, acc_m

    zero = jnp.zeros((ROWS, 128), jnp.float32)
    lame_sum, shear_sum = lax.fori_loop(0, planes // 8, load_material, (zero, zero))
    for side in range(2):
        for h in range(HALO):
            at = h if side == 0 else HALO + planes + h
            parts = []
            for f in range(2):
                base = ((side * 2 + f) * HALO + h) * ROWS
                parts.append(
                    jnp.concatenate(
                        [halo_ref[pl.ds(base + q, 8, stride=4), :] for q in range(4)], axis=0
                    )
                )
            lame_v[at] = lame_base * parts[0]
            shear_v[at] = parts[1]

    scale1 = gain1 * gain2 * precond / centre
    strain1 = [scale1 * e for e in strain]

    def put_carry(stress):
        carry_v[0] = stress[0]
        carry_v[1] = stress[4]
        carry_v[2] = stress[5]

    def get_carry():
        return carry_v[0], carry_v[1], carry_v[2]

    def pick(stress):
        return stress[0], stress[4], stress[5]

    put_carry(uniform_stress(lame_v[0], shear_v[0], strain1))

    def sweep1(t, _):
        below = get_carry()
        for u in range(step):
            at = t * step + 1 + u
            stress = uniform_stress(lame_v[at], shear_v[at], strain1)
            r = plane_divergence(stress, below)
            for c in range(3):
                w1_v[c, at] = r[c]
            below = pick(stress)
        put_carry(stress)
        return 0

    lax.fori_loop(0, pl.cdiv(planes + 5, step), sweep1, 0)

    def load3(ref, at):
        return ref[0, at], ref[1, at], ref[2, at]

    strain2 = [gain1 * gain2 * e for e in strain]
    ratio1 = (1.0 + keep1) / gain1
    put_carry(
        plane_stress(load3(w1_v, 1), load3(w1_v, 2), lame_v[1], shear_v[1], strain2)
    )

    def sweep2(t, _):
        below = get_carry()
        w = load3(w1_v, t * step + 2)
        for u in range(step):
            at = t * step + 2 + u
            above = load3(w1_v, at + 1)
            stress = plane_stress(w, above, lame_v[at], shear_v[at], strain2)
            r = plane_divergence(stress, below)
            for c in range(3):
                w2_v[c, at] = ratio1 * w[c] + r[c]
            below = pick(stress)
            w = above
        put_carry(stress)
        return 0

    lax.fori_loop(0, pl.cdiv(planes + 3, step), sweep2, 0)

    strain3 = [gain2 * e for e in strain]
    ratio2 = (1.0 + keep2) / gain2
    ratio3 = keep2 / (gain1 * gain2)
    put_carry(
        plane_stress(load3(w2_v, 2), load3(w2_v, 3), lame_v[2], shear_v[2], strain3)
    )

    def sweep3(t, _):
        below = get_carry()
        w = load3(w2_v, t * step + 3)
        for u in range(step):
            at = t * step + 3 + u
            above = load3(w2_v, at + 1)
            stress = plane_stress(w, above, lame_v[at], shear_v[at], strain3)
            r = plane_divergence(stress, below)
            for c in range(3):
                w3_v[c, at] = ratio2 * w[c] - ratio3 * w1_v[c, at] + r[c]
            below = pick(stress)
            w = above
        put_carry(stress)
        return 0

    lax.fori_loop(0, pl.cdiv(planes + 1, step), sweep3, 0)

    def put_out(g):
        span = pl.ds(pl.multiple_of(g * (8 * ROWS), 8 * ROWS), 8 * ROWS)
        return pltpu.make_async_copy(out_v.at[:, span, :], stress_ref.at[:, span, :], sem)

    def final(g, acc):
        acc = list(acc)
        w = load3(w3_v, g * 8 + HALO)
        for s in range(8):
            at = g * 8 + s + HALO
            above = load3(w3_v, at + 1)
            stress = plane_stress(w, above, lame_v[at], shear_v[at], strain)
            for c in range(6):
                acc[c] = acc[c] + (
                    (stress[c][:8] + stress[c][8:16]) + (stress[c][16:24] + stress[c][24:])
                )
                for q in range(4):
                    out_v[c, native(g, s, q), :] = stress[c][8 * q : 8 * q + 8]
            w = above
        put_out(g).start()
        return tuple(acc)

    small = jnp.zeros((8, 128), jnp.float32)
    acc = lax.fori_loop(0, planes // 8, final, (small,) * 6)

    totals = list(acc)
    for big in (lame_sum, shear_sum):
        totals.append((big[:8] + big[8:16]) + (big[16:24] + big[24:]))
    at_lane = lax.broadcasted_iota(jnp.int32, sums_ref.shape, 1)
    row = jnp.zeros(sums_ref.shape, jnp.float32)
    for c in range(8):
        row = jnp.where(at_lane == c, jnp.sum(totals[c], axis=(0, 1), keepdims=True), row)
    sums_ref[...] = row

    def drain(g, _):
        put_out(g).wait()
        return 0

    lax.fori_loop(0, planes // 8, drain, 0)


def node_kernel(
    sums_ref,
    gathered_ref,
    elem_ref,
    connectivity,
    block_slot,
    hom_ref,
    force_ref,
    tangent_ref,
):
    points = gathered_ref.shape[0]
    elems = connectivity.shape[0]
    own = lax.axis_index("macro")
    scale = 1.0 / float(EDGE * EDGE * EDGE)
    means = sums_ref[0]
    for v in range(1, sums_ref.shape[0]):
        means = means + sums_ref[v]
    means = means * scale

    def col(x, c):
        return x[:, c : c + 1]

    place = lax.broadcasted_iota(jnp.int32, means.shape, 0)
    hom_ref[...] = jnp.sum(jnp.where(place == own, means, 0.0), axis=0, keepdims=True)[:, :6]

    grads = gathered_ref[...]
    elem = elem_ref[...]
    corner = jnp.full(elem.shape, -1, jnp.int32)
    slots = [jnp.full(elem.shape, -1, jnp.int32) for l in range(8)]
    for e in range(elems):
        at = jnp.int32(-1)
        for k in range(8):
            at = jnp.where(connectivity[e, k] == own, k, at)
        here = elem == e
        corner = jnp.where(here, at, corner)
        safe = jnp.maximum(at, 0)
        for l in range(8):
            slots[l] = jnp.where(here, block_slot[e, safe * 8 + l], slots[l])
    lane = lax.broadcasted_iota(jnp.int32, grads.shape, 1)
    mine = []
    for c in range(3):
        hit = (lane == corner + (3 + 8 * c)) & (corner >= 0)
        mine.append(jnp.sum(jnp.where(hit, grads, 0.0), axis=1, keepdims=True))
    m0, m1, m2 = mine
    sxx, syy, szz, syz, sxz, sxy, lame, shear = [col(means, c) for c in range(8)]
    pull = [
        sxx * m0 + sxy * m1 + sxz * m2,
        sxy * m0 + syy * m1 + syz * m2,
        sxz * m0 + syz * m1 + szz * m2,
    ]
    wide = lax.broadcasted_iota(jnp.int32, (points, BLOCK), 1)
    slot_of = wide // 9
    inner = wide - 9 * slot_of
    a_of = inner // 3
    b_of = inner - 3 * a_of

    def by(which, x, y, z):
        return jnp.where(which == 0, x, jnp.where(which == 1, y, z))

    tri = lax.broadcasted_iota(jnp.int32, (points, 3), 1)
    force_ref[...] = jnp.sum(by(tri, *pull), axis=0, keepdims=True)

    lame_a = lame * by(a_of, m0, m1, m2)
    shear_b = shear * by(b_of, m0, m1, m2)
    diagonal = a_of == b_of
    total = jnp.zeros((points, BLOCK), jnp.float32)
    for l in range(8):
        g0, g1, g2 = [col(grads, 3 + 8 * c + l) for c in range(3)]
        dots = shear * (m0 * g0 + m1 * g1 + m2 * g2)
        block = lame_a * by(b_of, g0, g1, g2) + shear_b * by(a_of, g0, g1, g2)
        block = block + jnp.where(diagonal, dots, 0.0)
        total = total + jnp.where(slot_of == slots[l], block, 0.0)
    tangent_ref[...] = jnp.sum(total, axis=0, keepdims=True)


def to_all(x, axes, count):
    return lax.all_to_all(x, axes, split_axis=0, concat_axis=0, tiled=True)


def on_device(
    nodal_disp,
    weighted_shape_gradients,
    rve_element,
    connectivity,
    block_slot,
    stiffness,
    yielded_mask,
):
    rve_count, planes, plane_size = stiffness.shape
    macro_size = lax.axis_size("macro")
    vox_size = lax.axis_size("vox")
    assert rve_count == 1 and nodal_disp.shape[0] == 1
    assert planes % 8 == 0 and plane_size == EDGE * EDGE

    def rim(first):
        stiff = lax.slice_in_dim(stiffness[0], first, first + HALO, axis=0)
        mask = lax.slice_in_dim(yielded_mask[0], first, first + HALO, axis=0)
        shear = shear_base * stiff * jnp.where(mask == 1, yield_ratio, 1.0)
        return jnp.stack([stiff, shear]).reshape(2 * HALO * ROWS, 128)

    upper, lower = rim(planes - HALO), rim(0)
    if vox_size == 2:
        both = jnp.concatenate([upper, lower], axis=0)
        halo = lax.ppermute(both, "vox", [(0, 1), (1, 0)])
    else:
        forward = [(i, (i + 1) % vox_size) for i in range(vox_size)]
        backward = [(t, s) for s, t in forward]
        halo = jnp.concatenate(
            [lax.ppermute(upper, "vox", forward), lax.ppermute(lower, "vox", backward)], axis=0
        )

    packet = jnp.concatenate(
        [
            nodal_disp.reshape(1, 3),
            weighted_shape_gradients.reshape(1, 24),
            jnp.zeros((1, 5), jnp.float32),
        ],
        axis=1,
    )
    gathered = to_all(jnp.broadcast_to(packet, (macro_size, 32)), "macro", macro_size)

    def flat(field):
        parted = field.reshape(planes // 8, 8, ROWS, 128)
        return parted.transpose(0, 2, 1, 3).reshape(planes * ROWS, 128)

    smem = pl.BlockSpec(memory_space=pltpu.SMEM)
    vmem = pl.BlockSpec(memory_space=pltpu.VMEM)
    everywhere = macro_size * vox_size
    step = 4
    depth = planes + 2 * HALO + step
    field = pltpu.VMEM((3, depth, ROWS, 128), jnp.float32)
    stress, strain, sums = pl.pallas_call(
        functools.partial(slab_kernel, step),
        out_shape=(
            jax.ShapeDtypeStruct((6, planes * ROWS, 128), jnp.float32),
            jax.ShapeDtypeStruct((1, 6), jnp.float32),
            jax.ShapeDtypeStruct((everywhere, 8), jnp.float32),
        ),
        in_specs=[smem, smem, smem, vmem, vmem, vmem],
        out_specs=(pl.BlockSpec(memory_space=pl.ANY), smem, vmem),
        scratch_shapes=[
            pltpu.VMEM((depth, ROWS, 128), jnp.float32),
            pltpu.VMEM((depth, ROWS, 128), jnp.float32),
            field,
            field,
            field,
            pltpu.VMEM((3, ROWS, 128), jnp.float32),
            pltpu.VMEM((6, planes * ROWS, 128), jnp.float32),
            pltpu.SemaphoreType.DMA,
        ],
        compiler_params=pltpu.CompilerParams(vmem_limit_bytes=24 * 1024 * 1024),
        cost_estimate=pl.CostEstimate(
            flops=300 * planes * plane_size,
            bytes_accessed=32 * planes * plane_size,
            transcendentals=0,
        ),
        name="slab",
    )(gathered, rve_element, connectivity, flat(stiffness), flat(yielded_mask), halo)

    voxel_stress = (
        stress.reshape(6, planes // 8, ROWS, 8, 128)
        .transpose(0, 1, 3, 2, 4)
        .reshape(1, 6, planes, plane_size)
    )

    all_sums = to_all(sums, ("vox", "macro"), everywhere).reshape(vox_size, macro_size, 8)
    homogenized, internal_node_force, tangent = pl.pallas_call(
        node_kernel,
        out_shape=(
            jax.ShapeDtypeStruct((1, 6), jnp.float32),
            jax.ShapeDtypeStruct((1, 3), jnp.float32),
            jax.ShapeDtypeStruct((1, BLOCK), jnp.float32),
        ),
        in_specs=[vmem, vmem, vmem, smem, smem],
        out_specs=(vmem, vmem, vmem),
        name="nodes",
    )(
        all_sums,
        gathered,
        rve_element.reshape(-1, 1),
        connectivity,
        block_slot.reshape(block_slot.shape[0], 64),
    )
    return (voxel_stress, homogenized, strain, internal_node_force, tangent)


def solution(mesh):
    in_specs = (
        P("macro", None),
        P("macro", None, None),
        P(),
        P(),
        P(),
        P("macro", "vox", None),
        P("macro", "vox", None),
    )
    out_specs = (
        P("macro", None, "vox", None),
        P("macro", None),
        P("macro", None),
        P("macro", None),
        P("macro", None),
    )
    return jax.shard_map(
        on_device, mesh=mesh, in_specs=in_specs, out_specs=out_specs, check_vma=False
    )
```

```python
import jax
import jax.numpy as jnp
from jax import lax
from jax.experimental import pallas as pl
from jax.experimental.pallas import tpu as pltpu
from jax.sharding import PartitionSpec as P

EDGE = 64
SWEEPS = 3
NEIGHBOUR_SLOTS = 12
BLOCK = NEIGHBOUR_SLOTS * 9

lame_base = 1.5
shear_base = 1.0
yield_ratio = 0.2
precond = 1.0 / 42.0
lower_bound = 0.05
upper_bound = 2.0

ROWS = EDGE * EDGE // 128
HALO = 3


def chebyshev_terms(count):
    centre = 0.5 * (upper_bound + lower_bound)
    half_width = 0.5 * (upper_bound - lower_bound)
    ratio_bound = centre / half_width
    rho_prev = 1.0 / ratio_bound
    weights = []
    for number in range(count):
        rho_next = 1.0 / (2.0 * ratio_bound - rho_prev)
        weights.append((rho_next * rho_prev, 2.0 * rho_next / half_width))
        rho_prev = rho_next
    return (centre, weights)


centre, ((keep1, push1), (keep2, push2)) = chebyshev_terms(SWEEPS - 1)
gain1 = push1 * precond
gain2 = push2 * precond

def steps_for(count, most):
    return min(range(1, most + 1), key=lambda s: (-(-count // s) * s + 2 * -(-count // s), -s))


class Ops:
    def __init__(self):
        lane = lax.broadcasted_iota(jnp.int32, (8, 128), 1)
        self.low = lane < 64
        self.first = (lane & 63) == 0
        self.last = (lane & 63) == 63

    def next_row(self, x):
        y = [pltpu.roll(v, 64, 1) for v in x]
        after = y[1:] + [pltpu.roll(y[0], 7, 0)]
        return [jnp.where(self.low, here, there) for here, there in zip(y, after)]

    def prev_row(self, x):
        y = [pltpu.roll(v, 64, 1) for v in x]
        before = [pltpu.roll(y[3], 1, 0)] + y[:3]
        return [jnp.where(self.low, there, here) for here, there in zip(y, before)]

    def next_lane(self, x):
        return [jnp.where(self.last, pltpu.roll(v, 63, 1), pltpu.roll(v, 127, 1)) for v in x]

    def prev_lane(self, x):
        return [jnp.where(self.first, pltpu.roll(v, 65, 1), pltpu.roll(v, 1, 1)) for v in x]

    def stress(self, w, above, lame, shear, strain):
        row0, row1, row2 = [self.next_row(v) for v in w]
        lane0, lane1, lane2 = [self.next_lane(v) for v in w]
        out = [[] for c in range(6)]
        for q in range(4):
            w0, w1, w2 = [v[q] for v in w]
            n0, n1, n2 = [v[q] for v in above]
            e0 = (n0 - w0) + strain[0]
            e1 = (row1[q] - w1) + strain[1]
            e2 = (lane2[q] - w2) + strain[2]
            g3 = (lane1[q] + row2[q]) - (w1 + w2) + strain[3]
            g4 = (lane0[q] + n2) - (w0 + w2) + strain[4]
            g5 = (row0[q] + n1) - (w0 + w1) + strain[5]
            bulk = lame[q] * (e0 + e1 + e2)
            twice = shear[q] + shear[q]
            out[0].append(bulk + twice * e0)
            out[1].append(bulk + twice * e1)
            out[2].append(bulk + twice * e2)
            out[3].append(shear[q] * g3)
            out[4].append(shear[q] * g4)
            out[5].append(shear[q] * g5)
        return out

    def uniform(self, lame, shear, strain):
        trace = strain[0] + strain[1] + strain[2]
        twice = [2.0 * strain[c] for c in range(3)]
        out = [[] for c in range(6)]
        for q in range(4):
            bulk = lame[q] * trace
            for c in range(3):
                out[c].append(bulk + shear[q] * twice[c])
            for c in range(3, 6):
                out[c].append(shear[q] * strain[c])
        return out

    def divergence(self, stress, below):
        xx, yy, zz, yz, xz, xy = stress
        pxx, pxz, pxy = below
        xy_row, yy_row, yz_row = [self.prev_row(v) for v in (xy, yy, yz)]
        xz_lane, yz_lane, zz_lane = [self.prev_lane(v) for v in (xz, yz, zz)]
        r0 = [
            (xx[q] - pxx[q]) + (xy[q] - xy_row[q]) + (xz[q] - xz_lane[q]) for q in range(4)
        ]
        r1 = [
            (xy[q] - pxy[q]) + (yy[q] - yy_row[q]) + (yz[q] - yz_lane[q]) for q in range(4)
        ]
        r2 = [
            (xz[q] - pxz[q]) + (yz[q] - yz_row[q]) + (zz[q] - zz_lane[q]) for q in range(4)
        ]
        return r0, r1, r2


def get(ref, *at):
    return [ref[(*at, pl.ds(8 * q, 8), slice(None))] for q in range(4)]


def put(ref, x, *at):
    for q in range(4):
        ref[(*at, pl.ds(8 * q, 8), slice(None))] = x[q]


def native(group, s, q):
    return pl.ds(group * (8 * ROWS) + s + 8 * q, 8, stride=ROWS)


def fold(x):
    return (x[0] + x[1]) + (x[2] + x[3])


def total(x):
    return jnp.sum(x, axis=(0, 1), keepdims=True)


def corner_columns(grads):
    corner = lax.broadcasted_iota(jnp.int32, (8, 128), 0)
    columns = []
    for c in range(3):
        column = jnp.full((8, 128), grads[c, 0], jnp.float32)
        for k in range(1, 8):
            column = jnp.where(corner == k, grads[c, k], column)
        columns.append(column)
    return columns


def material_kernel(
    grads,
    rve_element,
    block_slot,
    stiff_ref,
    mask_ref,
    halo_ref,
    lame_ref,
    shear_ref,
    rows_ref,
):
    planes = stiff_ref.shape[0] // ROWS
    elem = rve_element[lax.axis_index("macro")]

    def load(g, acc):
        acc_l, acc_m = acc
        for s in range(8):
            lame, shear = [], []
            for q in range(4):
                stiff = stiff_ref[native(g, s, q), :]
                mask = mask_ref[native(g, s, q), :]
                lame.append(lame_base * stiff)
                shear.append(
                    stiff * jnp.where(mask == 1, shear_base * yield_ratio, shear_base)
                )
            put(lame_ref, lame, g * 8 + s + HALO)
            put(shear_ref, shear, g * 8 + s + HALO)
            acc_l = acc_l + fold(lame)
            acc_m = acc_m + fold(shear)
        return acc_l, acc_m

    zero = jnp.zeros((8, 128), jnp.float32)
    acc_l, acc_m = lax.fori_loop(0, planes // 8, load, (zero, zero))
    for side in range(2):
        for h in range(HALO):
            at = h if side == 0 else HALO + planes + h
            parts = []
            for f in range(2):
                base = ((side * 2 + f) * HALO + h) * ROWS
                parts.append([halo_ref[pl.ds(base + q, 8, stride=4), :] for q in range(4)])
            put(lame_ref, [lame_base * v for v in parts[0]], at)
            put(shear_ref, parts[1], at)

    scale = 1.0 / float(EDGE * EDGE * EDGE)
    lame, shear = total(acc_l) * scale, total(acc_m) * scale
    mine = corner_columns(grads)
    corner = lax.broadcasted_iota(jnp.int32, (8, 128), 0)
    lane = lax.broadcasted_iota(jnp.int32, (8, 128), 1)
    slot_of = jnp.zeros((8, 128), jnp.int32)
    for s in range(1, NEIGHBOUR_SLOTS + 1):
        slot_of = slot_of + jnp.where(lane >= 9 * s, 1, 0)
    inner = lane - 9 * slot_of
    a_of = jnp.where(inner >= 3, 1, 0) + jnp.where(inner >= 6, 1, 0)
    b_of = inner - 3 * a_of

    def by(which, x, y, z):
        return jnp.where(which == 0, x, jnp.where(which == 1, y, z))

    lame_a = lame * by(a_of, *mine)
    shear_b = shear * by(b_of, *mine)
    diagonal = jnp.where(a_of == b_of, shear, 0.0)
    rows = jnp.zeros((8, 128), jnp.float32)
    for l in range(8):
        other = [grads[c, l] for c in range(3)]
        dots = mine[0] * other[0] + mine[1] * other[1] + mine[2] * other[2]
        block = lame_a * by(b_of, *other) + shear_b * by(a_of, *other) + diagonal * dots
        slot = jnp.full((8, 128), block_slot[elem, 0, l], jnp.int32)
        for k in range(1, 8):
            slot = jnp.where(corner == k, block_slot[elem, k, l], slot)
        rows = rows + jnp.where(slot_of == slot, block, 0.0)
    rows_ref[...] = rows


FORCE = BLOCK
SUMS = BLOCK + 4


def slab_kernel(
    grads,
    rve_element,
    connectivity,
    gathered,
    lame_v,
    shear_v,
    rows_ref,
    stress_ref,
    strain_ref,
    packet_ref,
    w1_v,
    w2_v,
    w3_v,
    carry_v,
    out_v,
    sem,
):
    planes = out_v.shape[1] // ROWS
    point = lax.axis_index("macro")
    elem = rve_element[point]
    ops = Ops()

    nodes = [connectivity[elem, k] for k in range(8)]
    moves = [[gathered[n ^ point, a] for n in nodes] for a in range(3)]

    def dot(c, a):
        result = grads[c, 0] * moves[a][0]
        for k in range(1, 8):
            result = result + grads[c, k] * moves[a][k]
        return result

    strain = [
        dot(0, 0),
        dot(1, 1),
        dot(2, 2),
        dot(2, 1) + dot(1, 2),
        dot(2, 0) + dot(0, 2),
        dot(1, 0) + dot(0, 1),
    ]
    for c in range(6):
        strain_ref[0, c] = strain[c]

    def material(at):
        return get(lame_v, at), get(shear_v, at)

    def load3(ref, at):
        return [get(ref, c, at) for c in range(3)]

    def pick(stress):
        return stress[0], stress[4], stress[5]

    def put_carry(stress):
        for c, x in enumerate(pick(stress)):
            put(carry_v, x, c)

    def get_carry():
        return [get(carry_v, c) for c in range(3)]

    scale1 = gain1 * gain2 * precond / centre
    strain1 = [scale1 * e for e in strain]
    put_carry(ops.uniform(*material(0), strain1))
    step1 = steps_for(planes + 5, 12)

    def sweep1(t, _):
        below = get_carry()
        for u in range(step1):
            at = t * step1 + 1 + u
            stress = ops.uniform(*material(at), strain1)
            r = ops.divergence(stress, below)
            for c in range(3):
                put(w1_v, r[c], c, at)
            below = pick(stress)
        put_carry(stress)
        return 0

    lax.fori_loop(0, pl.cdiv(planes + 5, step1), sweep1, 0)

    strain2 = [gain1 * gain2 * e for e in strain]
    ratio1 = (1.0 + keep1) / gain1
    put_carry(ops.stress(load3(w1_v, 1), load3(w1_v, 2), *material(1), strain2))
    step2 = steps_for(planes + 3, 12)

    def sweep2(t, _):
        below = get_carry()
        w = load3(w1_v, t * step2 + 2)
        for u in range(step2):
            at = t * step2 + 2 + u
            above = load3(w1_v, at + 1)
            stress = ops.stress(w, above, *material(at), strain2)
            r = ops.divergence(stress, below)
            for c in range(3):
                put(w2_v, [ratio1 * x + y for x, y in zip(w[c], r[c])], c, at)
            below = pick(stress)
            w = above
        put_carry(stress)
        return 0

    lax.fori_loop(0, pl.cdiv(planes + 3, step2), sweep2, 0)

    strain3 = [gain2 * e for e in strain]
    ratio2 = (1.0 + keep2) / gain2
    ratio3 = keep2 / (gain1 * gain2)
    put_carry(ops.stress(load3(w2_v, 2), load3(w2_v, 3), *material(2), strain3))
    step3 = steps_for(planes + 1, 12)

    def sweep3(t, _):
        below = get_carry()
        w = load3(w2_v, t * step3 + 3)
        for u in range(step3):
            at = t * step3 + 3 + u
            above = load3(w2_v, at + 1)
            stress = ops.stress(w, above, *material(at), strain3)
            r = ops.divergence(stress, below)
            old = load3(w1_v, at)
            for c in range(3):
                put(
                    w3_v,
                    [ratio2 * x - ratio3 * o + y for x, o, y in zip(w[c], old[c], r[c])],
                    c,
                    at,
                )
            below = pick(stress)
            w = above
        put_carry(stress)
        return 0

    lax.fori_loop(0, pl.cdiv(planes + 1, step3), sweep3, 0)

    def put_out(g):
        span = pl.ds(pl.multiple_of(g * (8 * ROWS), 8 * ROWS), 8 * ROWS)
        return pltpu.make_async_copy(out_v.at[:, span, :], stress_ref.at[:, span, :], sem)

    def final(g, acc):
        acc = list(acc)
        w = load3(w3_v, g * 8 + HALO)
        for s in range(8):
            at = g * 8 + s + HALO
            above = load3(w3_v, at + 1)
            stress = ops.stress(w, above, *material(at), strain)
            for c in range(6):
                acc[c] = acc[c] + fold(stress[c])
                for q in range(4):
                    out_v[c, native(g, s, q), :] = stress[c][q]
            w = above
        put_out(g).start()
        return tuple(acc)

    acc = lax.fori_loop(0, planes // 8, final, (jnp.zeros((8, 128), jnp.float32),) * 6)

    scale = 1.0 / float(EDGE * EDGE * EDGE)
    xx, yy, zz, yz, xz, xy = means = [total(x) * scale for x in acc]
    g0, g1, g2 = corner_columns(grads)
    lane = lax.broadcasted_iota(jnp.int32, (8, 128), 1)
    rows = rows_ref[...]
    rows = jnp.where(lane == FORCE, xx * g0 + xy * g1 + xz * g2, rows)
    rows = jnp.where(lane == FORCE + 1, xy * g0 + yy * g1 + yz * g2, rows)
    rows = jnp.where(lane == FORCE + 2, xz * g0 + yz * g1 + zz * g2, rows)
    sums = jnp.zeros((8, 128), jnp.float32)
    for c in range(6):
        sums = jnp.where(lane == SUMS + c, means[c], sums)
    rows = jnp.where(lane >= SUMS, sums, rows)
    for g in range(packet_ref.shape[0] // 8):
        packet_ref[8 * g : 8 * g + 8, :] = sums
    count = lax.axis_size("macro")
    for v in range(lax.axis_size("vox")):
        for k in range(8):
            packet_ref[pl.ds(v * count + nodes[k], 1), :] = rows[k : k + 1]

    def drain(g, _):
        put_out(g).wait()
        return 0

    lax.fori_loop(0, planes // 8, drain, 0)


def node_kernel(packets_ref, hom_ref, force_ref, tangent_ref):
    packets = packets_ref[...]
    count = lax.axis_size("macro")
    place = lax.broadcasted_iota(jnp.int32, packets.shape, 0)
    point = lax.axis_index("macro")
    own = place == point
    for v in range(1, lax.axis_size("vox")):
        own = own | (place == v * count + point)
    row = jnp.sum(packets, axis=0, keepdims=True)
    means = jnp.sum(jnp.where(own, packets, 0.0), axis=0, keepdims=True)
    tangent_ref[...] = row[:, :BLOCK]
    force_ref[...] = row[:, FORCE : FORCE + 3]
    hom_ref[...] = means[:, SUMS : SUMS + 6]


def gather_by_exchange(x, axis):
    size = lax.axis_size(axis)
    assert size & (size - 1) == 0
    stride = 1
    while stride < size:
        radix = min(4, size // stride)
        parts = [x]
        for j in range(1, radix):
            parts.append(lax.ppermute(x, axis, [(i, i ^ (j * stride)) for i in range(size)]))
        x = jnp.concatenate(parts, axis=0)
        stride *= radix
    return x


def on_device(
    nodal_disp,
    weighted_shape_gradients,
    rve_element,
    connectivity,
    block_slot,
    stiffness,
    yielded_mask,
):
    rve_count, planes, plane_size = stiffness.shape
    macro_size = lax.axis_size("macro")
    vox_size = lax.axis_size("vox")
    assert rve_count == 1 and nodal_disp.shape[0] == 1
    assert planes % 8 == 0 and plane_size == EDGE * EDGE

    gathered = gather_by_exchange(nodal_disp, "macro")

    def rim(first):
        stiff = lax.slice_in_dim(stiffness[0], first, first + HALO, axis=0)
        mask = lax.slice_in_dim(yielded_mask[0], first, first + HALO, axis=0)
        shear = shear_base * stiff * jnp.where(mask == 1, yield_ratio, 1.0)
        return jnp.stack([stiff, shear]).reshape(2 * HALO * ROWS, 128)

    upper, lower = rim(planes - HALO), rim(0)
    if vox_size == 2:
        both = jnp.concatenate([upper, lower], axis=0)
        halo = lax.ppermute(both, "vox", [(0, 1), (1, 0)])
    else:
        forward = [(i, (i + 1) % vox_size) for i in range(vox_size)]
        backward = [(t, s) for s, t in forward]
        halo = jnp.concatenate(
            [lax.ppermute(upper, "vox", forward), lax.ppermute(lower, "vox", backward)], axis=0
        )

    def flat(field):
        parted = field.reshape(planes // 8, 8, ROWS, 128)
        return parted.transpose(0, 2, 1, 3).reshape(planes * ROWS, 128)

    smem = pl.BlockSpec(memory_space=pltpu.SMEM)
    vmem = pl.BlockSpec(memory_space=pltpu.VMEM)
    grads = weighted_shape_gradients[0]
    depth = planes + 2 * HALO + 12
    layer = jax.ShapeDtypeStruct((depth, ROWS, 128), jnp.float32)
    lame, shear, rows = pl.pallas_call(
        material_kernel,
        out_shape=(layer, layer, jax.ShapeDtypeStruct((8, 128), jnp.float32)),
        in_specs=[smem, smem, smem, vmem, vmem, vmem],
        out_specs=(vmem, vmem, vmem),
        compiler_params=pltpu.CompilerParams(vmem_limit_bytes=8 * 1024 * 1024),
        cost_estimate=pl.CostEstimate(
            flops=10 * planes * plane_size,
            bytes_accessed=16 * planes * plane_size,
            transcendentals=0,
        ),
        name="material",
    )(grads, rve_element, block_slot, flat(stiffness), flat(yielded_mask), halo)

    everywhere = macro_size * vox_size
    field = pltpu.VMEM((3, depth, ROWS, 128), jnp.float32)
    stress, strain, packet = pl.pallas_call(
        slab_kernel,
        out_shape=(
            jax.ShapeDtypeStruct((6, planes * ROWS, 128), jnp.float32),
            jax.ShapeDtypeStruct((1, 6), jnp.float32),
            jax.ShapeDtypeStruct((everywhere, 128), jnp.float32),
        ),
        in_specs=[smem, smem, smem, smem, vmem, vmem, vmem],
        out_specs=(pl.BlockSpec(memory_space=pl.ANY), smem, vmem),
        scratch_shapes=[
            field,
            field,
            field,
            pltpu.VMEM((3, ROWS, 128), jnp.float32),
            pltpu.VMEM((6, planes * ROWS, 128), jnp.float32),
            pltpu.SemaphoreType.DMA,
        ],
        compiler_params=pltpu.CompilerParams(vmem_limit_bytes=20 * 1024 * 1024),
        cost_estimate=pl.CostEstimate(
            flops=300 * planes * plane_size,
            bytes_accessed=32 * planes * plane_size,
            transcendentals=0,
        ),
        name="slab",
    )(grads, rve_element, connectivity, gathered, lame, shear, rows)

    voxel_stress = (
        stress.reshape(6, planes // 8, ROWS, 8, 128)
        .transpose(0, 1, 3, 2, 4)
        .reshape(1, 6, planes, plane_size)
    )

    packets = lax.all_to_all(
        packet, ("vox", "macro"), split_axis=0, concat_axis=0, tiled=True
    )
    homogenized, internal_node_force, tangent = pl.pallas_call(
        node_kernel,
        out_shape=(
            jax.ShapeDtypeStruct((1, 6), jnp.float32),
            jax.ShapeDtypeStruct((1, 3), jnp.float32),
            jax.ShapeDtypeStruct((1, BLOCK), jnp.float32),
        ),
        in_specs=[vmem],
        out_specs=(vmem, vmem, vmem),
        name="nodes",
    )(packets)
    return (voxel_stress, homogenized, strain, internal_node_force, tangent)


def solution(mesh):
    in_specs = (
        P("macro", None),
        P("macro", None, None),
        P(),
        P(),
        P(),
        P("macro", "vox", None),
        P("macro", "vox", None),
    )
    out_specs = (
        P("macro", None, "vox", None),
        P("macro", None),
        P("macro", None),
        P("macro", None),
        P("macro", None),
    )
    return jax.shard_map(
        on_device, mesh=mesh, in_specs=in_specs, out_specs=out_specs, check_vma=False
    )
```

```python
import jax
import jax.numpy as jnp
from jax import lax
from jax.experimental import pallas as pl
from jax.experimental.pallas import tpu as pltpu
from jax.sharding import PartitionSpec as P

EDGE = 64
SWEEPS = 3
NEIGHBOUR_SLOTS = 12
BLOCK = NEIGHBOUR_SLOTS * 9

lame_base = 1.5
shear_base = 1.0
yield_ratio = 0.2
precond = 1.0 / 42.0
lower_bound = 0.05
upper_bound = 2.0

ROWS = EDGE * EDGE // 128
WIDE = 256
HALO = 3


def chebyshev_terms(count):
    centre = 0.5 * (upper_bound + lower_bound)
    half_width = 0.5 * (upper_bound - lower_bound)
    ratio_bound = centre / half_width
    rho_prev = 1.0 / ratio_bound
    weights = []
    for number in range(count):
        rho_next = 1.0 / (2.0 * ratio_bound - rho_prev)
        weights.append((rho_next * rho_prev, 2.0 * rho_next / half_width))
        rho_prev = rho_next
    return (centre, weights)


centre, ((keep1, push1), (keep2, push2)) = chebyshev_terms(SWEEPS - 1)
gain1 = push1 * precond
gain2 = push2 * precond

def best_step(count, most):
    return min(range(1, most + 1), key=lambda s: (-(-count // s) * s, -s))


def spot(at, jj):
    half = (jj & 1) * 128
    return at, pl.ds(8 * (jj // 2), 8), pl.ds(half, 128)


def load(ref, at, jj):
    return ref[spot(at, jj)]


def load3(ref, at, jj):
    return [ref[(c, *spot(at, jj))] for c in range(3)]


def next_row(ref, c, at, jj):
    if jj < 7:
        return ref[(c, *spot(at, jj + 1))]
    return pltpu.roll(ref[(c, *spot(at, 0))], 7, 0)


def next_lane(x):
    return pltpu.roll(x, 126, 1)


def prev_lane(x):
    return pltpu.roll(x, 2, 1)


def stress_at(w_ref, at, jj, w, lame, shear, strain):
    w0, w1, w2 = w
    n0, n1, n2 = load3(w_ref, at + 1, jj)
    row0, row1, row2 = [next_row(w_ref, c, at, jj) for c in range(3)]
    lane0, lane1, lane2 = [next_lane(x) for x in w]
    e0 = (n0 - w0) + strain[0]
    e1 = (row1 - w1) + strain[1]
    e2 = (lane2 - w2) + strain[2]
    g3 = (lane1 + row2) - (w1 + w2) + strain[3]
    g4 = (lane0 + n2) - (w0 + w2) + strain[4]
    g5 = (row0 + n1) - (w0 + w1) + strain[5]
    bulk = lame * (e0 + e1 + e2)
    twice = shear + shear
    return (
        bulk + twice * e0,
        bulk + twice * e1,
        bulk + twice * e2,
        shear * g3,
        shear * g4,
        shear * g5,
    )


def sweep_plane(w_ref, lame_ref, shear_ref, carry_v, old, new, at, strain, update):
    first = None
    row_xy = row_yy = row_yz = None
    for jj in range(8):
        w = load3(w_ref, at, jj)
        stress = stress_at(
            w_ref, at, jj, w, load(lame_ref, at, jj), load(shear_ref, at, jj), strain
        )
        xx, yy, zz, yz, xz, xy = stress
        pxx, pxz, pxy = [carry_v[(old, c, *spot(0, jj)[1:])] for c in range(3)]
        for c, x in enumerate((xx, xz, xy)):
            carry_v[(new, c, *spot(0, jj)[1:])] = x
        r = [
            (xx - pxx) + (xz - prev_lane(xz)) + xy,
            (xy - pxy) + (yz - prev_lane(yz)) + yy,
            (xz - pxz) + (zz - prev_lane(zz)) + yz,
        ]
        if jj == 0:
            first = r
        else:
            update(jj, w, [r[0] - row_xy, r[1] - row_yy, r[2] - row_yz])
        row_xy, row_yy, row_yz = xy, yy, yz
    rows = [pltpu.roll(x, 1, 0) for x in (row_xy, row_yy, row_yz)]
    update(0, load3(w_ref, at, 0), [x - y for x, y in zip(first, rows)])


def carry_plane(w_ref, lame_ref, shear_ref, carry_v, at, strain):
    for jj in range(8):
        w = load3(w_ref, at, jj)
        xx, yy, zz, yz, xz, xy = stress_at(
            w_ref, at, jj, w, load(lame_ref, at, jj), load(shear_ref, at, jj), strain
        )
        for c, x in enumerate((xx, xz, xy)):
            carry_v[(0, c, *spot(0, jj)[1:])] = x


def target_lane(m):
    return ((m >> 6) & 1) * 128 + (m & 63) * 2 + (m >> 7)


def lane_matrix(inverse):
    row = lax.broadcasted_iota(jnp.int32, (WIDE, WIDE), 0)
    column = lax.broadcasted_iota(jnp.int32, (WIDE, WIDE), 1)
    hit = (target_lane(column) == row) if inverse else (target_lane(row) == column)
    return jnp.where(hit, 1.0, 0.0).astype(jnp.bfloat16)


def permute_lanes(x, matrix, terms):
    result = None
    for t in range(terms):
        part = x.astype(jnp.bfloat16)
        moved = jnp.dot(part, matrix, preferred_element_type=jnp.float32)
        result = moved if result is None else result + moved
        if t + 1 < terms:
            x = x - part.astype(jnp.float32)
    return result


def native(plane, q):
    return pl.ds((plane // 8) * (8 * ROWS) + plane % 8 + 8 * q, 8, stride=ROWS)


def total(x):
    return jnp.sum(x, axis=(0, 1), keepdims=True)


def corner_columns(grads):
    corner = lax.broadcasted_iota(jnp.int32, (8, 128), 0)
    columns = []
    for c in range(3):
        column = jnp.full((8, 128), grads[c, 0], jnp.float32)
        for k in range(1, 8):
            column = jnp.where(corner == k, grads[c, k], column)
        columns.append(column)
    return columns


FORCE = BLOCK
SUMS = BLOCK + 4
LAME_MEAN = 120
SHEAR_MEAN = 121


def material_kernel(
    grads,
    rve_element,
    block_slot,
    stiff_hbm,
    mask_hbm,
    halo_ref,
    lame_ref,
    shear_ref,
    dlame_ref,
    dshear_ref,
    rows_ref,
    stiff_v,
    mask_v,
    lame_in,
    shear_in,
    sems,
):
    copies = [
        pltpu.make_async_copy(stiff_hbm, stiff_v, sems.at[0]),
        pltpu.make_async_copy(mask_hbm, mask_v, sems.at[1]),
    ]
    for copy in copies:
        copy.start()
    planes = stiff_v.shape[0] // ROWS
    half = planes // 2
    depth = half + 2 * HALO
    elem = rve_element[lax.axis_index("macro")]
    matrix = lane_matrix(False)
    for copy in copies:
        copy.wait()

    acc_l = acc_m = jnp.zeros((8, 128), jnp.float32)
    for h in range(2):
        for at in range(depth):
            plane = at - HALO + h * half
            for q in range(4):
                if 0 <= plane < planes:
                    stiff = stiff_v[native(plane, q), :]
                    mask = mask_v[native(plane, q), :]
                    shear = stiff * jnp.where(mask == 1, shear_base * yield_ratio, shear_base)
                else:
                    side, far = (0, plane + HALO) if plane < 0 else (1, plane - planes)
                    base = (side * 2 * HALO + far) * ROWS + q
                    stiff = halo_ref[pl.ds(base, 8, stride=4), :]
                    shear = halo_ref[pl.ds(base + HALO * ROWS, 8, stride=4), :]
                lame = lame_base * stiff
                place = (at, pl.ds(8 * q, 8), pl.ds(128 * h, 128))
                lame_in[place] = lame
                shear_in[place] = shear
                if HALO <= at < HALO + half:
                    acc_l = acc_l + lame
                    acc_m = acc_m + shear

    for source, target in ((lame_in, lame_ref), (shear_in, shear_ref)):
        x = source[...].reshape(depth * ROWS, WIDE)
        target[pl.ds(0, depth)] = permute_lanes(x, matrix, 3).reshape(depth, ROWS, WIDE)

    def difference(t, _):
        at = t + 1
        for source, target in ((lame_ref, dlame_ref), (shear_ref, dshear_ref)):
            for jj in range(8):
                here = load(source, at, jj)
                before = load(source, at, jj - 1) if jj else pltpu.roll(load(source, at, 7), 1, 0)
                target[(0, *spot(at, jj))] = here - load(source, at - 1, jj)
                target[(1, *spot(at, jj))] = here - before
                target[(2, *spot(at, jj))] = here - prev_lane(here)
        return 0

    lax.fori_loop(0, depth - 1, difference, 0)

    scale = 1.0 / float(EDGE * EDGE * EDGE)
    lame, shear = total(acc_l) * scale, total(acc_m) * scale
    mine = corner_columns(grads)
    corner = lax.broadcasted_iota(jnp.int32, (8, 128), 0)
    lane = lax.broadcasted_iota(jnp.int32, (8, 128), 1)
    slot_of = jnp.zeros((8, 128), jnp.int32)
    for s in range(1, NEIGHBOUR_SLOTS + 1):
        slot_of = slot_of + jnp.where(lane >= 9 * s, 1, 0)
    inner = lane - 9 * slot_of
    a_of = jnp.where(inner >= 3, 1, 0) + jnp.where(inner >= 6, 1, 0)
    b_of = inner - 3 * a_of

    def by(which, x, y, z):
        return jnp.where(which == 0, x, jnp.where(which == 1, y, z))

    lame_a = lame * by(a_of, *mine)
    shear_b = shear * by(b_of, *mine)
    diagonal = jnp.where(a_of == b_of, shear, 0.0)
    rows = jnp.zeros((8, 128), jnp.float32)
    for l in range(8):
        other = [grads[c, l] for c in range(3)]
        dots = mine[0] * other[0] + mine[1] * other[1] + mine[2] * other[2]
        block = lame_a * by(b_of, *other) + shear_b * by(a_of, *other) + diagonal * dots
        slot = jnp.full((8, 128), block_slot[elem, 0, l], jnp.int32)
        for k in range(1, 8):
            slot = jnp.where(corner == k, block_slot[elem, k, l], slot)
        rows = rows + jnp.where(slot_of == slot, block, 0.0)
    rows = jnp.where(lane == LAME_MEAN, lame, rows)
    rows = jnp.where(lane == SHEAR_MEAN, shear, rows)
    rows_ref[...] = rows


def sweep_kernel(
    grads,
    rve_element,
    connectivity,
    gathered,
    lame_ref,
    shear_ref,
    dlame_ref,
    dshear_ref,
    rows_ref,
    w3_ref,
    strain_ref,
    packet_ref,
    w1_v,
    w2_v,
    carry_v,
):
    half = lame_ref.shape[0] - 2 * HALO - MARGIN
    elem = rve_element[lax.axis_index("macro")]
    nodes = [connectivity[elem, k] for k in range(8)]
    moves = [[gathered[n, a] for n in nodes] for a in range(3)]

    def dot(c, a):
        result = grads[c, 0] * moves[a][0]
        for k in range(1, 8):
            result = result + grads[c, k] * moves[a][k]
        return result

    strain = [
        dot(0, 0),
        dot(1, 1),
        dot(2, 2),
        dot(2, 1) + dot(1, 2),
        dot(2, 0) + dot(0, 2),
        dot(1, 0) + dot(0, 1),
    ]
    for c in range(6):
        strain_ref[0, c] = strain[c]

    scale1 = gain1 * gain2 * precond / centre
    strain1 = [scale1 * e for e in strain]
    trace1 = strain1[0] + strain1[1] + strain1[2]
    twice1 = [2.0 * strain1[c] for c in range(3)]
    step1 = best_step(half + 5, STEP)

    def sweep1(t, _):
        for u in range(step1):
            at = t * step1 + 1 + u
            for jj in range(8):
                l0, l1, l2 = load3(dlame_ref, at, jj)
                m0, m1, m2 = load3(dshear_ref, at, jj)
                w1_v[(0, *spot(at, jj))] = (
                    trace1 * l0 + twice1[0] * m0 + (strain1[5] * m1 + strain1[4] * m2)
                )
                w1_v[(1, *spot(at, jj))] = (
                    trace1 * l1 + twice1[1] * m1 + (strain1[5] * m0 + strain1[3] * m2)
                )
                w1_v[(2, *spot(at, jj))] = (
                    trace1 * l2 + twice1[2] * m2 + (strain1[4] * m0 + strain1[3] * m1)
                )
        return 0

    lax.fori_loop(0, pl.cdiv(half + 5, step1), sweep1, 0)

    strain2 = [gain1 * gain2 * e for e in strain]
    ratio1 = (1.0 + keep1) / gain1
    step2 = best_step(half + 3, STEP)
    carry_plane(w1_v, lame_ref, shear_ref, carry_v, 1, strain2)

    def sweep2(t, _):
        for u in range(step2):
            at = t * step2 + 2 + u

            def update(jj, w, r):
                for c in range(3):
                    w2_v[(c, *spot(at, jj))] = ratio1 * w[c] + r[c]

            sweep_plane(
                w1_v, lame_ref, shear_ref, carry_v, u, (u + 1) % step2, at, strain2, update
            )
        return 0

    lax.fori_loop(0, pl.cdiv(half + 3, step2), sweep2, 0)

    strain3 = [gain2 * e for e in strain]
    ratio2 = (1.0 + keep2) / gain2
    ratio3 = keep2 / (gain1 * gain2)
    step3 = best_step(half + 1, STEP)
    carry_plane(w2_v, lame_ref, shear_ref, carry_v, 2, strain3)

    def sweep3(t, _):
        for u in range(step3):
            at = t * step3 + 3 + u

            def update(jj, w, r):
                old = load3(w1_v, at, jj)
                for c in range(3):
                    w3_ref[(c, *spot(at, jj))] = (ratio2 * w[c] - ratio3 * old[c]) + r[c]

            sweep_plane(
                w2_v, lame_ref, shear_ref, carry_v, u, (u + 1) % step3, at, strain3, update
            )
        return 0

    lax.fori_loop(0, pl.cdiv(half + 1, step3), sweep3, 0)

    def by_parts(t, acc):
        bulk, a0, a1, a2, a3, a4, a5 = acc
        at = t + HALO
        for jj in range(8):
            w0, w1, w2 = load3(w3_ref, at, jj)
            l0, l1, l2 = load3(dlame_ref, at, jj)
            m0, m1, m2 = load3(dshear_ref, at, jj)
            bulk = bulk + (l0 * w0 + l1 * w1 + l2 * w2)
            a0 = a0 + m0 * w0
            a1 = a1 + m1 * w1
            a2 = a2 + m2 * w2
            a3 = a3 + (m2 * w1 + m1 * w2)
            a4 = a4 + (m2 * w0 + m0 * w2)
            a5 = a5 + (m1 * w0 + m0 * w1)
        return bulk, a0, a1, a2, a3, a4, a5

    zero = jnp.zeros((8, 128), jnp.float32)
    acc = lax.fori_loop(0, half, by_parts, (zero,) * 7)
    scale = 1.0 / float(EDGE * EDGE * EDGE)
    bulk, *parts = [total(x) * scale for x in acc]
    rows = rows_ref[...]
    lame = rows[:1, LAME_MEAN : LAME_MEAN + 1]
    shear = rows[:1, SHEAR_MEAN : SHEAR_MEAN + 1]
    bulk = lame * (strain[0] + strain[1] + strain[2]) - bulk
    means = [bulk + 2.0 * (shear * strain[c] - parts[c]) for c in range(3)]
    means += [shear * strain[c] - parts[c] for c in range(3, 6)]

    xx, yy, zz, yz, xz, xy = means
    g0, g1, g2 = corner_columns(grads)
    lane = lax.broadcasted_iota(jnp.int32, (8, 128), 1)
    rows = jnp.where(lane == FORCE, xx * g0 + xy * g1 + xz * g2, rows)
    rows = jnp.where(lane == FORCE + 1, xy * g0 + yy * g1 + yz * g2, rows)
    rows = jnp.where(lane == FORCE + 2, xz * g0 + yz * g1 + zz * g2, rows)
    sums = jnp.zeros((8, 128), jnp.float32)
    for c in range(6):
        sums = jnp.where(lane == SUMS + c, means[c], sums)
    rows = jnp.where(lane >= SUMS, sums, rows)
    for g in range(packet_ref.shape[0] // 8):
        packet_ref[8 * g : 8 * g + 8, :] = sums
    count = lax.axis_size("macro")
    for v in range(lax.axis_size("vox")):
        for k in range(8):
            packet_ref[pl.ds(v * count + nodes[k], 1), :] = rows[k : k + 1]


def stress_kernel(
    strain_in,
    lame_ref,
    shear_ref,
    w3_ref,
    stress_ref,
    out_v,
    work_v,
    sem,
):
    half = lame_ref.shape[0] - 2 * HALO - MARGIN
    strain = [strain_in[0, c] for c in range(6)]
    matrix = lane_matrix(True)
    copies = []
    for first in range(0, half, GROUP):
        slot = (first // GROUP) % 2
        for u in range(GROUP):
            at = first + u + HALO
            for jj in range(8):
                stress = stress_at(
                    w3_ref,
                    at,
                    jj,
                    load3(w3_ref, at, jj),
                    load(lame_ref, at, jj),
                    load(shear_ref, at, jj),
                    strain,
                )
                for c in range(6):
                    work_v[(slot, u, c, *spot(0, jj)[1:])] = stress[c]
        x = work_v[slot].reshape(GROUP * 6 * ROWS, WIDE)
        y = permute_lanes(x, matrix, 2)
        for u in range(GROUP):
            for c in range(6):
                for q in range(4):
                    row = ((u * 6 + c) * 4 + q) * 8
                    for h in range(2):
                        plane = first + u + h * half
                        out_v[c, native(plane, q), :] = y[row : row + 8, 128 * h : 128 * h + 128]
        done = []
        if half % 8 == 0 and (first + GROUP) % 8 == 0:
            done = [(first + GROUP) // 8 - 1 + h * (half // 8) for h in range(2)]
        elif first + GROUP == half:
            done = range(2 * half // 8)
        if done:
            for group in done:
                span = pl.ds(group * (8 * ROWS), 8 * ROWS)
                copy = pltpu.make_async_copy(
                    out_v.at[:, span, :], stress_ref.at[:, span, :], sem.at[len(copies)]
                )
                copy.start()
                copies.append(copy)
    for copy in copies:
        copy.wait()


STEP = 3
GROUP = 4
MARGIN = 3


def node_kernel(packets_ref, hom_ref, force_ref, tangent_ref):
    packets = packets_ref[...]
    count = lax.axis_size("macro")
    place = lax.broadcasted_iota(jnp.int32, packets.shape, 0)
    point = lax.axis_index("macro")
    own = place == point
    for v in range(1, lax.axis_size("vox")):
        own = own | (place == v * count + point)
    row = jnp.sum(packets, axis=0, keepdims=True)
    means = jnp.sum(jnp.where(own, packets, 0.0), axis=0, keepdims=True)
    tangent_ref[...] = row[:, :BLOCK]
    force_ref[...] = row[:, FORCE : FORCE + 3]
    hom_ref[...] = means[:, SUMS : SUMS + 6]


def on_device(
    nodal_disp,
    weighted_shape_gradients,
    rve_element,
    connectivity,
    block_slot,
    stiffness,
    yielded_mask,
):
    rve_count, planes, plane_size = stiffness.shape
    macro_size = lax.axis_size("macro")
    vox_size = lax.axis_size("vox")
    everywhere = macro_size * vox_size
    assert rve_count == 1 and nodal_disp.shape[0] == 1
    assert planes % 8 == 0 and plane_size == EDGE * EDGE

    gathered = lax.all_to_all(
        jnp.broadcast_to(nodal_disp, (macro_size, 3)),
        "macro",
        split_axis=0,
        concat_axis=0,
        tiled=True,
    )

    def rim(first):
        stiff = lax.slice_in_dim(stiffness[0], first, first + HALO, axis=0)
        mask = lax.slice_in_dim(yielded_mask[0], first, first + HALO, axis=0)
        shear = shear_base * stiff * jnp.where(mask == 1, yield_ratio, 1.0)
        return jnp.stack([stiff, shear]).reshape(2 * HALO * ROWS, 128)

    upper, lower = rim(planes - HALO), rim(0)
    if vox_size == 2:
        both = jnp.concatenate([upper, lower], axis=0)
        halo = lax.ppermute(both, "vox", [(0, 1), (1, 0)])
    else:
        forward = [(i, (i + 1) % vox_size) for i in range(vox_size)]
        backward = [(t, s) for s, t in forward]
        halo = jnp.concatenate(
            [lax.ppermute(upper, "vox", forward), lax.ppermute(lower, "vox", backward)], axis=0
        )

    def flat(field):
        parted = field.reshape(planes // 8, 8, ROWS, 128)
        return parted.transpose(0, 2, 1, 3).reshape(planes * ROWS, 128)

    smem = pl.BlockSpec(memory_space=pltpu.SMEM)
    vmem = pl.BlockSpec(memory_space=pltpu.VMEM)
    anywhere = pl.BlockSpec(memory_space=pl.ANY)
    mib = 1024 * 1024
    f32 = jnp.float32
    grads = weighted_shape_gradients[0]
    half = planes // 2
    depth = half + 2 * HALO + MARGIN
    scalar = jax.ShapeDtypeStruct((depth, ROWS, WIDE), f32)
    vector = jax.ShapeDtypeStruct((3, depth, ROWS, WIDE), f32)
    native_field = pltpu.VMEM((planes * ROWS, 128), f32)
    half_field = pltpu.VMEM((half + 2 * HALO, ROWS, WIDE), f32)

    def cost(flops, size):
        return pl.CostEstimate(
            flops=flops * planes * plane_size,
            bytes_accessed=size * planes * plane_size,
            transcendentals=0,
        )

    lame, shear, dlame, dshear, rows = pl.pallas_call(
        material_kernel,
        out_shape=(scalar, scalar, vector, vector, jax.ShapeDtypeStruct((8, 128), f32)),
        in_specs=[smem, smem, smem, anywhere, anywhere, vmem],
        out_specs=(vmem,) * 5,
        scratch_shapes=[
            native_field,
            pltpu.VMEM((planes * ROWS, 128), jnp.int32),
            half_field,
            half_field,
            pltpu.SemaphoreType.DMA((2,)),
        ],
        compiler_params=pltpu.CompilerParams(vmem_limit_bytes=16 * mib),
        cost_estimate=cost(100, 40),
        name="material",
    )(grads, rve_element, block_slot, flat(stiffness), flat(yielded_mask), halo)

    field = pltpu.VMEM((3, depth, ROWS, WIDE), f32)
    w3, strain, packet = pl.pallas_call(
        sweep_kernel,
        out_shape=(
            vector,
            jax.ShapeDtypeStruct((1, 6), f32),
            jax.ShapeDtypeStruct((everywhere, 128), f32),
        ),
        in_specs=[smem] * 4 + [vmem] * 5,
        out_specs=(vmem, smem, vmem),
        scratch_shapes=[field, field, pltpu.VMEM((STEP, 3, ROWS, WIDE), f32)],
        compiler_params=pltpu.CompilerParams(vmem_limit_bytes=16 * mib),
        cost_estimate=cost(200, 40),
        name="sweeps",
    )(grads, rve_element, connectivity, gathered, lame, shear, dlame, dshear, rows)

    packets = lax.all_to_all(
        packet, ("vox", "macro"), split_axis=0, concat_axis=0, tiled=True
    )

    stress = pl.pallas_call(
        stress_kernel,
        out_shape=jax.ShapeDtypeStruct((6, planes * ROWS, 128), f32),
        in_specs=[smem, vmem, vmem, vmem],
        out_specs=anywhere,
        scratch_shapes=[
            pltpu.VMEM((6, planes * ROWS, 128), f32),
            pltpu.VMEM((2, GROUP, 6, ROWS, WIDE), f32),
            pltpu.SemaphoreType.DMA((planes // 8,)),
        ],
        compiler_params=pltpu.CompilerParams(vmem_limit_bytes=20 * mib),
        cost_estimate=cost(100, 40),
        name="stress",
    )(strain, lame, shear, w3)
    voxel_stress = (
        stress.reshape(6, planes // 8, ROWS, 8, 128)
        .transpose(0, 1, 3, 2, 4)
        .reshape(1, 6, planes, plane_size)
    )

    homogenized, internal_node_force, tangent = pl.pallas_call(
        node_kernel,
        out_shape=(
            jax.ShapeDtypeStruct((1, 6), f32),
            jax.ShapeDtypeStruct((1, 3), f32),
            jax.ShapeDtypeStruct((1, BLOCK), f32),
        ),
        in_specs=[vmem],
        out_specs=(vmem, vmem, vmem),
        name="nodes",
    )(packets)
    return (voxel_stress, homogenized, strain, internal_node_force, tangent)


def solution(mesh):
    in_specs = (
        P("macro", None),
        P("macro", None, None),
        P(),
        P(),
        P(),
        P("macro", "vox", None),
        P("macro", "vox", None),
    )
    out_specs = (
        P("macro", None, "vox", None),
        P("macro", None),
        P("macro", None),
        P("macro", None),
        P("macro", None),
    )
    return jax.shard_map(
        on_device, mesh=mesh, in_specs=in_specs, out_specs=out_specs, check_vma=False
    )
```

```python
import jax
import jax.numpy as jnp
from jax import lax
from jax.experimental import pallas as pl
from jax.experimental.pallas import tpu as pltpu
from jax.sharding import PartitionSpec as P

EDGE = 64
SWEEPS = 3
NEIGHBOUR_SLOTS = 12
BLOCK = NEIGHBOUR_SLOTS * 9

lame_base = 1.5
shear_base = 1.0
yield_ratio = 0.2
precond = 1.0 / 42.0
lower_bound = 0.05
upper_bound = 2.0

ROWS = EDGE * EDGE // 128
WIDE = 256
HALO = 3


def chebyshev_terms(count):
    centre = 0.5 * (upper_bound + lower_bound)
    half_width = 0.5 * (upper_bound - lower_bound)
    ratio_bound = centre / half_width
    rho_prev = 1.0 / ratio_bound
    weights = []
    for number in range(count):
        rho_next = 1.0 / (2.0 * ratio_bound - rho_prev)
        weights.append((rho_next * rho_prev, 2.0 * rho_next / half_width))
        rho_prev = rho_next
    return (centre, weights)


centre, ((keep1, push1), (keep2, push2)) = chebyshev_terms(SWEEPS - 1)
gain1 = push1 * precond
gain2 = push2 * precond

def best_step(count, most):
    return min(range(1, most + 1), key=lambda s: (-(-count // s) * s, -s))


def spot(at, jj):
    half = (jj & 1) * 128
    return at, pl.ds(8 * (jj // 2), 8), pl.ds(half, 128)


def load(ref, at, jj):
    return ref[spot(at, jj)]


def load3(refs, at, jj):
    return [load(ref, at, jj) for ref in refs]


def next_row(ref, at, jj):
    if jj < 7:
        return load(ref, at, jj + 1)
    return pltpu.roll(load(ref, at, 0), 7, 0)


def prev_row(ref, at, jj):
    if jj > 0:
        return load(ref, at, jj - 1)
    return pltpu.roll(load(ref, at, 7), 1, 0)


def next_lane(x):
    return pltpu.roll(x, 126, 1)


def prev_lane(x):
    return pltpu.roll(x, 2, 1)


def differences(ref, at, jj):
    here = load(ref, at, jj)
    return (
        here - load(ref, at - 1, jj),
        here - prev_row(ref, at, jj),
        here - prev_lane(here),
    )


def stress_at(w_refs, at, jj, w, lame, shear, strain):
    w0, w1, w2 = w
    n0, n1, n2 = load3(w_refs, at + 1, jj)
    row0, row1, row2 = [next_row(ref, at, jj) for ref in w_refs]
    lane0, lane1, lane2 = [next_lane(x) for x in w]
    e0 = (n0 - w0) + strain[0]
    e1 = (row1 - w1) + strain[1]
    e2 = (lane2 - w2) + strain[2]
    g3 = (lane1 + row2) - (w1 + w2) + strain[3]
    g4 = (lane0 + n2) - (w0 + w2) + strain[4]
    g5 = (row0 + n1) - (w0 + w1) + strain[5]
    bulk = lame * (e0 + e1 + e2)
    twice = shear + shear
    return (
        bulk + twice * e0,
        bulk + twice * e1,
        bulk + twice * e2,
        shear * g3,
        shear * g4,
        shear * g5,
    )


def sweep_plane(w_refs, lame_ref, shear_ref, carry_v, old, new, at, strain, update):
    first = None
    row_xy = row_yy = row_yz = None
    for jj in range(8):
        w = load3(w_refs, at, jj)
        stress = stress_at(
            w_refs, at, jj, w, load(lame_ref, at, jj), load(shear_ref, at, jj), strain
        )
        xx, yy, zz, yz, xz, xy = stress
        pxx, pxz, pxy = [carry_v[(old, c, *spot(0, jj)[1:])] for c in range(3)]
        for c, x in enumerate((xx, xz, xy)):
            carry_v[(new, c, *spot(0, jj)[1:])] = x
        r = [
            (xx - pxx) + (xz - prev_lane(xz)) + xy,
            (xy - pxy) + (yz - prev_lane(yz)) + yy,
            (xz - pxz) + (zz - prev_lane(zz)) + yz,
        ]
        if jj == 0:
            first = r
        else:
            update(jj, w, [r[0] - row_xy, r[1] - row_yy, r[2] - row_yz])
        row_xy, row_yy, row_yz = xy, yy, yz
    rows = [pltpu.roll(x, 1, 0) for x in (row_xy, row_yy, row_yz)]
    update(0, load3(w_refs, at, 0), [x - y for x, y in zip(first, rows)])


def carry_plane(w_refs, lame_ref, shear_ref, carry_v, at, strain):
    for jj in range(8):
        w = load3(w_refs, at, jj)
        xx, yy, zz, yz, xz, xy = stress_at(
            w_refs, at, jj, w, load(lame_ref, at, jj), load(shear_ref, at, jj), strain
        )
        for c, x in enumerate((xx, xz, xy)):
            carry_v[(0, c, *spot(0, jj)[1:])] = x


def target_lane(m):
    return ((m >> 6) & 1) * 128 + (m & 63) * 2 + (m >> 7)


def lane_matrix(inverse):
    row = lax.broadcasted_iota(jnp.int32, (WIDE, WIDE), 0)
    column = lax.broadcasted_iota(jnp.int32, (WIDE, WIDE), 1)
    hit = (target_lane(column) == row) if inverse else (target_lane(row) == column)
    return jnp.where(hit, 1.0, 0.0).astype(jnp.bfloat16)


def permute_lanes(x, matrix, terms):
    result = None
    for t in range(terms):
        part = x.astype(jnp.bfloat16)
        moved = jnp.dot(part, matrix, preferred_element_type=jnp.float32)
        result = moved if result is None else result + moved
        if t + 1 < terms:
            x = x - part.astype(jnp.float32)
    return result


def native(plane, q):
    return pl.ds((plane // 8) * (8 * ROWS) + plane % 8 + 8 * q, 8, stride=ROWS)


def total(x):
    return jnp.sum(x, axis=(0, 1), keepdims=True)


def corner_columns(grads):
    corner = lax.broadcasted_iota(jnp.int32, (8, 128), 0)
    columns = []
    for c in range(3):
        column = jnp.full((8, 128), grads[c, 0], jnp.float32)
        for k in range(1, 8):
            column = jnp.where(corner == k, grads[c, k], column)
        columns.append(column)
    return columns


FORCE = BLOCK
SUMS = BLOCK + 4
LAME_MEAN = 120
SHEAR_MEAN = 121


def prepare_kernel(disp_hbm, stiff_hbm, mask_hbm, disp_ref, halo_ref, disp_v, ends_v, mask_v, sems):
    groups = stiff_hbm.shape[0] // (8 * ROWS)
    ends = [pl.ds((groups - 1) * (8 * ROWS), 8 * ROWS), pl.ds(0, 8 * ROWS)]
    copies = [pltpu.make_async_copy(disp_hbm, disp_v, sems.at[0])]
    for e in range(2):
        copies += [
            pltpu.make_async_copy(stiff_hbm.at[ends[e], :], ends_v.at[e], sems.at[1 + 2 * e]),
            pltpu.make_async_copy(mask_hbm.at[ends[e], :], mask_v.at[e], sems.at[2 + 2 * e]),
        ]
    for copy in copies:
        copy.start()
    for copy in copies:
        copy.wait()
    disp_ref[...] = jnp.broadcast_to(disp_v[...], disp_ref.shape)
    row = 0
    for e, first in ((0, 8 - HALO), (1, 0)):
        for field in (ends_v, mask_v):
            for plane in range(first, first + HALO):
                for q in range(4):
                    x = field[e, native(plane, q), :]
                    halo_ref[row : row + 8, :] = x.astype(jnp.float32)
                    row += 8


def material_kernel(
    grads,
    rve_hbm,
    slot_hbm,
    stiff_v,
    mask_v,
    halo_ref,
    lame_ref,
    shear_ref,
    rows_ref,
    stiff_in,
    mask_in,
    rve_element,
    block_slot,
    sems,
):
    copies = [
        pltpu.make_async_copy(rve_hbm, rve_element, sems.at[0]),
        pltpu.make_async_copy(slot_hbm, block_slot, sems.at[1]),
    ]
    for copy in copies:
        copy.start()
    planes = stiff_v.shape[0] // ROWS
    half = planes // 2
    depth = half + 2 * HALO
    matrix = lane_matrix(False)

    for h in range(2):
        for at in range(depth):
            plane = at - HALO + h * half
            for q in range(4):
                if 0 <= plane < planes:
                    stiff = stiff_v[native(plane, q), :]
                    mask = mask_v[native(plane, q), :].astype(jnp.float32)
                else:
                    side, far = (0, plane + HALO) if plane < 0 else (1, plane - planes)
                    base = (side * 2 * HALO + far) * ROWS + 8 * q
                    stiff = halo_ref[base : base + 8, :]
                    mask = halo_ref[base + HALO * ROWS : base + HALO * ROWS + 8, :]
                place = (at, pl.ds(8 * q, 8), pl.ds(128 * h, 128))
                stiff_in[place] = stiff
                mask_in[place] = mask

    acc_l = acc_m = jnp.zeros((8, 128), jnp.float32)
    for first in range(0, depth, 2):
        count = min(2, depth - first)
        shape = (count * ROWS, WIDE)
        stiff = permute_lanes(stiff_in[first : first + count].reshape(shape), matrix, 2)
        mask = permute_lanes(mask_in[first : first + count].reshape(shape), matrix, 1)
        lame = lame_base * stiff
        shear = jnp.where(mask == 1.0, (shear_base * yield_ratio) * stiff, shear_base * stiff)
        lame_ref[first : first + count] = lame.reshape(count, ROWS, WIDE)
        shear_ref[first : first + count] = shear.reshape(count, ROWS, WIDE)
        for u in range(count):
            if HALO <= first + u < HALO + half:
                for jj in range(8):
                    acc_l = acc_l + load(lame_ref, first + u, jj)
                    acc_m = acc_m + load(shear_ref, first + u, jj)
    for copy in copies:
        copy.wait()
    elem = rve_element[lax.axis_index("macro")]

    scale = 1.0 / float(EDGE * EDGE * EDGE)
    lame, shear = total(acc_l) * scale, total(acc_m) * scale
    mine = corner_columns(grads)
    corner = lax.broadcasted_iota(jnp.int32, (8, 128), 0)
    lane = lax.broadcasted_iota(jnp.int32, (8, 128), 1)
    slot_of = jnp.zeros((8, 128), jnp.int32)
    for s in range(1, NEIGHBOUR_SLOTS + 1):
        slot_of = slot_of + jnp.where(lane >= 9 * s, 1, 0)
    inner = lane - 9 * slot_of
    a_of = jnp.where(inner >= 3, 1, 0) + jnp.where(inner >= 6, 1, 0)
    b_of = inner - 3 * a_of

    def by(which, x, y, z):
        return jnp.where(which == 0, x, jnp.where(which == 1, y, z))

    lame_a = lame * by(a_of, *mine)
    shear_b = shear * by(b_of, *mine)
    diagonal = jnp.where(a_of == b_of, shear, 0.0)
    rows = jnp.zeros((8, 128), jnp.float32)
    for l in range(8):
        other = [grads[c, l] for c in range(3)]
        dots = mine[0] * other[0] + mine[1] * other[1] + mine[2] * other[2]
        block = lame_a * by(b_of, *other) + shear_b * by(a_of, *other) + diagonal * dots
        slot = jnp.full((8, 128), block_slot[elem, 0, l], jnp.int32)
        for k in range(1, 8):
            slot = jnp.where(corner == k, block_slot[elem, k, l], slot)
        rows = rows + jnp.where(slot_of == slot, block, 0.0)
    rows = jnp.where(lane == LAME_MEAN, lame, rows)
    rows = jnp.where(lane == SHEAR_MEAN, shear, rows)
    rows_ref[...] = rows


def sweep_kernel(
    grads,
    rve_element,
    connectivity,
    gathered,
    lame_ref,
    shear_ref,
    rows_ref,
    w30_ref,
    w31_ref,
    w32_ref,
    strain_ref,
    strain_out,
    packet_ref,
    w10_v,
    w11_v,
    w12_v,
    w20_v,
    w21_v,
    w22_v,
    carry_v,
):
    half = lame_ref.shape[0] - 2 * HALO - MARGIN
    elem = rve_element[lax.axis_index("macro")]
    nodes = [connectivity[elem, k] for k in range(8)]
    moves = [[gathered[n, a] for n in nodes] for a in range(3)]

    def dot(c, a):
        result = grads[c, 0] * moves[a][0]
        for k in range(1, 8):
            result = result + grads[c, k] * moves[a][k]
        return result

    strain = [
        dot(0, 0),
        dot(1, 1),
        dot(2, 2),
        dot(2, 1) + dot(1, 2),
        dot(2, 0) + dot(0, 2),
        dot(1, 0) + dot(0, 1),
    ]
    for c in range(6):
        strain_ref[0, c] = strain[c]
        strain_out[8 * c : 8 * c + 8, :] = jnp.full((8, 128), strain[c], jnp.float32)
    w1_v = [w10_v, w11_v, w12_v]
    w2_v = [w20_v, w21_v, w22_v]
    w3_v = [w30_ref, w31_ref, w32_ref]

    scale1 = gain1 * gain2 * precond / centre
    strain1 = [scale1 * e for e in strain]
    trace1 = strain1[0] + strain1[1] + strain1[2]
    twice1 = [2.0 * strain1[c] for c in range(3)]
    step1 = best_step(half + 5, STEP)

    def sweep1(t, _):
        for u in range(step1):
            at = t * step1 + 1 + u
            for jj in range(8):
                l0, l1, l2 = differences(lame_ref, at, jj)
                m0, m1, m2 = differences(shear_ref, at, jj)
                w1_v[0][spot(at, jj)] = (
                    trace1 * l0 + twice1[0] * m0 + (strain1[5] * m1 + strain1[4] * m2)
                )
                w1_v[1][spot(at, jj)] = (
                    trace1 * l1 + twice1[1] * m1 + (strain1[5] * m0 + strain1[3] * m2)
                )
                w1_v[2][spot(at, jj)] = (
                    trace1 * l2 + twice1[2] * m2 + (strain1[4] * m0 + strain1[3] * m1)
                )
        return 0

    lax.fori_loop(0, pl.cdiv(half + 5, step1), sweep1, 0)

    strain2 = [gain1 * gain2 * e for e in strain]
    ratio1 = (1.0 + keep1) / gain1
    step2 = best_step(half + 3, STEP)
    carry_plane(w1_v, lame_ref, shear_ref, carry_v, 1, strain2)

    def sweep2(t, _):
        for u in range(step2):
            at = t * step2 + 2 + u

            def update(jj, w, r):
                for c in range(3):
                    w2_v[c][spot(at, jj)] = ratio1 * w[c] + r[c]

            sweep_plane(
                w1_v, lame_ref, shear_ref, carry_v, u, (u + 1) % step2, at, strain2, update
            )
        return 0

    lax.fori_loop(0, pl.cdiv(half + 3, step2), sweep2, 0)

    strain3 = [gain2 * e for e in strain]
    ratio2 = (1.0 + keep2) / gain2
    ratio3 = keep2 / (gain1 * gain2)
    step3 = best_step(half + 1, STEP)
    carry_plane(w2_v, lame_ref, shear_ref, carry_v, 2, strain3)

    def sweep3(t, _):
        for u in range(step3):
            at = t * step3 + 3 + u

            def update(jj, w, r):
                old = load3(w1_v, at, jj)
                for c in range(3):
                    w3_v[c][spot(at, jj)] = (ratio2 * w[c] - ratio3 * old[c]) + r[c]

            sweep_plane(
                w2_v, lame_ref, shear_ref, carry_v, u, (u + 1) % step3, at, strain3, update
            )
        return 0

    lax.fori_loop(0, pl.cdiv(half + 1, step3), sweep3, 0)

    def by_parts(t, acc):
        bulk, a0, a1, a2, a3, a4, a5 = acc
        at = t + HALO
        for jj in range(8):
            w0, w1, w2 = load3(w3_v, at, jj)
            l0, l1, l2 = differences(lame_ref, at, jj)
            m0, m1, m2 = differences(shear_ref, at, jj)
            bulk = bulk + (l0 * w0 + l1 * w1 + l2 * w2)
            a0 = a0 + m0 * w0
            a1 = a1 + m1 * w1
            a2 = a2 + m2 * w2
            a3 = a3 + (m2 * w1 + m1 * w2)
            a4 = a4 + (m2 * w0 + m0 * w2)
            a5 = a5 + (m1 * w0 + m0 * w1)
        return bulk, a0, a1, a2, a3, a4, a5

    zero = jnp.zeros((8, 128), jnp.float32)
    acc = lax.fori_loop(0, half, by_parts, (zero,) * 7)
    scale = 1.0 / float(EDGE * EDGE * EDGE)
    bulk, *parts = [total(x) * scale for x in acc]
    rows = rows_ref[...]
    lame = rows[:1, LAME_MEAN : LAME_MEAN + 1]
    shear = rows[:1, SHEAR_MEAN : SHEAR_MEAN + 1]
    bulk = lame * (strain[0] + strain[1] + strain[2]) - bulk
    means = [bulk + 2.0 * (shear * strain[c] - parts[c]) for c in range(3)]
    means += [shear * strain[c] - parts[c] for c in range(3, 6)]

    xx, yy, zz, yz, xz, xy = means
    g0, g1, g2 = corner_columns(grads)
    lane = lax.broadcasted_iota(jnp.int32, (8, 128), 1)
    rows = jnp.where(lane == FORCE, xx * g0 + xy * g1 + xz * g2, rows)
    rows = jnp.where(lane == FORCE + 1, xy * g0 + yy * g1 + yz * g2, rows)
    rows = jnp.where(lane == FORCE + 2, xz * g0 + yz * g1 + zz * g2, rows)
    sums = jnp.zeros((8, 128), jnp.float32)
    for c in range(6):
        sums = jnp.where(lane == SUMS + c, means[c], sums)
    rows = jnp.where(lane >= SUMS, sums, rows)
    for g in range(packet_ref.shape[0] // 8):
        packet_ref[8 * g : 8 * g + 8, :] = sums
    count = lax.axis_size("macro")
    for v in range(lax.axis_size("vox")):
        for k in range(8):
            packet_ref[pl.ds(v * count + nodes[k], 1), :] = rows[k : k + 1]


def stress_kernel(
    strain_in,
    lame_ref,
    shear_ref,
    w30_ref,
    w31_ref,
    w32_ref,
    stress_ref,
    out_v,
    work_v,
    turn_v,
    sem,
):
    half = lame_ref.shape[0] - 2 * HALO - MARGIN
    w3_v = [w30_ref, w31_ref, w32_ref]
    strain = [strain_in[8 * c : 8 * c + 8, :] for c in range(6)]
    matrix = lane_matrix(True)
    copies = []
    for first in range(0, half, GROUP):
        slot = (first // GROUP) % 2
        for u in range(GROUP):
            at = first + u + HALO
            for jj in range(8):
                stress = stress_at(
                    w3_v,
                    at,
                    jj,
                    load3(w3_v, at, jj),
                    load(lame_ref, at, jj),
                    load(shear_ref, at, jj),
                    strain,
                )
                for c in range(6):
                    work_v[(slot, c, u, *spot(0, jj)[1:])] = stress[c]
        for c in range(6):
            y = permute_lanes(work_v[slot, c].reshape(GROUP * ROWS, WIDE), matrix, 2)
            for u in range(GROUP):
                for q in range(4):
                    row = (u * 4 + q) * 8
                    for h in range(2):
                        s = (first + u + h * half) % 8
                        turn_v[h, c, pl.ds(s * TURN_S + q * 8 * TURN_R, 8, stride=TURN_R), :] = y[
                            row : row + 8, 128 * h : 128 * h + 128
                        ]
        done = []
        if half % 8 == 0 and (first + GROUP) % 8 == 0:
            done = [((first + GROUP) // 8 - 1 + h * (half // 8), h) for h in range(2)]
        elif half % 8 and first + GROUP == half:
            done = [(0, None)]
        for group, h in done:
            for c in range(6):
                for q in range(4):
                    for r in range(8):
                        row = group * (8 * ROWS) + (4 * r + q) * 8
                        start = (q * 8 + r) * TURN_R
                        if h is None:
                            low = turn_v[0, c, pl.ds(start, 8, stride=TURN_S), :]
                            high = turn_v[1, c, pl.ds(start, 8, stride=TURN_S), :]
                            sub = lax.broadcasted_iota(jnp.int32, (8, 128), 0)
                            out_v[c, row : row + 8, :] = jnp.where(sub < half, low, high)
                        else:
                            out_v[c, row : row + 8, :] = turn_v[
                                h, c, pl.ds(start, 8, stride=TURN_S), :
                            ]
            span = pl.ds(group * (8 * ROWS), 8 * ROWS)
            copy = pltpu.make_async_copy(
                out_v.at[:, span, :], stress_ref.at[:, span, :], sem.at[len(copies)]
            )
            copy.start()
            copies.append(copy)
    for copy in copies:
        copy.wait()


TURN_R = 3
TURN_S = TURN_R * ROWS + 1
STEP = 3
GROUP = 4
MARGIN = 3


def node_kernel(packets_ref, hom_ref, force_ref, tangent_ref):
    packets = packets_ref[...]
    count = lax.axis_size("macro")
    place = lax.broadcasted_iota(jnp.int32, packets.shape, 0)
    point = lax.axis_index("macro")
    own = place == point
    for v in range(1, lax.axis_size("vox")):
        own = own | (place == v * count + point)
    row = jnp.sum(packets, axis=0, keepdims=True)
    means = jnp.sum(jnp.where(own, packets, 0.0), axis=0, keepdims=True)
    tangent_ref[...] = row[:, :BLOCK]
    force_ref[...] = row[:, FORCE : FORCE + 3]
    hom_ref[...] = means[:, SUMS : SUMS + 6]


def on_device(
    nodal_disp,
    weighted_shape_gradients,
    rve_element,
    connectivity,
    block_slot,
    stiffness,
    yielded_mask,
):
    rve_count, planes, plane_size = stiffness.shape
    macro_size = lax.axis_size("macro")
    vox_size = lax.axis_size("vox")
    everywhere = macro_size * vox_size
    assert rve_count == 1 and nodal_disp.shape[0] == 1
    assert planes % 8 == 0 and plane_size == EDGE * EDGE

    def flat(field):
        parted = field.reshape(planes // 8, 8, ROWS, 128)
        return parted.transpose(0, 2, 1, 3).reshape(planes * ROWS, 128)

    smem = pl.BlockSpec(memory_space=pltpu.SMEM)
    vmem = pl.BlockSpec(memory_space=pltpu.VMEM)
    hbm = pl.BlockSpec(memory_space=pltpu.HBM)
    anywhere = pl.BlockSpec(memory_space=pl.ANY)
    mib = 1024 * 1024
    f32 = jnp.float32
    half = planes // 2
    depth = half + 2 * HALO + MARGIN
    packed = 4 * HALO * ROWS
    layer = jax.ShapeDtypeStruct((depth, ROWS, WIDE), f32)
    field = pltpu.VMEM((depth, ROWS, WIDE), f32)
    half_field = pltpu.VMEM((half + 2 * HALO, ROWS, WIDE), f32)

    def cost(flops, size):
        return pl.CostEstimate(
            flops=flops * planes * plane_size,
            bytes_accessed=size * planes * plane_size,
            transcendentals=0,
        )

    disp, rims = pl.pallas_call(
        prepare_kernel,
        out_shape=(
            jax.ShapeDtypeStruct((macro_size, 3), f32),
            jax.ShapeDtypeStruct((packed, 128), f32),
        ),
        in_specs=[hbm] * 3,
        out_specs=(vmem,) * 2,
        scratch_shapes=[
            pltpu.VMEM((1, 3), f32),
            pltpu.VMEM((2, 8 * ROWS, 128), f32),
            pltpu.VMEM((2, 8 * ROWS, 128), jnp.int32),
            pltpu.SemaphoreType.DMA((5,)),
        ],
        compiler_params=pltpu.CompilerParams(vmem_limit_bytes=56 * mib),
        cost_estimate=cost(10**4, 1),
        name="prepare",
    )(nodal_disp, flat(stiffness), flat(yielded_mask))

    if vox_size == 2:
        halo = lax.ppermute(rims, "vox", [(0, 1), (1, 0)])
    else:
        forward = [(i, (i + 1) % vox_size) for i in range(vox_size)]
        backward = [(t, s) for s, t in forward]
        halo = jnp.concatenate(
            [
                lax.ppermute(rims[: packed // 2], "vox", forward),
                lax.ppermute(rims[packed // 2 :], "vox", backward),
            ],
            axis=0,
        )
    gathered = lax.all_to_all(disp, "macro", split_axis=0, concat_axis=0, tiled=True)

    grads = weighted_shape_gradients[0]
    lame, shear, rows = pl.pallas_call(
        material_kernel,
        out_shape=(layer, layer, jax.ShapeDtypeStruct((8, 128), f32)),
        in_specs=[smem, hbm, hbm, vmem, vmem, vmem],
        out_specs=(vmem,) * 3,
        scratch_shapes=[
            half_field,
            half_field,
            pltpu.SMEM(rve_element.shape, jnp.int32),
            pltpu.SMEM(block_slot.shape, jnp.int32),
            pltpu.SemaphoreType.DMA((2,)),
        ],
        compiler_params=pltpu.CompilerParams(vmem_limit_bytes=8 * mib),
        cost_estimate=cost(10**4, 1),
        name="material",
    )(grads, rve_element, block_slot, flat(stiffness), flat(yielded_mask), halo)

    *w3, strain, strain_rows, packet = pl.pallas_call(
        sweep_kernel,
        out_shape=(
            layer,
            layer,
            layer,
            jax.ShapeDtypeStruct((1, 6), f32),
            jax.ShapeDtypeStruct((48, 128), f32),
            jax.ShapeDtypeStruct((everywhere, 128), f32),
        ),
        in_specs=[smem] * 4 + [vmem] * 3,
        out_specs=(vmem, vmem, vmem, smem, vmem, vmem),
        scratch_shapes=[field] * 6 + [pltpu.VMEM((STEP, 3, ROWS, WIDE), f32)],
        compiler_params=pltpu.CompilerParams(vmem_limit_bytes=12 * mib),
        cost_estimate=cost(2 * 10**4, 1),
        name="sweeps",
    )(grads, rve_element, connectivity, gathered, lame, shear, rows)

    packets = lax.all_to_all(
        packet, ("vox", "macro"), split_axis=0, concat_axis=0, tiled=True
    )

    stress = pl.pallas_call(
        stress_kernel,
        out_shape=jax.ShapeDtypeStruct((6, planes * ROWS, 128), f32),
        in_specs=[vmem] * 6,
        out_specs=hbm,
        scratch_shapes=[
            pltpu.VMEM((6, planes * ROWS, 128), f32),
            pltpu.VMEM((2, 6, GROUP, ROWS, WIDE), f32),
            pltpu.VMEM((2, 6, 8 * TURN_S, 128), f32),
            pltpu.SemaphoreType.DMA((planes // 8,)),
        ],
        compiler_params=pltpu.CompilerParams(vmem_limit_bytes=16 * mib),
        cost_estimate=cost(10**4, 1),
        name="stress",
    )(strain_rows, lame, shear, *w3)
    voxel_stress = (
        stress.reshape(6, planes // 8, ROWS, 8, 128)
        .transpose(0, 1, 3, 2, 4)
        .reshape(1, 6, planes, plane_size)
    )

    homogenized, internal_node_force, tangent = pl.pallas_call(
        node_kernel,
        out_shape=(
            jax.ShapeDtypeStruct((1, 6), f32),
            jax.ShapeDtypeStruct((1, 3), f32),
            jax.ShapeDtypeStruct((1, BLOCK), f32),
        ),
        in_specs=[vmem],
        out_specs=(vmem, vmem, vmem),
        compiler_params=pltpu.CompilerParams(vmem_limit_bytes=4 * mib),
        name="nodes",
    )(packets)
    return (voxel_stress, homogenized, strain, internal_node_force, tangent)


def solution(mesh):
    in_specs = (
        P("macro", None),
        P("macro", None, None),
        P(),
        P(),
        P(),
        P("macro", "vox", None),
        P("macro", "vox", None),
    )
    out_specs = (
        P("macro", None, "vox", None),
        P("macro", None),
        P("macro", None),
        P("macro", None),
        P("macro", None),
    )
    return jax.shard_map(
        on_device, mesh=mesh, in_specs=in_specs, out_specs=out_specs, check_vma=False
    )
```

```python
import jax
import jax.numpy as jnp
from jax import lax
from jax.experimental import pallas as pl
from jax.experimental.pallas import tpu as pltpu
from jax.sharding import PartitionSpec as P

EDGE = 64
SWEEPS = 3
NEIGHBOUR_SLOTS = 12
BLOCK = NEIGHBOUR_SLOTS * 9

lame_base = 1.5
shear_base = 1.0
yield_ratio = 0.2
precond = 1.0 / 42.0
lower_bound = 0.05
upper_bound = 2.0

ROWS = EDGE * EDGE // 128
WIDE = 256
HALO = 3


def chebyshev_terms(count):
    centre = 0.5 * (upper_bound + lower_bound)
    half_width = 0.5 * (upper_bound - lower_bound)
    ratio_bound = centre / half_width
    rho_prev = 1.0 / ratio_bound
    weights = []
    for number in range(count):
        rho_next = 1.0 / (2.0 * ratio_bound - rho_prev)
        weights.append((rho_next * rho_prev, 2.0 * rho_next / half_width))
        rho_prev = rho_next
    return (centre, weights)


centre, ((keep1, push1), (keep2, push2)) = chebyshev_terms(SWEEPS - 1)
gain1 = push1 * precond
gain2 = push2 * precond

def spot(at, jj):
    half = (jj & 1) * 128
    return at, pl.ds(8 * (jj // 2), 8), pl.ds(half, 128)


def load(ref, at, jj):
    return ref[spot(at, jj)]


def load3(refs, at, jj):
    return [load(ref, at, jj) for ref in refs]


def prev_row(ref, at, jj):
    if jj > 0:
        return load(ref, at, jj - 1)
    return pltpu.roll(load(ref, at, 7), 1, 0)


def next_lane(x):
    return pltpu.roll(x, 126, 1)


def prev_lane(x):
    return pltpu.roll(x, 2, 1)


def differences(ref, at, jj):
    here = load(ref, at, jj)
    return (
        here - load(ref, at - 1, jj),
        here - prev_row(ref, at, jj),
        here - prev_lane(here),
    )


def plane_stress(w_refs, at, lame_ref, shear_ref, lame_at, strain):
    ahead = first = load3(w_refs, at, 0)
    for jj in range(8):
        w0, w1, w2 = w = ahead
        ahead = load3(w_refs, at, jj + 1) if jj < 7 else [pltpu.roll(x, 7, 0) for x in first]
        row0, row1, row2 = ahead
        n0, n1, n2 = load3(w_refs, at + 1, jj)
        lane0, lane1, lane2 = [next_lane(x) for x in w]
        lame = load(lame_ref, lame_at, jj)
        shear = load(shear_ref, lame_at, jj)
        e0 = (n0 - w0) + strain[0]
        e1 = (row1 - w1) + strain[1]
        e2 = (lane2 - w2) + strain[2]
        g3 = (lane1 + row2) - (w1 + w2) + strain[3]
        g4 = (lane0 + n2) - (w0 + w2) + strain[4]
        g5 = (row0 + n1) - (w0 + w1) + strain[5]
        bulk = lame * (e0 + e1 + e2)
        twice = shear + shear
        yield jj, w, (
            bulk + twice * e0,
            bulk + twice * e1,
            bulk + twice * e2,
            shear * g3,
            shear * g4,
            shear * g5,
        )


def residual_plane(registers, carry_v, old, new):
    begin = None
    row_xy = row_yy = row_yz = None
    for jj, w, stress in registers:
        xx, yy, zz, yz, xz, xy = stress
        pxx, pxz, pxy = [load(carry_v.at[old], c, jj) for c in range(3)]
        for c, x in enumerate((xx, xz, xy)):
            carry_v[(new, *spot(c, jj))] = x
        r = [
            (xx - pxx) + (xz - prev_lane(xz)) + xy,
            (xy - pxy) + (yz - prev_lane(yz)) + yy,
            (xz - pxz) + (zz - prev_lane(zz)) + yz,
        ]
        if jj == 0:
            begin = w, r
        else:
            yield jj, w, [r[0] - row_xy, r[1] - row_yy, r[2] - row_yz]
        row_xy, row_yy, row_yz = xy, yy, yz
    rows = [pltpu.roll(x, 1, 0) for x in (row_xy, row_yy, row_yz)]
    yield 0, begin[0], [x - y for x, y in zip(begin[1], rows)]


def target_lane(m):
    return ((m >> 6) & 1) * 128 + (m & 63) * 2 + (m >> 7)


def lane_matrix(inverse):
    row = lax.broadcasted_iota(jnp.int32, (WIDE, WIDE), 0)
    column = lax.broadcasted_iota(jnp.int32, (WIDE, WIDE), 1)
    hit = (target_lane(column) == row) if inverse else (target_lane(row) == column)
    return jnp.where(hit, 1.0, 0.0).astype(jnp.bfloat16)


def permute_lanes(x, matrix, terms):
    result = None
    for t in range(terms):
        part = x.astype(jnp.bfloat16)
        moved = jnp.dot(part, matrix, preferred_element_type=jnp.float32)
        result = moved if result is None else result + moved
        if t + 1 < terms:
            x = x - part.astype(jnp.float32)
    return result


def native(plane, q):
    return pl.ds((plane // 8) * (8 * ROWS) + plane % 8 + 8 * q, 8, stride=ROWS)


def total(x):
    return jnp.sum(x, axis=(0, 1), keepdims=True)


def corner_columns(grads):
    corner = lax.broadcasted_iota(jnp.int32, (8, 128), 0)
    columns = []
    for c in range(3):
        column = jnp.full((8, 128), grads[c, 0], jnp.float32)
        for k in range(1, 8):
            column = jnp.where(corner == k, grads[c, k], column)
        columns.append(column)
    return columns


FORCE = BLOCK
SUMS = BLOCK + 4
LAME_MEAN = 120
SHEAR_MEAN = 121


def prepare_kernel(disp_hbm, stiff_hbm, mask_hbm, disp_ref, halo_ref, disp_v, ends_v, mask_v, sems):
    groups = stiff_hbm.shape[0] // (8 * ROWS)
    ends = [pl.ds((groups - 1) * (8 * ROWS), 8 * ROWS), pl.ds(0, 8 * ROWS)]
    copies = [pltpu.make_async_copy(disp_hbm, disp_v, sems.at[0])]
    for e in range(2):
        copies += [
            pltpu.make_async_copy(stiff_hbm.at[ends[e], :], ends_v.at[e], sems.at[1 + 2 * e]),
            pltpu.make_async_copy(mask_hbm.at[ends[e], :], mask_v.at[e], sems.at[2 + 2 * e]),
        ]
    for copy in copies:
        copy.start()
    for copy in copies:
        copy.wait()
    disp_ref[...] = jnp.broadcast_to(disp_v[...], disp_ref.shape)
    row = 0
    for e, first in ((0, 8 - HALO), (1, 0)):
        for field in (ends_v, mask_v):
            for plane in range(first, first + HALO):
                for q in range(4):
                    x = field[e, native(plane, q), :]
                    halo_ref[row : row + 8, :] = x.astype(jnp.float32)
                    row += 8


def material_kernel(
    grads,
    rve_hbm,
    slot_hbm,
    stiff_v,
    mask_v,
    halo_ref,
    lame_ref,
    shear_ref,
    rows_ref,
    stiff_in,
    mask_in,
    rve_element,
    block_slot,
    sems,
):
    copies = [
        pltpu.make_async_copy(rve_hbm, rve_element, sems.at[0]),
        pltpu.make_async_copy(slot_hbm, block_slot, sems.at[1]),
    ]
    for copy in copies:
        copy.start()
    planes = stiff_v.shape[0] // ROWS
    half = planes // 2
    depth = half + 2 * HALO
    matrix = lane_matrix(False)

    for h in range(2):
        for at in range(depth):
            plane = at - HALO + h * half
            for q in range(4):
                if 0 <= plane < planes:
                    stiff = stiff_v[native(plane, q), :]
                    mask = mask_v[native(plane, q), :].astype(jnp.float32)
                else:
                    side, far = (0, plane + HALO) if plane < 0 else (1, plane - planes)
                    base = (side * 2 * HALO + far) * ROWS + 8 * q
                    stiff = halo_ref[base : base + 8, :]
                    mask = halo_ref[base + HALO * ROWS : base + HALO * ROWS + 8, :]
                place = (at, pl.ds(8 * q, 8), pl.ds(128 * h, 128))
                stiff_in[place] = stiff
                mask_in[place] = mask

    acc_l = acc_m = jnp.zeros((8, 128), jnp.float32)
    for first in range(0, depth, 2):
        count = min(2, depth - first)
        shape = (count * ROWS, WIDE)
        stiff = permute_lanes(stiff_in[first : first + count].reshape(shape), matrix, 2)
        mask = permute_lanes(mask_in[first : first + count].reshape(shape), matrix, 1)
        lame = lame_base * stiff
        shear = jnp.where(mask == 1.0, (shear_base * yield_ratio) * stiff, shear_base * stiff)
        lame_ref[first : first + count] = lame.reshape(count, ROWS, WIDE)
        shear_ref[first : first + count] = shear.reshape(count, ROWS, WIDE)
        for u in range(count):
            if HALO <= first + u < HALO + half:
                for jj in range(8):
                    acc_l = acc_l + load(lame_ref, first + u, jj)
                    acc_m = acc_m + load(shear_ref, first + u, jj)
    for copy in copies:
        copy.wait()
    elem = rve_element[lax.axis_index("macro")]

    scale = 1.0 / float(EDGE * EDGE * EDGE)
    lame, shear = total(acc_l) * scale, total(acc_m) * scale
    mine = corner_columns(grads)
    corner = lax.broadcasted_iota(jnp.int32, (8, 128), 0)
    lane = lax.broadcasted_iota(jnp.int32, (8, 128), 1)
    slot_of = jnp.zeros((8, 128), jnp.int32)
    for s in range(1, NEIGHBOUR_SLOTS + 1):
        slot_of = slot_of + jnp.where(lane >= 9 * s, 1, 0)
    inner = lane - 9 * slot_of
    a_of = jnp.where(inner >= 3, 1, 0) + jnp.where(inner >= 6, 1, 0)
    b_of = inner - 3 * a_of

    def by(which, x, y, z):
        return jnp.where(which == 0, x, jnp.where(which == 1, y, z))

    lame_a = lame * by(a_of, *mine)
    shear_b = shear * by(b_of, *mine)
    diagonal = jnp.where(a_of == b_of, shear, 0.0)
    rows = jnp.zeros((8, 128), jnp.float32)
    for l in range(8):
        other = [grads[c, l] for c in range(3)]
        dots = mine[0] * other[0] + mine[1] * other[1] + mine[2] * other[2]
        block = lame_a * by(b_of, *other) + shear_b * by(a_of, *other) + diagonal * dots
        slot = jnp.full((8, 128), block_slot[elem, 0, l], jnp.int32)
        for k in range(1, 8):
            slot = jnp.where(corner == k, block_slot[elem, k, l], slot)
        rows = rows + jnp.where(slot_of == slot, block, 0.0)
    rows = jnp.where(lane == LAME_MEAN, lame, rows)
    rows = jnp.where(lane == SHEAR_MEAN, shear, rows)
    rows_ref[...] = rows


def sweep_kernel(
    grads,
    rve_element,
    connectivity,
    gathered,
    lame_ref,
    shear_ref,
    rows_ref,
    w30_ref,
    w31_ref,
    w32_ref,
    strain_ref,
    strain_out,
    packet_ref,
    w10_v,
    w11_v,
    w12_v,
    w20_v,
    w21_v,
    w22_v,
    carry2_v,
    carry3_v,
):
    half = lame_ref.shape[0] - 2 * HALO
    elem = rve_element[lax.axis_index("macro")]
    nodes = [connectivity[elem, k] for k in range(8)]
    moves = [[gathered[n, a] for n in nodes] for a in range(3)]

    def dot(c, a):
        result = grads[c, 0] * moves[a][0]
        for k in range(1, 8):
            result = result + grads[c, k] * moves[a][k]
        return result

    strain = [
        dot(0, 0),
        dot(1, 1),
        dot(2, 2),
        dot(2, 1) + dot(1, 2),
        dot(2, 0) + dot(0, 2),
        dot(1, 0) + dot(0, 1),
    ]
    for c in range(6):
        strain_ref[0, c] = strain[c]
        strain_out[8 * c : 8 * c + 8, :] = jnp.full((8, 128), strain[c], jnp.float32)
    w1_v = [w10_v, w11_v, w12_v]
    w2_v = [w20_v, w21_v, w22_v]
    w3_v = [w30_ref, w31_ref, w32_ref]

    scale1 = gain1 * gain2 * precond / centre
    strain1 = [scale1 * e for e in strain]
    trace1 = strain1[0] + strain1[1] + strain1[2]
    twice1 = [2.0 * strain1[c] for c in range(3)]
    strain2 = [gain1 * gain2 * e for e in strain]
    ratio1 = (1.0 + keep1) / gain1
    strain3 = [gain2 * e for e in strain]
    ratio2 = (1.0 + keep2) / gain2
    ratio3 = keep2 / (gain1 * gain2)

    def sweep1(at):
        for jj in range(8):
            l0, l1, l2 = differences(lame_ref, at, jj)
            m0, m1, m2 = differences(shear_ref, at, jj)
            w1_v[0][spot(at, jj)] = (
                trace1 * l0 + twice1[0] * m0 + (strain1[5] * m1 + strain1[4] * m2)
            )
            w1_v[1][spot(at, jj)] = (
                trace1 * l1 + twice1[1] * m1 + (strain1[5] * m0 + strain1[3] * m2)
            )
            w1_v[2][spot(at, jj)] = (
                trace1 * l2 + twice1[2] * m2 + (strain1[4] * m0 + strain1[3] * m1)
            )

    def below(w_refs, at, carry, strain_here):
        for jj, _, stress in plane_stress(w_refs, at, lame_ref, shear_ref, at, strain_here):
            for c, x in enumerate((stress[0], stress[4], stress[5])):
                carry[(at % SLOTS, *spot(c, jj))] = x

    def sweep2(at):
        registers = plane_stress(w1_v, at, lame_ref, shear_ref, at, strain2)
        for jj, w, r in residual_plane(registers, carry2_v, (at - 1) % SLOTS, at % SLOTS):
            for c in range(3):
                w2_v[c][spot(at, jj)] = ratio1 * w[c] + r[c]

    def sweep3(at):
        registers = plane_stress(w2_v, at, lame_ref, shear_ref, at, strain3)
        for jj, w, r in residual_plane(registers, carry3_v, (at - 1) % SLOTS, at % SLOTS):
            for c in range(3):
                old = load(w1_v[c], at, jj)
                w3_v[c][spot(at - HALO, jj)] = (ratio2 * w[c] - ratio3 * old) + r[c]

    def by_parts(at, acc):
        bulk, a0, a1, a2, a3, a4, a5 = acc
        for jj in range(8):
            w0, w1, w2 = load3(w3_v, at - HALO, jj)
            l0, l1, l2 = differences(lame_ref, at, jj)
            m0, m1, m2 = differences(shear_ref, at, jj)
            bulk = bulk + (l0 * w0 + l1 * w1 + l2 * w2)
            a0 = a0 + m0 * w0
            a1 = a1 + m1 * w1
            a2 = a2 + m2 * w2
            a3 = a3 + (m2 * w1 + m1 * w2)
            a4 = a4 + (m2 * w0 + m0 * w2)
            a5 = a5 + (m1 * w0 + m0 * w1)
        return bulk, a0, a1, a2, a3, a4, a5

    acc = (jnp.zeros((8, 128), jnp.float32),) * 7
    last = half + HALO
    for at in range(1, last + 8):
        if at <= last + 2:
            sweep1(at)
        if at - 2 == 1:
            below(w1_v, 1, carry2_v, strain2)
        if 2 <= at - 2 <= last + 1:
            sweep2(at - 2)
        if at - 4 == 2:
            below(w2_v, 2, carry3_v, strain3)
        if 3 <= at - 4 <= last:
            sweep3(at - 4)
        if HALO <= at - 5 < last:
            acc = by_parts(at - 5, acc)
    scale = 1.0 / float(EDGE * EDGE * EDGE)
    bulk, *parts = [total(x) * scale for x in acc]
    rows = rows_ref[...]
    lame = rows[:1, LAME_MEAN : LAME_MEAN + 1]
    shear = rows[:1, SHEAR_MEAN : SHEAR_MEAN + 1]
    bulk = lame * (strain[0] + strain[1] + strain[2]) - bulk
    means = [bulk + 2.0 * (shear * strain[c] - parts[c]) for c in range(3)]
    means += [shear * strain[c] - parts[c] for c in range(3, 6)]

    xx, yy, zz, yz, xz, xy = means
    g0, g1, g2 = corner_columns(grads)
    lane = lax.broadcasted_iota(jnp.int32, (8, 128), 1)
    rows = jnp.where(lane == FORCE, xx * g0 + xy * g1 + xz * g2, rows)
    rows = jnp.where(lane == FORCE + 1, xy * g0 + yy * g1 + yz * g2, rows)
    rows = jnp.where(lane == FORCE + 2, xz * g0 + yz * g1 + zz * g2, rows)
    sums = jnp.zeros((8, 128), jnp.float32)
    for c in range(6):
        sums = jnp.where(lane == SUMS + c, means[c], sums)
    rows = jnp.where(lane >= SUMS, sums, rows)
    for g in range(packet_ref.shape[0] // 8):
        packet_ref[8 * g : 8 * g + 8, :] = sums
    count = lax.axis_size("macro")
    for v in range(lax.axis_size("vox")):
        for k in range(8):
            packet_ref[pl.ds(v * count + nodes[k], 1), :] = rows[k : k + 1]


def stress_kernel(
    strain_in,
    lame_ref,
    shear_ref,
    w30_ref,
    w31_ref,
    w32_ref,
    stress_ref,
    out_v,
    work_v,
    turn_v,
    sem,
):
    half = lame_ref.shape[0] - 2 * HALO
    w3_v = [w30_ref, w31_ref, w32_ref]
    strain = [strain_in[8 * c : 8 * c + 8, :] for c in range(6)]
    matrix = lane_matrix(True)
    copies = []
    for first in range(0, half, GROUP):
        slot = (first // GROUP) % 2
        for u in range(GROUP):
            at = first + u
            for jj, _, stress in plane_stress(w3_v, at, lame_ref, shear_ref, at + HALO, strain):
                for c in range(6):
                    work_v[(slot, c, u, *spot(0, jj)[1:])] = stress[c]
        for c in range(6):
            y = permute_lanes(work_v[slot, c].reshape(GROUP * ROWS, WIDE), matrix, 2)
            for u in range(GROUP):
                for q in range(4):
                    row = (u * 4 + q) * 8
                    for h in range(2):
                        s = (first + u + h * half) % 8
                        turn_v[h, c, pl.ds(s * TURN_S + q * 8 * TURN_R, 8, stride=TURN_R), :] = y[
                            row : row + 8, 128 * h : 128 * h + 128
                        ]
        done = []
        if half % 8 == 0 and (first + GROUP) % 8 == 0:
            done = [((first + GROUP) // 8 - 1 + h * (half // 8), h) for h in range(2)]
        elif half % 8 and first + GROUP == half:
            done = [(0, None)]
        for group, h in done:
            for c in range(6):
                for q in range(4):
                    for r in range(8):
                        row = group * (8 * ROWS) + (4 * r + q) * 8
                        start = (q * 8 + r) * TURN_R
                        if h is None:
                            low = turn_v[0, c, pl.ds(start, 8, stride=TURN_S), :]
                            high = turn_v[1, c, pl.ds(start, 8, stride=TURN_S), :]
                            sub = lax.broadcasted_iota(jnp.int32, (8, 128), 0)
                            out_v[c, row : row + 8, :] = jnp.where(sub < half, low, high)
                        else:
                            out_v[c, row : row + 8, :] = turn_v[
                                h, c, pl.ds(start, 8, stride=TURN_S), :
                            ]
            span = pl.ds(group * (8 * ROWS), 8 * ROWS)
            copy = pltpu.make_async_copy(
                out_v.at[:, span, :], stress_ref.at[:, span, :], sem.at[len(copies)]
            )
            copy.start()
            copies.append(copy)
    for copy in copies:
        copy.wait()


TURN_R = 3
TURN_S = TURN_R * ROWS + 1
SLOTS = 4
GROUP = 4


def node_kernel(packets_ref, hom_ref, force_ref, tangent_ref):
    packets = packets_ref[...]
    count = lax.axis_size("macro")
    place = lax.broadcasted_iota(jnp.int32, packets.shape, 0)
    point = lax.axis_index("macro")
    own = place == point
    for v in range(1, lax.axis_size("vox")):
        own = own | (place == v * count + point)
    row = jnp.sum(packets, axis=0, keepdims=True)
    means = jnp.sum(jnp.where(own, packets, 0.0), axis=0, keepdims=True)
    tangent_ref[...] = row[:, :BLOCK]
    force_ref[...] = row[:, FORCE : FORCE + 3]
    hom_ref[...] = means[:, SUMS : SUMS + 6]


def on_device(
    nodal_disp,
    weighted_shape_gradients,
    rve_element,
    connectivity,
    block_slot,
    stiffness,
    yielded_mask,
):
    rve_count, planes, plane_size = stiffness.shape
    macro_size = lax.axis_size("macro")
    vox_size = lax.axis_size("vox")
    everywhere = macro_size * vox_size
    assert rve_count == 1 and nodal_disp.shape[0] == 1
    assert planes % 8 == 0 and plane_size == EDGE * EDGE

    def flat(field):
        parted = field.reshape(planes // 8, 8, ROWS, 128)
        return parted.transpose(0, 2, 1, 3).reshape(planes * ROWS, 128)

    smem = pl.BlockSpec(memory_space=pltpu.SMEM)
    vmem = pl.BlockSpec(memory_space=pltpu.VMEM)
    hbm = pl.BlockSpec(memory_space=pltpu.HBM)
    anywhere = pl.BlockSpec(memory_space=pl.ANY)
    mib = 1024 * 1024
    f32 = jnp.float32
    half = planes // 2
    depth = half + 2 * HALO
    packed = 4 * HALO * ROWS
    layer = jax.ShapeDtypeStruct((depth, ROWS, WIDE), f32)
    field = pltpu.VMEM((depth, ROWS, WIDE), f32)
    carry = pltpu.VMEM((SLOTS, 3, ROWS, WIDE), f32)
    last_layer = jax.ShapeDtypeStruct((half + 1, ROWS, WIDE), f32)

    def cost(flops, size):
        return pl.CostEstimate(
            flops=flops * planes * plane_size,
            bytes_accessed=size * planes * plane_size,
            transcendentals=0,
        )

    disp, rims = pl.pallas_call(
        prepare_kernel,
        out_shape=(
            jax.ShapeDtypeStruct((macro_size, 3), f32),
            jax.ShapeDtypeStruct((packed, 128), f32),
        ),
        in_specs=[hbm] * 3,
        out_specs=(vmem,) * 2,
        scratch_shapes=[
            pltpu.VMEM((1, 3), f32),
            pltpu.VMEM((2, 8 * ROWS, 128), f32),
            pltpu.VMEM((2, 8 * ROWS, 128), jnp.int32),
            pltpu.SemaphoreType.DMA((5,)),
        ],
        compiler_params=pltpu.CompilerParams(vmem_limit_bytes=56 * mib),
        cost_estimate=cost(10**4, 1),
        name="prepare",
    )(nodal_disp, flat(stiffness), flat(yielded_mask))

    if vox_size == 2:
        halo = lax.ppermute(rims, "vox", [(0, 1), (1, 0)])
    else:
        forward = [(i, (i + 1) % vox_size) for i in range(vox_size)]
        backward = [(t, s) for s, t in forward]
        halo = jnp.concatenate(
            [
                lax.ppermute(rims[: packed // 2], "vox", forward),
                lax.ppermute(rims[packed // 2 :], "vox", backward),
            ],
            axis=0,
        )
    gathered = lax.all_to_all(disp, "macro", split_axis=0, concat_axis=0, tiled=True)

    grads = weighted_shape_gradients[0]
    lame, shear, rows = pl.pallas_call(
        material_kernel,
        out_shape=(layer, layer, jax.ShapeDtypeStruct((8, 128), f32)),
        in_specs=[smem, hbm, hbm, vmem, vmem, vmem],
        out_specs=(vmem,) * 3,
        scratch_shapes=[
            field,
            field,
            pltpu.SMEM(rve_element.shape, jnp.int32),
            pltpu.SMEM(block_slot.shape, jnp.int32),
            pltpu.SemaphoreType.DMA((2,)),
        ],
        compiler_params=pltpu.CompilerParams(vmem_limit_bytes=8 * mib),
        cost_estimate=cost(10**4, 1),
        name="material",
    )(grads, rve_element, block_slot, flat(stiffness), flat(yielded_mask), halo)

    *w3, strain, strain_rows, packet = pl.pallas_call(
        sweep_kernel,
        out_shape=(
            last_layer,
            last_layer,
            last_layer,
            jax.ShapeDtypeStruct((1, 6), f32),
            jax.ShapeDtypeStruct((48, 128), f32),
            jax.ShapeDtypeStruct((everywhere, 128), f32),
        ),
        in_specs=[smem] * 4 + [vmem] * 3,
        out_specs=(vmem, vmem, vmem, smem, vmem, vmem),
        scratch_shapes=[field] * 6 + [carry] * 2,
        compiler_params=pltpu.CompilerParams(vmem_limit_bytes=12 * mib),
        cost_estimate=cost(2 * 10**4, 1),
        name="sweeps",
    )(grads, rve_element, connectivity, gathered, lame, shear, rows)

    packets = lax.all_to_all(
        packet, ("vox", "macro"), split_axis=0, concat_axis=0, tiled=True
    )

    stress = pl.pallas_call(
        stress_kernel,
        out_shape=jax.ShapeDtypeStruct((6, planes * ROWS, 128), f32),
        in_specs=[vmem] * 6,
        out_specs=hbm,
        scratch_shapes=[
            pltpu.VMEM((6, planes * ROWS, 128), f32),
            pltpu.VMEM((2, 6, GROUP, ROWS, WIDE), f32),
            pltpu.VMEM((2, 6, 8 * TURN_S, 128), f32),
            pltpu.SemaphoreType.DMA((planes // 8,)),
        ],
        compiler_params=pltpu.CompilerParams(vmem_limit_bytes=16 * mib),
        cost_estimate=cost(10**4, 1),
        name="stress",
    )(strain_rows, lame, shear, *w3)
    voxel_stress = (
        stress.reshape(6, planes // 8, ROWS, 8, 128)
        .transpose(0, 1, 3, 2, 4)
        .reshape(1, 6, planes, plane_size)
    )

    homogenized, internal_node_force, tangent = pl.pallas_call(
        node_kernel,
        out_shape=(
            jax.ShapeDtypeStruct((1, 6), f32),
            jax.ShapeDtypeStruct((1, 3), f32),
            jax.ShapeDtypeStruct((1, BLOCK), f32),
        ),
        in_specs=[vmem],
        out_specs=(vmem, vmem, vmem),
        compiler_params=pltpu.CompilerParams(vmem_limit_bytes=4 * mib),
        name="nodes",
    )(packets)
    return (voxel_stress, homogenized, strain, internal_node_force, tangent)


def solution(mesh):
    in_specs = (
        P("macro", None),
        P("macro", None, None),
        P(),
        P(),
        P(),
        P("macro", "vox", None),
        P("macro", "vox", None),
    )
    out_specs = (
        P("macro", None, "vox", None),
        P("macro", None),
        P("macro", None),
        P("macro", None),
        P("macro", None),
    )
    return jax.shard_map(
        on_device, mesh=mesh, in_specs=in_specs, out_specs=out_specs, check_vma=False
    )
```

```python
import jax
import jax.numpy as jnp
from jax import lax
from jax.experimental import pallas as pl
from jax.experimental.pallas import tpu as pltpu
from jax.sharding import PartitionSpec as P

EDGE = 64
SWEEPS = 3
NEIGHBOUR_SLOTS = 12
BLOCK = NEIGHBOUR_SLOTS * 9

lame_base = 1.5
shear_base = 1.0
yield_ratio = 0.2
precond = 1.0 / 42.0
lower_bound = 0.05
upper_bound = 2.0

ROWS = EDGE * EDGE // 128
WIDE = 256
HALO = 3


def chebyshev_terms(count):
    centre = 0.5 * (upper_bound + lower_bound)
    half_width = 0.5 * (upper_bound - lower_bound)
    ratio_bound = centre / half_width
    rho_prev = 1.0 / ratio_bound
    weights = []
    for number in range(count):
        rho_next = 1.0 / (2.0 * ratio_bound - rho_prev)
        weights.append((rho_next * rho_prev, 2.0 * rho_next / half_width))
        rho_prev = rho_next
    return (centre, weights)


centre, ((keep1, push1), (keep2, push2)) = chebyshev_terms(SWEEPS - 1)
gain1 = push1 * precond
gain2 = push2 * precond

def spot(at, jj):
    half = (jj & 1) * 128
    return at, pl.ds(8 * (jj // 2), 8), pl.ds(half, 128)


def load(ref, at, jj):
    return ref[spot(at, jj)]


def load3(refs, at, jj):
    return [load(ref, at, jj) for ref in refs]


def prev_row(ref, at, jj):
    if jj > 0:
        return load(ref, at, jj - 1)
    return pltpu.roll(load(ref, at, 7), 1, 0)


def next_lane(x):
    return pltpu.roll(x, 126, 1)


def prev_lane(x):
    return pltpu.roll(x, 2, 1)


def differences(ref, at, jj):
    here = load(ref, at, jj)
    return (
        here - load(ref, at - 1, jj),
        here - prev_row(ref, at, jj),
        here - prev_lane(here),
    )


def plane_stress(w_refs, at, lame_ref, shear_ref, lame_at, strain):
    ahead = first = load3(w_refs, at, 0)
    for jj in range(8):
        w0, w1, w2 = w = ahead
        ahead = load3(w_refs, at, jj + 1) if jj < 7 else [pltpu.roll(x, 7, 0) for x in first]
        row0, row1, row2 = ahead
        n0, n1, n2 = load3(w_refs, at + 1, jj)
        lane0, lane1, lane2 = [next_lane(x) for x in w]
        lame = load(lame_ref, lame_at, jj)
        shear = load(shear_ref, lame_at, jj)
        e0 = (n0 - w0) + strain[0]
        e1 = (row1 - w1) + strain[1]
        e2 = (lane2 - w2) + strain[2]
        g3 = (lane1 + row2) - (w1 + w2) + strain[3]
        g4 = (lane0 + n2) - (w0 + w2) + strain[4]
        g5 = (row0 + n1) - (w0 + w1) + strain[5]
        bulk = lame * (e0 + e1 + e2)
        twice = shear + shear
        yield jj, w, (
            bulk + twice * e0,
            bulk + twice * e1,
            bulk + twice * e2,
            shear * g3,
            shear * g4,
            shear * g5,
        )


def residual_plane(registers, carry_v):
    begin = None
    row_xy = row_yy = row_yz = None
    for jj, w, stress in registers:
        xx, yy, zz, yz, xz, xy = stress
        pxx, pxz, pxy = [load(carry_v, c, jj) for c in range(3)]
        for c, x in enumerate((xx, xz, xy)):
            carry_v[spot(c, jj)] = x
        r = [
            (xx - pxx) + (xz - prev_lane(xz)) + xy,
            (xy - pxy) + (yz - prev_lane(yz)) + yy,
            (xz - pxz) + (zz - prev_lane(zz)) + yz,
        ]
        if jj == 0:
            begin = w, r
        else:
            yield jj, w, [r[0] - row_xy, r[1] - row_yy, r[2] - row_yz]
        row_xy, row_yy, row_yz = xy, yy, yz
    rows = [pltpu.roll(x, 1, 0) for x in (row_xy, row_yy, row_yz)]
    yield 0, begin[0], [x - y for x, y in zip(begin[1], rows)]


def target_lane(m):
    return ((m >> 6) & 1) * 128 + (m & 63) * 2 + (m >> 7)


def lane_matrix(inverse):
    row = lax.broadcasted_iota(jnp.int32, (WIDE, WIDE), 0)
    column = lax.broadcasted_iota(jnp.int32, (WIDE, WIDE), 1)
    hit = (target_lane(column) == row) if inverse else (target_lane(row) == column)
    return jnp.where(hit, 1.0, 0.0).astype(jnp.bfloat16)


def permute_lanes(x, matrix, terms):
    result = None
    for t in range(terms):
        part = x.astype(jnp.bfloat16)
        moved = jnp.dot(part, matrix, preferred_element_type=jnp.float32)
        result = moved if result is None else result + moved
        if t + 1 < terms:
            x = x - part.astype(jnp.float32)
    return result


def native(plane, q):
    return pl.ds((plane // 8) * (8 * ROWS) + plane % 8 + 8 * q, 8, stride=ROWS)


def total(x):
    return jnp.sum(x, axis=(0, 1), keepdims=True)


def corner_columns(grads):
    corner = lax.broadcasted_iota(jnp.int32, (8, 128), 0)
    columns = []
    for c in range(3):
        column = jnp.full((8, 128), grads[c, 0], jnp.float32)
        for k in range(1, 8):
            column = jnp.where(corner == k, grads[c, k], column)
        columns.append(column)
    return columns


FORCE = BLOCK
SUMS = BLOCK + 4
LAME_MEAN = 120
SHEAR_MEAN = 121


def prepare_kernel(disp_hbm, stiff_hbm, mask_hbm, disp_ref, halo_ref, disp_v, ends_v, mask_v, sems):
    groups = stiff_hbm.shape[0] // (8 * ROWS)
    ends = [pl.ds((groups - 1) * (8 * ROWS), 8 * ROWS), pl.ds(0, 8 * ROWS)]
    copies = [pltpu.make_async_copy(disp_hbm, disp_v, sems.at[0])]
    for e in range(2):
        copies += [
            pltpu.make_async_copy(stiff_hbm.at[ends[e], :], ends_v.at[e], sems.at[1 + 2 * e]),
            pltpu.make_async_copy(mask_hbm.at[ends[e], :], mask_v.at[e], sems.at[2 + 2 * e]),
        ]
    for copy in copies:
        copy.start()
    for copy in copies:
        copy.wait()
    disp_ref[...] = jnp.broadcast_to(disp_v[...], disp_ref.shape)
    row = 0
    for e, first in ((0, 8 - HALO), (1, 0)):
        for field in (ends_v, mask_v):
            for plane in range(first, first + HALO):
                for q in range(4):
                    x = field[e, native(plane, q), :]
                    halo_ref[row : row + 8, :] = x.astype(jnp.float32)
                    row += 8


def material_kernel(
    grads,
    rve_hbm,
    slot_hbm,
    stiff_v,
    mask_v,
    halo_ref,
    lame_ref,
    shear_ref,
    rows_ref,
    stiff_in,
    mask_in,
    rve_element,
    block_slot,
    sems,
):
    copies = [
        pltpu.make_async_copy(rve_hbm, rve_element, sems.at[0]),
        pltpu.make_async_copy(slot_hbm, block_slot, sems.at[1]),
    ]
    for copy in copies:
        copy.start()
    planes = stiff_v.shape[0] // ROWS
    half = planes // 2
    depth = half + 2 * HALO
    matrix = lane_matrix(False)

    for h in range(2):
        for at in range(depth):
            plane = at - HALO + h * half
            for q in range(4):
                if 0 <= plane < planes:
                    stiff = stiff_v[native(plane, q), :]
                    mask = mask_v[native(plane, q), :].astype(jnp.float32)
                else:
                    side, far = (0, plane + HALO) if plane < 0 else (1, plane - planes)
                    base = (side * 2 * HALO + far) * ROWS + 8 * q
                    stiff = halo_ref[base : base + 8, :]
                    mask = halo_ref[base + HALO * ROWS : base + HALO * ROWS + 8, :]
                place = (at, pl.ds(8 * q, 8), pl.ds(128 * h, 128))
                stiff_in[place] = stiff
                mask_in[place] = mask

    acc_l = acc_m = jnp.zeros((8, 128), jnp.float32)
    for first in range(0, depth, 2):
        count = min(2, depth - first)
        shape = (count * ROWS, WIDE)
        stiff = permute_lanes(stiff_in[first : first + count].reshape(shape), matrix, 2)
        mask = permute_lanes(mask_in[first : first + count].reshape(shape), matrix, 1)
        lame = lame_base * stiff
        shear = jnp.where(mask == 1.0, (shear_base * yield_ratio) * stiff, shear_base * stiff)
        lame_ref[first : first + count] = lame.reshape(count, ROWS, WIDE)
        shear_ref[first : first + count] = shear.reshape(count, ROWS, WIDE)
        for u in range(count):
            if HALO <= first + u < HALO + half:
                for jj in range(8):
                    acc_l = acc_l + load(lame_ref, first + u, jj)
                    acc_m = acc_m + load(shear_ref, first + u, jj)
    for copy in copies:
        copy.wait()
    elem = rve_element[lax.axis_index("macro")]

    scale = 1.0 / float(EDGE * EDGE * EDGE)
    lame, shear = total(acc_l) * scale, total(acc_m) * scale
    mine = corner_columns(grads)
    corner = lax.broadcasted_iota(jnp.int32, (8, 128), 0)
    lane = lax.broadcasted_iota(jnp.int32, (8, 128), 1)
    slot_of = jnp.zeros((8, 128), jnp.int32)
    for s in range(1, NEIGHBOUR_SLOTS + 1):
        slot_of = slot_of + jnp.where(lane >= 9 * s, 1, 0)
    inner = lane - 9 * slot_of
    a_of = jnp.where(inner >= 3, 1, 0) + jnp.where(inner >= 6, 1, 0)
    b_of = inner - 3 * a_of

    def by(which, x, y, z):
        return jnp.where(which == 0, x, jnp.where(which == 1, y, z))

    lame_a = lame * by(a_of, *mine)
    shear_b = shear * by(b_of, *mine)
    diagonal = jnp.where(a_of == b_of, shear, 0.0)
    rows = jnp.zeros((8, 128), jnp.float32)
    for l in range(8):
        other = [grads[c, l] for c in range(3)]
        dots = mine[0] * other[0] + mine[1] * other[1] + mine[2] * other[2]
        block = lame_a * by(b_of, *other) + shear_b * by(a_of, *other) + diagonal * dots
        slot = jnp.full((8, 128), block_slot[elem, 0, l], jnp.int32)
        for k in range(1, 8):
            slot = jnp.where(corner == k, block_slot[elem, k, l], slot)
        rows = rows + jnp.where(slot_of == slot, block, 0.0)
    rows = jnp.where(lane == LAME_MEAN, lame, rows)
    rows = jnp.where(lane == SHEAR_MEAN, shear, rows)
    rows_ref[...] = rows


def sweep_kernel(
    grads,
    rve_element,
    connectivity,
    gathered,
    lame_ref,
    shear_ref,
    rows_ref,
    w30_ref,
    w31_ref,
    w32_ref,
    strain_ref,
    strain_out,
    packet_ref,
    w10_v,
    w11_v,
    w12_v,
    w20_v,
    w21_v,
    w22_v,
    carry2_v,
    carry3_v,
):
    half = lame_ref.shape[0] - 2 * HALO
    elem = rve_element[lax.axis_index("macro")]
    nodes = [connectivity[elem, k] for k in range(8)]
    moves = [[gathered[n, a] for n in nodes] for a in range(3)]

    def dot(c, a):
        result = grads[c, 0] * moves[a][0]
        for k in range(1, 8):
            result = result + grads[c, k] * moves[a][k]
        return result

    strain = [
        dot(0, 0),
        dot(1, 1),
        dot(2, 2),
        dot(2, 1) + dot(1, 2),
        dot(2, 0) + dot(0, 2),
        dot(1, 0) + dot(0, 1),
    ]
    for c in range(6):
        strain_ref[0, c] = strain[c]
        strain_out[8 * c : 8 * c + 8, :] = jnp.full((8, 128), strain[c], jnp.float32)
    w1_v = [w10_v, w11_v, w12_v]
    w2_v = [w20_v, w21_v, w22_v]
    w3_v = [w30_ref, w31_ref, w32_ref]

    scale1 = gain1 * gain2 * precond / centre
    strain1 = [scale1 * e for e in strain]
    trace1 = strain1[0] + strain1[1] + strain1[2]
    twice1 = [2.0 * strain1[c] for c in range(3)]
    strain2 = [gain1 * gain2 * e for e in strain]
    ratio1 = (1.0 + keep1) / gain1
    strain3 = [gain2 * e for e in strain]
    ratio2 = (1.0 + keep2) / gain2
    ratio3 = keep2 / (gain1 * gain2)

    def sweep1(at):
        for jj in range(8):
            l0, l1, l2 = differences(lame_ref, at, jj)
            m0, m1, m2 = differences(shear_ref, at, jj)
            w1_v[0][spot(at, jj)] = (
                trace1 * l0 + twice1[0] * m0 + (strain1[5] * m1 + strain1[4] * m2)
            )
            w1_v[1][spot(at, jj)] = (
                trace1 * l1 + twice1[1] * m1 + (strain1[5] * m0 + strain1[3] * m2)
            )
            w1_v[2][spot(at, jj)] = (
                trace1 * l2 + twice1[2] * m2 + (strain1[4] * m0 + strain1[3] * m1)
            )

    def sweep2(at):
        registers = plane_stress(w1_v, at, lame_ref, shear_ref, at, strain2)
        for jj, w, r in residual_plane(registers, carry2_v):
            for c in range(3):
                w2_v[c][spot(at, jj)] = ratio1 * w[c] + r[c]

    def sweep3(at, place):
        registers = plane_stress(w2_v, at, lame_ref, shear_ref, at, strain3)
        for jj, w, r in residual_plane(registers, carry3_v):
            for c in range(3):
                old = load(w1_v[c], at, jj)
                w3_v[c][spot(place, jj)] = (ratio2 * w[c] - ratio3 * old) + r[c]

    def by_parts(at, acc):
        bulk, a0, a1, a2, a3, a4, a5 = acc
        for jj in range(8):
            w0, w1, w2 = load3(w3_v, at - HALO, jj)
            l0, l1, l2 = differences(lame_ref, at, jj)
            m0, m1, m2 = differences(shear_ref, at, jj)
            bulk = bulk + (l0 * w0 + l1 * w1 + l2 * w2)
            a0 = a0 + m0 * w0
            a1 = a1 + m1 * w1
            a2 = a2 + m2 * w2
            a3 = a3 + (m2 * w1 + m1 * w2)
            a4 = a4 + (m2 * w0 + m0 * w2)
            a5 = a5 + (m1 * w0 + m0 * w1)
        return bulk, a0, a1, a2, a3, a4, a5

    def first_loop(t, _):
        sweep1(t + 1)
        return 0

    lax.fori_loop(0, half + 5, first_loop, 0)

    def second_loop(t, _):
        at = jnp.maximum(t - 1, 0)
        sweep3(at, jnp.where(at < HALO, half, at - HALO))
        sweep2(t + 1)
        return 0

    lax.fori_loop(0, half + 5, second_loop, 0)

    zero = jnp.zeros((8, 128), jnp.float32)
    acc = lax.fori_loop(0, half, lambda t, acc: by_parts(t + HALO, acc), (zero,) * 7)
    scale = 1.0 / float(EDGE * EDGE * EDGE)
    bulk, *parts = [total(x) * scale for x in acc]
    rows = rows_ref[...]
    lame = rows[:1, LAME_MEAN : LAME_MEAN + 1]
    shear = rows[:1, SHEAR_MEAN : SHEAR_MEAN + 1]
    bulk = lame * (strain[0] + strain[1] + strain[2]) - bulk
    means = [bulk + 2.0 * (shear * strain[c] - parts[c]) for c in range(3)]
    means += [shear * strain[c] - parts[c] for c in range(3, 6)]

    xx, yy, zz, yz, xz, xy = means
    g0, g1, g2 = corner_columns(grads)
    lane = lax.broadcasted_iota(jnp.int32, (8, 128), 1)
    rows = jnp.where(lane == FORCE, xx * g0 + xy * g1 + xz * g2, rows)
    rows = jnp.where(lane == FORCE + 1, xy * g0 + yy * g1 + yz * g2, rows)
    rows = jnp.where(lane == FORCE + 2, xz * g0 + yz * g1 + zz * g2, rows)
    sums = jnp.zeros((8, 128), jnp.float32)
    for c in range(6):
        sums = jnp.where(lane == SUMS + c, means[c], sums)
    rows = jnp.where(lane >= SUMS, sums, rows)
    for g in range(packet_ref.shape[0] // 8):
        packet_ref[8 * g : 8 * g + 8, :] = sums
    count = lax.axis_size("macro")
    for v in range(lax.axis_size("vox")):
        for k in range(8):
            packet_ref[pl.ds(v * count + nodes[k], 1), :] = rows[k : k + 1]


def stress_kernel(
    strain_in,
    lame_ref,
    shear_ref,
    w30_ref,
    w31_ref,
    w32_ref,
    stress_ref,
    out_v,
    work_v,
    turn_v,
    sem,
):
    half = lame_ref.shape[0] - 2 * HALO
    w3_v = [w30_ref, w31_ref, w32_ref]
    strain = [strain_in[8 * c : 8 * c + 8, :] for c in range(6)]
    matrix = lane_matrix(True)
    copies = []
    for first in range(0, half, GROUP):
        slot = (first // GROUP) % 2
        for u in range(GROUP):
            at = first + u
            for jj, _, stress in plane_stress(w3_v, at, lame_ref, shear_ref, at + HALO, strain):
                for c in range(6):
                    work_v[(slot, c, u, *spot(0, jj)[1:])] = stress[c]
        for c in range(6):
            y = permute_lanes(work_v[slot, c].reshape(GROUP * ROWS, WIDE), matrix, 2)
            for u in range(GROUP):
                for q in range(4):
                    row = (u * 4 + q) * 8
                    for h in range(2):
                        s = (first + u + h * half) % 8
                        turn_v[h, c, pl.ds(s * TURN_S + q * 8 * TURN_R, 8, stride=TURN_R), :] = y[
                            row : row + 8, 128 * h : 128 * h + 128
                        ]
        done = []
        if half % 8 == 0 and (first + GROUP) % 8 == 0:
            done = [((first + GROUP) // 8 - 1 + h * (half // 8), h) for h in range(2)]
        elif half % 8 and first + GROUP == half:
            done = [(0, None)]
        for group, h in done:
            for c in range(6):
                for q in range(4):
                    for r in range(8):
                        row = group * (8 * ROWS) + (4 * r + q) * 8
                        start = (q * 8 + r) * TURN_R
                        if h is None:
                            low = turn_v[0, c, pl.ds(start, 8, stride=TURN_S), :]
                            high = turn_v[1, c, pl.ds(start, 8, stride=TURN_S), :]
                            sub = lax.broadcasted_iota(jnp.int32, (8, 128), 0)
                            out_v[c, row : row + 8, :] = jnp.where(sub < half, low, high)
                        else:
                            out_v[c, row : row + 8, :] = turn_v[
                                h, c, pl.ds(start, 8, stride=TURN_S), :
                            ]
            span = pl.ds(group * (8 * ROWS), 8 * ROWS)
            copy = pltpu.make_async_copy(
                out_v.at[:, span, :], stress_ref.at[:, span, :], sem.at[len(copies)]
            )
            copy.start()
            copies.append(copy)
    for copy in copies:
        copy.wait()


TURN_R = 3
TURN_S = TURN_R * ROWS + 1
GROUP = 4


def node_kernel(packets_ref, hom_ref, force_ref, tangent_ref):
    packets = packets_ref[...]
    count = lax.axis_size("macro")
    place = lax.broadcasted_iota(jnp.int32, packets.shape, 0)
    point = lax.axis_index("macro")
    own = place == point
    for v in range(1, lax.axis_size("vox")):
        own = own | (place == v * count + point)
    row = jnp.sum(packets, axis=0, keepdims=True)
    means = jnp.sum(jnp.where(own, packets, 0.0), axis=0, keepdims=True)
    tangent_ref[...] = row[:, :BLOCK]
    force_ref[...] = row[:, FORCE : FORCE + 3]
    hom_ref[...] = means[:, SUMS : SUMS + 6]


def on_device(
    nodal_disp,
    weighted_shape_gradients,
    rve_element,
    connectivity,
    block_slot,
    stiffness,
    yielded_mask,
):
    rve_count, planes, plane_size = stiffness.shape
    macro_size = lax.axis_size("macro")
    vox_size = lax.axis_size("vox")
    everywhere = macro_size * vox_size
    assert rve_count == 1 and nodal_disp.shape[0] == 1
    assert planes % 8 == 0 and plane_size == EDGE * EDGE

    def flat(field):
        parted = field.reshape(planes // 8, 8, ROWS, 128)
        return parted.transpose(0, 2, 1, 3).reshape(planes * ROWS, 128)

    smem = pl.BlockSpec(memory_space=pltpu.SMEM)
    vmem = pl.BlockSpec(memory_space=pltpu.VMEM)
    hbm = pl.BlockSpec(memory_space=pltpu.HBM)
    anywhere = pl.BlockSpec(memory_space=pl.ANY)
    mib = 1024 * 1024
    f32 = jnp.float32
    half = planes // 2
    depth = half + 2 * HALO
    packed = 4 * HALO * ROWS
    layer = jax.ShapeDtypeStruct((depth, ROWS, WIDE), f32)
    field = pltpu.VMEM((depth, ROWS, WIDE), f32)
    carry = pltpu.VMEM((3, ROWS, WIDE), f32)
    beyond = pltpu.VMEM((depth + 1, ROWS, WIDE), f32)
    last_layer = jax.ShapeDtypeStruct((half + 1, ROWS, WIDE), f32)

    def cost(flops, size):
        return pl.CostEstimate(
            flops=flops * planes * plane_size,
            bytes_accessed=size * planes * plane_size,
            transcendentals=0,
        )

    disp, rims = pl.pallas_call(
        prepare_kernel,
        out_shape=(
            jax.ShapeDtypeStruct((macro_size, 3), f32),
            jax.ShapeDtypeStruct((packed, 128), f32),
        ),
        in_specs=[hbm] * 3,
        out_specs=(vmem,) * 2,
        scratch_shapes=[
            pltpu.VMEM((1, 3), f32),
            pltpu.VMEM((2, 8 * ROWS, 128), f32),
            pltpu.VMEM((2, 8 * ROWS, 128), jnp.int32),
            pltpu.SemaphoreType.DMA((5,)),
        ],
        compiler_params=pltpu.CompilerParams(vmem_limit_bytes=56 * mib),
        cost_estimate=cost(10**4, 1),
        name="prepare",
    )(nodal_disp, flat(stiffness), flat(yielded_mask))

    if vox_size == 2:
        halo = lax.ppermute(rims, "vox", [(0, 1), (1, 0)])
    else:
        forward = [(i, (i + 1) % vox_size) for i in range(vox_size)]
        backward = [(t, s) for s, t in forward]
        halo = jnp.concatenate(
            [
                lax.ppermute(rims[: packed // 2], "vox", forward),
                lax.ppermute(rims[packed // 2 :], "vox", backward),
            ],
            axis=0,
        )
    gathered = lax.all_to_all(disp, "macro", split_axis=0, concat_axis=0, tiled=True)

    grads = weighted_shape_gradients[0]
    lame, shear, rows = pl.pallas_call(
        material_kernel,
        out_shape=(layer, layer, jax.ShapeDtypeStruct((8, 128), f32)),
        in_specs=[smem, hbm, hbm, vmem, vmem, vmem],
        out_specs=(vmem,) * 3,
        scratch_shapes=[
            field,
            field,
            pltpu.SMEM(rve_element.shape, jnp.int32),
            pltpu.SMEM(block_slot.shape, jnp.int32),
            pltpu.SemaphoreType.DMA((2,)),
        ],
        compiler_params=pltpu.CompilerParams(vmem_limit_bytes=8 * mib),
        cost_estimate=cost(10**4, 1),
        name="material",
    )(grads, rve_element, block_slot, flat(stiffness), flat(yielded_mask), halo)

    *w3, strain, strain_rows, packet = pl.pallas_call(
        sweep_kernel,
        out_shape=(
            last_layer,
            last_layer,
            last_layer,
            jax.ShapeDtypeStruct((1, 6), f32),
            jax.ShapeDtypeStruct((48, 128), f32),
            jax.ShapeDtypeStruct((everywhere, 128), f32),
        ),
        in_specs=[smem] * 4 + [vmem] * 3,
        out_specs=(vmem, vmem, vmem, smem, vmem, vmem),
        scratch_shapes=[beyond] * 3 + [field] * 3 + [carry] * 2,
        compiler_params=pltpu.CompilerParams(vmem_limit_bytes=12 * mib),
        cost_estimate=cost(2 * 10**4, 1),
        name="sweeps",
    )(grads, rve_element, connectivity, gathered, lame, shear, rows)

    packets = lax.all_to_all(
        packet, ("vox", "macro"), split_axis=0, concat_axis=0, tiled=True
    )

    stress = pl.pallas_call(
        stress_kernel,
        out_shape=jax.ShapeDtypeStruct((6, planes * ROWS, 128), f32),
        in_specs=[vmem] * 6,
        out_specs=hbm,
        scratch_shapes=[
            pltpu.VMEM((6, planes * ROWS, 128), f32),
            pltpu.VMEM((2, 6, GROUP, ROWS, WIDE), f32),
            pltpu.VMEM((2, 6, 8 * TURN_S, 128), f32),
            pltpu.SemaphoreType.DMA((planes // 8,)),
        ],
        compiler_params=pltpu.CompilerParams(vmem_limit_bytes=16 * mib),
        cost_estimate=cost(10**4, 1),
        name="stress",
    )(strain_rows, lame, shear, *w3)
    voxel_stress = (
        stress.reshape(6, planes // 8, ROWS, 8, 128)
        .transpose(0, 1, 3, 2, 4)
        .reshape(1, 6, planes, plane_size)
    )

    homogenized, internal_node_force, tangent = pl.pallas_call(
        node_kernel,
        out_shape=(
            jax.ShapeDtypeStruct((1, 6), f32),
            jax.ShapeDtypeStruct((1, 3), f32),
            jax.ShapeDtypeStruct((1, BLOCK), f32),
        ),
        in_specs=[vmem],
        out_specs=(vmem, vmem, vmem),
        compiler_params=pltpu.CompilerParams(vmem_limit_bytes=4 * mib),
        name="nodes",
    )(packets)
    return (voxel_stress, homogenized, strain, internal_node_force, tangent)


def solution(mesh):
    in_specs = (
        P("macro", None),
        P("macro", None, None),
        P(),
        P(),
        P(),
        P("macro", "vox", None),
        P("macro", "vox", None),
    )
    out_specs = (
        P("macro", None, "vox", None),
        P("macro", None),
        P("macro", None),
        P("macro", None),
        P("macro", None),
    )
    return jax.shard_map(
        on_device, mesh=mesh, in_specs=in_specs, out_specs=out_specs, check_vma=False
    )
```

```python
import jax
import jax.numpy as jnp
from jax import lax
from jax.experimental import pallas as pl
from jax.experimental.pallas import tpu as pltpu
from jax.sharding import PartitionSpec as P

EDGE = 64
SWEEPS = 3
NEIGHBOUR_SLOTS = 12
BLOCK = NEIGHBOUR_SLOTS * 9

lame_base = 1.5
shear_base = 1.0
yield_ratio = 0.2
precond = 1.0 / 42.0
lower_bound = 0.05
upper_bound = 2.0

ROWS = EDGE * EDGE // 128
WIDE = 256
HALO = 3


def chebyshev_terms(count):
    centre = 0.5 * (upper_bound + lower_bound)
    half_width = 0.5 * (upper_bound - lower_bound)
    ratio_bound = centre / half_width
    rho_prev = 1.0 / ratio_bound
    weights = []
    for number in range(count):
        rho_next = 1.0 / (2.0 * ratio_bound - rho_prev)
        weights.append((rho_next * rho_prev, 2.0 * rho_next / half_width))
        rho_prev = rho_next
    return (centre, weights)


def sweep_polynomial():
    centre, weights = chebyshev_terms(SWEEPS - 1)
    direction = [1.0 / centre]
    result = list(direction)
    for keep, push in weights:
        applied = [1.0] + result
        direction = [
            keep * (direction[k] if k < len(direction) else 0.0) + push * applied[k]
            for k in range(len(applied))
        ]
        result = [(result[k] if k < len(result) else 0.0) + direction[k] for k in range(len(applied))]
    return result


poly0, poly1, poly2 = sweep_polynomial()


def spot(at, jj):
    half = (jj & 1) * 128
    return at, pl.ds(8 * (jj // 2), 8), pl.ds(half, 128)


def load(ref, at, jj):
    return ref[spot(at, jj)]


def load3(refs, at, jj):
    return [load(ref, at, jj) for ref in refs]


def prev_row(ref, at, jj):
    if jj > 0:
        return load(ref, at, jj - 1)
    return pltpu.roll(load(ref, at, 7), 1, 0)


def next_lane(x):
    return pltpu.roll(x, 126, 1)


def prev_lane(x):
    return pltpu.roll(x, 2, 1)


def differences(ref, at, jj):
    here = load(ref, at, jj)
    return (
        here - load(ref, at - 1, jj),
        here - prev_row(ref, at, jj),
        here - prev_lane(here),
    )


def plane_stress(w_refs, at, lame_ref, shear_ref, lame_at, strain):
    ahead = first = load3(w_refs, at, 0)
    for jj in range(8):
        w0, w1, w2 = w = ahead
        ahead = load3(w_refs, at, jj + 1) if jj < 7 else [pltpu.roll(x, 7, 0) for x in first]
        row0, row1, row2 = ahead
        n0, n1, n2 = load3(w_refs, at + 1, jj)
        lane0, lane1, lane2 = [next_lane(x) for x in w]
        lame = load(lame_ref, lame_at, jj)
        shear = load(shear_ref, lame_at, jj)
        e0 = n0 - w0
        e1 = row1 - w1
        e2 = lane2 - w2
        g3 = (lane1 + row2) - (w1 + w2)
        g4 = (lane0 + n2) - (w0 + w2)
        g5 = (row0 + n1) - (w0 + w1)
        if strain is not None:
            e0, e1, e2 = e0 + strain[0], e1 + strain[1], e2 + strain[2]
            g3, g4, g5 = g3 + strain[3], g4 + strain[4], g5 + strain[5]
        bulk = lame * (e0 + e1 + e2)
        twice = shear + shear
        yield jj, w, (
            bulk + twice * e0,
            bulk + twice * e1,
            bulk + twice * e2,
            shear * g3,
            shear * g4,
            shear * g5,
        )


def residual_plane(registers, carry_v):
    begin = None
    row_xy = row_yy = row_yz = None
    for jj, w, stress in registers:
        xx, yy, zz, yz, xz, xy = stress
        pxx, pxz, pxy = [load(carry_v, c, jj) for c in range(3)]
        for c, x in enumerate((xx, xz, xy)):
            carry_v[spot(c, jj)] = x
        r = [
            (xx - pxx) + (xz - prev_lane(xz)) + xy,
            (xy - pxy) + (yz - prev_lane(yz)) + yy,
            (xz - pxz) + (zz - prev_lane(zz)) + yz,
        ]
        if jj == 0:
            begin = w, r
        else:
            yield jj, w, [r[0] - row_xy, r[1] - row_yy, r[2] - row_yz]
        row_xy, row_yy, row_yz = xy, yy, yz
    rows = [pltpu.roll(x, 1, 0) for x in (row_xy, row_yy, row_yz)]
    yield 0, begin[0], [x - y for x, y in zip(begin[1], rows)]


def target_lane(m):
    return ((m >> 6) & 1) * 128 + (m & 63) * 2 + (m >> 7)


def lane_matrix(inverse):
    row = lax.broadcasted_iota(jnp.int32, (WIDE, WIDE), 0)
    column = lax.broadcasted_iota(jnp.int32, (WIDE, WIDE), 1)
    hit = (target_lane(column) == row) if inverse else (target_lane(row) == column)
    return jnp.where(hit, 1.0, 0.0).astype(jnp.bfloat16)


def permute_lanes(x, matrix, terms):
    result = None
    for t in range(terms):
        part = x.astype(jnp.bfloat16)
        moved = jnp.dot(part, matrix, preferred_element_type=jnp.float32)
        result = moved if result is None else result + moved
        if t + 1 < terms:
            x = x - part.astype(jnp.float32)
    return result


def native(plane, q):
    return pl.ds((plane // 8) * (8 * ROWS) + plane % 8 + 8 * q, 8, stride=ROWS)


def total(x):
    return jnp.sum(x, axis=(0, 1), keepdims=True)


def corner_columns(grads):
    corner = lax.broadcasted_iota(jnp.int32, (8, 128), 0)
    columns = []
    for c in range(3):
        column = jnp.full((8, 128), grads[c, 0], jnp.float32)
        for k in range(1, 8):
            column = jnp.where(corner == k, grads[c, k], column)
        columns.append(column)
    return columns


FORCE = BLOCK
SUMS = BLOCK + 4
LAME_MEAN = 120
SHEAR_MEAN = 121


def prepare_kernel(disp_hbm, stiff_hbm, mask_hbm, disp_ref, halo_ref, disp_v, ends_v, mask_v, sems):
    groups = stiff_hbm.shape[0] // (8 * ROWS)
    ends = [pl.ds((groups - 1) * (8 * ROWS), 8 * ROWS), pl.ds(0, 8 * ROWS)]
    copies = [pltpu.make_async_copy(disp_hbm, disp_v, sems.at[0])]
    for e in range(2):
        copies += [
            pltpu.make_async_copy(stiff_hbm.at[ends[e], :], ends_v.at[e], sems.at[1 + 2 * e]),
            pltpu.make_async_copy(mask_hbm.at[ends[e], :], mask_v.at[e], sems.at[2 + 2 * e]),
        ]
    for copy in copies:
        copy.start()
    for copy in copies:
        copy.wait()
    disp_ref[...] = jnp.broadcast_to(disp_v[...], disp_ref.shape)
    row = 0
    for e, first in ((0, 8 - HALO), (1, 0)):
        for field in (ends_v, mask_v):
            for plane in range(first, first + HALO):
                for q in range(4):
                    x = field[e, native(plane, q), :]
                    halo_ref[row : row + 8, :] = x.astype(jnp.float32)
                    row += 8


def material_kernel(
    grads,
    rve_hbm,
    slot_hbm,
    stiff_v,
    mask_v,
    halo_ref,
    lame_ref,
    shear_ref,
    rows_ref,
    stiff_in,
    mask_in,
    rve_element,
    block_slot,
    sems,
):
    copies = [
        pltpu.make_async_copy(rve_hbm, rve_element, sems.at[0]),
        pltpu.make_async_copy(slot_hbm, block_slot, sems.at[1]),
    ]
    for copy in copies:
        copy.start()
    planes = stiff_v.shape[0] // ROWS
    half = planes // 2
    depth = half + 2 * HALO
    matrix = lane_matrix(False)

    for h in range(2):
        for at in range(depth):
            plane = at - HALO + h * half
            for q in range(4):
                if 0 <= plane < planes:
                    stiff = stiff_v[native(plane, q), :]
                    mask = mask_v[native(plane, q), :].astype(jnp.float32)
                else:
                    side, far = (0, plane + HALO) if plane < 0 else (1, plane - planes)
                    base = (side * 2 * HALO + far) * ROWS + 8 * q
                    stiff = halo_ref[base : base + 8, :]
                    mask = halo_ref[base + HALO * ROWS : base + HALO * ROWS + 8, :]
                place = (at, pl.ds(8 * q, 8), pl.ds(128 * h, 128))
                stiff_in[place] = stiff
                mask_in[place] = mask

    acc_l = acc_m = jnp.zeros((8, 128), jnp.float32)
    for first in range(0, depth, 2):
        count = min(2, depth - first)
        shape = (count * ROWS, WIDE)
        stiff = permute_lanes(stiff_in[first : first + count].reshape(shape), matrix, 2)
        mask = permute_lanes(mask_in[first : first + count].reshape(shape), matrix, 1)
        lame = lame_base * stiff
        shear = jnp.where(mask == 1.0, (shear_base * yield_ratio) * stiff, shear_base * stiff)
        lame_ref[first : first + count] = lame.reshape(count, ROWS, WIDE)
        shear_ref[first : first + count] = shear.reshape(count, ROWS, WIDE)
        for u in range(count):
            if HALO <= first + u < HALO + half:
                for jj in range(8):
                    acc_l = acc_l + load(lame_ref, first + u, jj)
                    acc_m = acc_m + load(shear_ref, first + u, jj)
    for copy in copies:
        copy.wait()
    elem = rve_element[lax.axis_index("macro")]

    scale = 1.0 / float(EDGE * EDGE * EDGE)
    lame, shear = total(acc_l) * scale, total(acc_m) * scale
    mine = corner_columns(grads)
    corner = lax.broadcasted_iota(jnp.int32, (8, 128), 0)
    lane = lax.broadcasted_iota(jnp.int32, (8, 128), 1)
    slot_of = jnp.zeros((8, 128), jnp.int32)
    for s in range(1, NEIGHBOUR_SLOTS + 1):
        slot_of = slot_of + jnp.where(lane >= 9 * s, 1, 0)
    inner = lane - 9 * slot_of
    a_of = jnp.where(inner >= 3, 1, 0) + jnp.where(inner >= 6, 1, 0)
    b_of = inner - 3 * a_of

    def by(which, x, y, z):
        return jnp.where(which == 0, x, jnp.where(which == 1, y, z))

    lame_a = lame * by(a_of, *mine)
    shear_b = shear * by(b_of, *mine)
    diagonal = jnp.where(a_of == b_of, shear, 0.0)
    rows = jnp.zeros((8, 128), jnp.float32)
    for l in range(8):
        other = [grads[c, l] for c in range(3)]
        dots = mine[0] * other[0] + mine[1] * other[1] + mine[2] * other[2]
        block = lame_a * by(b_of, *other) + shear_b * by(a_of, *other) + diagonal * dots
        slot = jnp.full((8, 128), block_slot[elem, 0, l], jnp.int32)
        for k in range(1, 8):
            slot = jnp.where(corner == k, block_slot[elem, k, l], slot)
        rows = rows + jnp.where(slot_of == slot, block, 0.0)
    rows = jnp.where(lane == LAME_MEAN, lame, rows)
    rows = jnp.where(lane == SHEAR_MEAN, shear, rows)
    rows_ref[...] = rows


def sweep_kernel(
    grads,
    rve_element,
    connectivity,
    gathered,
    lame_ref,
    shear_ref,
    rows_ref,
    w30_ref,
    w31_ref,
    w32_ref,
    strain_ref,
    strain_out,
    packet_ref,
    w10_v,
    w11_v,
    w12_v,
    w20_v,
    w21_v,
    w22_v,
    carry2_v,
    carry3_v,
):
    half = lame_ref.shape[0] - 2 * HALO
    elem = rve_element[lax.axis_index("macro")]
    nodes = [connectivity[elem, k] for k in range(8)]
    moves = [[gathered[n, a] for n in nodes] for a in range(3)]

    def dot(c, a):
        result = grads[c, 0] * moves[a][0]
        for k in range(1, 8):
            result = result + grads[c, k] * moves[a][k]
        return result

    strain = [
        dot(0, 0),
        dot(1, 1),
        dot(2, 2),
        dot(2, 1) + dot(1, 2),
        dot(2, 0) + dot(0, 2),
        dot(1, 0) + dot(0, 1),
    ]
    for c in range(6):
        strain_ref[0, c] = strain[c]
        strain_out[8 * c : 8 * c + 8, :] = jnp.full((8, 128), strain[c], jnp.float32)
    w1_v = [w10_v, w11_v, w12_v]
    w2_v = [w20_v, w21_v, w22_v]
    w3_v = [w30_ref, w31_ref, w32_ref]

    strain1 = [poly2 * precond**3 * e for e in strain]
    trace1 = strain1[0] + strain1[1] + strain1[2]
    twice1 = [2.0 * strain1[c] for c in range(3)]
    ratio1 = poly1 / (poly2 * precond)
    ratio0 = poly0 / (poly2 * precond**2)

    def sweep1(at):
        for jj in range(8):
            l0, l1, l2 = differences(lame_ref, at, jj)
            m0, m1, m2 = differences(shear_ref, at, jj)
            w1_v[0][spot(at, jj)] = (
                trace1 * l0 + twice1[0] * m0 + (strain1[5] * m1 + strain1[4] * m2)
            )
            w1_v[1][spot(at, jj)] = (
                trace1 * l1 + twice1[1] * m1 + (strain1[5] * m0 + strain1[3] * m2)
            )
            w1_v[2][spot(at, jj)] = (
                trace1 * l2 + twice1[2] * m2 + (strain1[4] * m0 + strain1[3] * m1)
            )

    def sweep2(at):
        registers = plane_stress(w1_v, at, lame_ref, shear_ref, at, None)
        for jj, w, r in residual_plane(registers, carry2_v):
            for c in range(3):
                w2_v[c][spot(at, jj)] = ratio1 * w[c] + r[c]

    def sweep3(at, place):
        registers = plane_stress(w2_v, at, lame_ref, shear_ref, at, None)
        for jj, _, r in residual_plane(registers, carry3_v):
            for c in range(3):
                w3_v[c][spot(place, jj)] = ratio0 * load(w1_v[c], at, jj) + r[c]

    def by_parts(at):
        bulk, a0, a1, a2, a3, a4, a5 = (jnp.zeros((8, 128), jnp.float32),) * 7
        for jj in range(8):
            w0, w1, w2 = load3(w3_v, at - HALO, jj)
            l0, l1, l2 = differences(lame_ref, at, jj)
            m0, m1, m2 = differences(shear_ref, at, jj)
            bulk = bulk + (l0 * w0 + l1 * w1 + l2 * w2)
            a0 = a0 + m0 * w0
            a1 = a1 + m1 * w1
            a2 = a2 + m2 * w2
            a3 = a3 + (m2 * w1 + m1 * w2)
            a4 = a4 + (m2 * w0 + m0 * w2)
            a5 = a5 + (m1 * w0 + m0 * w1)
        return bulk, a0, a1, a2, a3, a4, a5

    def step(t, acc):
        at = jnp.maximum(t - 4, HALO)
        sums = by_parts(at)
        acc = [x + jnp.where(t - 4 >= HALO, y, 0.0) for x, y in zip(acc, sums)]
        at = jnp.maximum(t - 3, 0)
        sweep3(at, jnp.where(at < HALO, half, at - HALO))
        sweep2(jnp.maximum(t - 1, 0))
        sweep1(jnp.minimum(t + 1, half + 5))
        return tuple(acc)

    zero = jnp.zeros((8, 128), jnp.float32)
    acc = lax.fori_loop(0, half + 7, step, (zero,) * 7)
    scale = 1.0 / float(EDGE * EDGE * EDGE)
    bulk, *parts = [total(x) * scale for x in acc]
    rows = rows_ref[...]
    lame = rows[:1, LAME_MEAN : LAME_MEAN + 1]
    shear = rows[:1, SHEAR_MEAN : SHEAR_MEAN + 1]
    bulk = lame * (strain[0] + strain[1] + strain[2]) - bulk
    means = [bulk + 2.0 * (shear * strain[c] - parts[c]) for c in range(3)]
    means += [shear * strain[c] - parts[c] for c in range(3, 6)]

    xx, yy, zz, yz, xz, xy = means
    g0, g1, g2 = corner_columns(grads)
    lane = lax.broadcasted_iota(jnp.int32, (8, 128), 1)
    rows = jnp.where(lane == FORCE, xx * g0 + xy * g1 + xz * g2, rows)
    rows = jnp.where(lane == FORCE + 1, xy * g0 + yy * g1 + yz * g2, rows)
    rows = jnp.where(lane == FORCE + 2, xz * g0 + yz * g1 + zz * g2, rows)
    sums = jnp.zeros((8, 128), jnp.float32)
    for c in range(6):
        sums = jnp.where(lane == SUMS + c, means[c], sums)
    rows = jnp.where(lane >= SUMS, sums, rows)
    for g in range(packet_ref.shape[0] // 8):
        packet_ref[8 * g : 8 * g + 8, :] = sums
    count = lax.axis_size("macro")
    for v in range(lax.axis_size("vox")):
        for k in range(8):
            packet_ref[pl.ds(v * count + nodes[k], 1), :] = rows[k : k + 1]


def stress_kernel(
    strain_in,
    lame_ref,
    shear_ref,
    w30_ref,
    w31_ref,
    w32_ref,
    stress_ref,
    out_v,
    work_v,
    turn_v,
    sem,
):
    half = lame_ref.shape[0] - 2 * HALO
    w3_v = [w30_ref, w31_ref, w32_ref]
    strain = [strain_in[8 * c : 8 * c + 8, :] for c in range(6)]
    matrix = lane_matrix(True)
    copies = []
    for first in range(0, half, GROUP):
        slot = (first // GROUP) % 2
        for u in range(GROUP):
            at = first + u
            for jj, _, stress in plane_stress(w3_v, at, lame_ref, shear_ref, at + HALO, strain):
                for c in range(6):
                    work_v[(slot, c, u, *spot(0, jj)[1:])] = stress[c]
        for c in range(6):
            y = permute_lanes(work_v[slot, c].reshape(GROUP * ROWS, WIDE), matrix, 2)
            for u in range(GROUP):
                for q in range(4):
                    row = (u * 4 + q) * 8
                    for h in range(2):
                        s = (first + u + h * half) % 8
                        turn_v[h, c, pl.ds(s * TURN_S + q * 8 * TURN_R, 8, stride=TURN_R), :] = y[
                            row : row + 8, 128 * h : 128 * h + 128
                        ]
        done = []
        if half % 8 == 0 and (first + GROUP) % 8 == 0:
            done = [((first + GROUP) // 8 - 1 + h * (half // 8), h) for h in range(2)]
        elif half % 8 and first + GROUP == half:
            done = [(0, None)]
        for group, h in done:
            for c in range(6):
                for q in range(4):
                    for r in range(8):
                        row = group * (8 * ROWS) + (4 * r + q) * 8
                        start = (q * 8 + r) * TURN_R
                        if h is None:
                            low = turn_v[0, c, pl.ds(start, 8, stride=TURN_S), :]
                            high = turn_v[1, c, pl.ds(start, 8, stride=TURN_S), :]
                            sub = lax.broadcasted_iota(jnp.int32, (8, 128), 0)
                            out_v[c, row : row + 8, :] = jnp.where(sub < half, low, high)
                        else:
                            out_v[c, row : row + 8, :] = turn_v[
                                h, c, pl.ds(start, 8, stride=TURN_S), :
                            ]
            span = pl.ds(group * (8 * ROWS), 8 * ROWS)
            copy = pltpu.make_async_copy(
                out_v.at[:, span, :], stress_ref.at[:, span, :], sem.at[len(copies)]
            )
            copy.start()
            copies.append(copy)
    for copy in copies:
        copy.wait()


TURN_R = 3
TURN_S = TURN_R * ROWS + 1
GROUP = 4


def node_kernel(packets_ref, hom_ref, force_ref, tangent_ref):
    packets = packets_ref[...]
    count = lax.axis_size("macro")
    place = lax.broadcasted_iota(jnp.int32, packets.shape, 0)
    point = lax.axis_index("macro")
    own = place == point
    for v in range(1, lax.axis_size("vox")):
        own = own | (place == v * count + point)
    row = jnp.sum(packets, axis=0, keepdims=True)
    means = jnp.sum(jnp.where(own, packets, 0.0), axis=0, keepdims=True)
    tangent_ref[...] = row[:, :BLOCK]
    force_ref[...] = row[:, FORCE : FORCE + 3]
    hom_ref[...] = means[:, SUMS : SUMS + 6]


def on_device(
    nodal_disp,
    weighted_shape_gradients,
    rve_element,
    connectivity,
    block_slot,
    stiffness,
    yielded_mask,
):
    rve_count, planes, plane_size = stiffness.shape
    macro_size = lax.axis_size("macro")
    vox_size = lax.axis_size("vox")
    everywhere = macro_size * vox_size
    assert rve_count == 1 and nodal_disp.shape[0] == 1
    assert planes % 8 == 0 and plane_size == EDGE * EDGE

    def flat(field):
        parted = field.reshape(planes // 8, 8, ROWS, 128)
        return parted.transpose(0, 2, 1, 3).reshape(planes * ROWS, 128)

    smem = pl.BlockSpec(memory_space=pltpu.SMEM)
    vmem = pl.BlockSpec(memory_space=pltpu.VMEM)
    hbm = pl.BlockSpec(memory_space=pltpu.HBM)
    anywhere = pl.BlockSpec(memory_space=pl.ANY)
    mib = 1024 * 1024
    f32 = jnp.float32
    half = planes // 2
    depth = half + 2 * HALO
    packed = 4 * HALO * ROWS
    layer = jax.ShapeDtypeStruct((depth, ROWS, WIDE), f32)
    field = pltpu.VMEM((depth, ROWS, WIDE), f32)
    carry = pltpu.VMEM((3, ROWS, WIDE), f32)
    beyond = pltpu.VMEM((depth + 1, ROWS, WIDE), f32)
    last_layer = jax.ShapeDtypeStruct((half + 1, ROWS, WIDE), f32)

    def cost(flops, size):
        return pl.CostEstimate(
            flops=flops * planes * plane_size,
            bytes_accessed=size * planes * plane_size,
            transcendentals=0,
        )

    disp, rims = pl.pallas_call(
        prepare_kernel,
        out_shape=(
            jax.ShapeDtypeStruct((macro_size, 3), f32),
            jax.ShapeDtypeStruct((packed, 128), f32),
        ),
        in_specs=[hbm] * 3,
        out_specs=(vmem,) * 2,
        scratch_shapes=[
            pltpu.VMEM((1, 3), f32),
            pltpu.VMEM((2, 8 * ROWS, 128), f32),
            pltpu.VMEM((2, 8 * ROWS, 128), jnp.int32),
            pltpu.SemaphoreType.DMA((5,)),
        ],
        compiler_params=pltpu.CompilerParams(vmem_limit_bytes=56 * mib),
        cost_estimate=cost(10**4, 1),
        name="prepare",
    )(nodal_disp, flat(stiffness), flat(yielded_mask))

    if vox_size == 2:
        halo = lax.ppermute(rims, "vox", [(0, 1), (1, 0)])
    else:
        forward = [(i, (i + 1) % vox_size) for i in range(vox_size)]
        backward = [(t, s) for s, t in forward]
        halo = jnp.concatenate(
            [
                lax.ppermute(rims[: packed // 2], "vox", forward),
                lax.ppermute(rims[packed // 2 :], "vox", backward),
            ],
            axis=0,
        )
    gathered = lax.all_to_all(disp, "macro", split_axis=0, concat_axis=0, tiled=True)

    grads = weighted_shape_gradients[0]
    lame, shear, rows = pl.pallas_call(
        material_kernel,
        out_shape=(layer, layer, jax.ShapeDtypeStruct((8, 128), f32)),
        in_specs=[smem, hbm, hbm, vmem, vmem, vmem],
        out_specs=(vmem,) * 3,
        scratch_shapes=[
            field,
            field,
            pltpu.SMEM(rve_element.shape, jnp.int32),
            pltpu.SMEM(block_slot.shape, jnp.int32),
            pltpu.SemaphoreType.DMA((2,)),
        ],
        compiler_params=pltpu.CompilerParams(vmem_limit_bytes=8 * mib),
        cost_estimate=cost(10**4, 1),
        name="material",
    )(grads, rve_element, block_slot, flat(stiffness), flat(yielded_mask), halo)

    *w3, strain, strain_rows, packet = pl.pallas_call(
        sweep_kernel,
        out_shape=(
            last_layer,
            last_layer,
            last_layer,
            jax.ShapeDtypeStruct((1, 6), f32),
            jax.ShapeDtypeStruct((48, 128), f32),
            jax.ShapeDtypeStruct((everywhere, 128), f32),
        ),
        in_specs=[smem] * 4 + [vmem] * 3,
        out_specs=(vmem, vmem, vmem, smem, vmem, vmem),
        scratch_shapes=[beyond] * 3 + [field] * 3 + [carry] * 2,
        compiler_params=pltpu.CompilerParams(vmem_limit_bytes=12 * mib),
        cost_estimate=cost(2 * 10**4, 1),
        name="sweeps",
    )(grads, rve_element, connectivity, gathered, lame, shear, rows)

    packets = lax.all_to_all(
        packet, ("vox", "macro"), split_axis=0, concat_axis=0, tiled=True
    )

    stress = pl.pallas_call(
        stress_kernel,
        out_shape=jax.ShapeDtypeStruct((6, planes * ROWS, 128), f32),
        in_specs=[vmem] * 6,
        out_specs=hbm,
        scratch_shapes=[
            pltpu.VMEM((6, planes * ROWS, 128), f32),
            pltpu.VMEM((2, 6, GROUP, ROWS, WIDE), f32),
            pltpu.VMEM((2, 6, 8 * TURN_S, 128), f32),
            pltpu.SemaphoreType.DMA((planes // 8,)),
        ],
        compiler_params=pltpu.CompilerParams(vmem_limit_bytes=16 * mib),
        cost_estimate=cost(10**4, 1),
        name="stress",
    )(strain_rows, lame, shear, *w3)
    voxel_stress = (
        stress.reshape(6, planes // 8, ROWS, 8, 128)
        .transpose(0, 1, 3, 2, 4)
        .reshape(1, 6, planes, plane_size)
    )

    homogenized, internal_node_force, tangent = pl.pallas_call(
        node_kernel,
        out_shape=(
            jax.ShapeDtypeStruct((1, 6), f32),
            jax.ShapeDtypeStruct((1, 3), f32),
            jax.ShapeDtypeStruct((1, BLOCK), f32),
        ),
        in_specs=[vmem],
        out_specs=(vmem, vmem, vmem),
        compiler_params=pltpu.CompilerParams(vmem_limit_bytes=4 * mib),
        name="nodes",
    )(packets)
    return (voxel_stress, homogenized, strain, internal_node_force, tangent)


def solution(mesh):
    in_specs = (
        P("macro", None),
        P("macro", None, None),
        P(),
        P(),
        P(),
        P("macro", "vox", None),
        P("macro", "vox", None),
    )
    out_specs = (
        P("macro", None, "vox", None),
        P("macro", None),
        P("macro", None),
        P("macro", None),
        P("macro", None),
    )
    return jax.shard_map(
        on_device, mesh=mesh, in_specs=in_specs, out_specs=out_specs, check_vma=False
    )
```

```python
import jax
import jax.numpy as jnp
from jax import lax
from jax.experimental import pallas as pl
from jax.experimental.pallas import tpu as pltpu
from jax.sharding import PartitionSpec as P

EDGE = 64
SWEEPS = 3
NEIGHBOUR_SLOTS = 12
BLOCK = NEIGHBOUR_SLOTS * 9

lame_base = 1.5
shear_base = 1.0
yield_ratio = 0.2
precond = 1.0 / 42.0
lower_bound = 0.05
upper_bound = 2.0

ROWS = EDGE * EDGE // 128
WIDE = 256
HALO = 3


def chebyshev_terms(count):
    centre = 0.5 * (upper_bound + lower_bound)
    half_width = 0.5 * (upper_bound - lower_bound)
    ratio_bound = centre / half_width
    rho_prev = 1.0 / ratio_bound
    weights = []
    for number in range(count):
        rho_next = 1.0 / (2.0 * ratio_bound - rho_prev)
        weights.append((rho_next * rho_prev, 2.0 * rho_next / half_width))
        rho_prev = rho_next
    return (centre, weights)


def sweep_polynomial():
    centre, weights = chebyshev_terms(SWEEPS - 1)
    direction = [1.0 / centre]
    result = list(direction)
    for keep, push in weights:
        applied = [1.0] + result
        direction = [
            keep * (direction[k] if k < len(direction) else 0.0) + push * applied[k]
            for k in range(len(applied))
        ]
        result = [(result[k] if k < len(result) else 0.0) + direction[k] for k in range(len(applied))]
    return result


poly0, poly1, poly2 = sweep_polynomial()


def spot(at, jj):
    half = (jj & 1) * 128
    return at, pl.ds(8 * (jj // 2), 8), pl.ds(half, 128)


def load(ref, at, jj):
    return ref[spot(at, jj)]


def load3(refs, at, jj):
    return [load(ref, at, jj) for ref in refs]


def prev_row(ref, at, jj):
    if jj > 0:
        return load(ref, at, jj - 1)
    return pltpu.roll(load(ref, at, 7), 1, 0)


def next_lane(x):
    return pltpu.roll(x, 126, 1)


def prev_lane(x):
    return pltpu.roll(x, 2, 1)


def differences(ref, at, jj):
    here = load(ref, at, jj)
    return (
        here - load(ref, at - 1, jj),
        here - prev_row(ref, at, jj),
        here - prev_lane(here),
    )


def plane_stress(w_refs, at, lame_ref, shear_ref, lame_at, strain):
    ahead = first = load3(w_refs, at, 0)
    for jj in range(8):
        w0, w1, w2 = w = ahead
        ahead = load3(w_refs, at, jj + 1) if jj < 7 else [pltpu.roll(x, 7, 0) for x in first]
        row0, row1, row2 = ahead
        n0, n1, n2 = load3(w_refs, at + 1, jj)
        lane0, lane1, lane2 = [next_lane(x) for x in w]
        lame = load(lame_ref, lame_at, jj)
        shear = load(shear_ref, lame_at, jj)
        e0 = n0 - w0
        e1 = row1 - w1
        e2 = lane2 - w2
        g3 = (lane1 + row2) - (w1 + w2)
        g4 = (lane0 + n2) - (w0 + w2)
        g5 = (row0 + n1) - (w0 + w1)
        if strain is not None:
            e0, e1, e2 = e0 + strain[0], e1 + strain[1], e2 + strain[2]
            g3, g4, g5 = g3 + strain[3], g4 + strain[4], g5 + strain[5]
        bulk = lame * (e0 + e1 + e2)
        twice = shear + shear
        yield jj, w, (
            bulk + twice * e0,
            bulk + twice * e1,
            bulk + twice * e2,
            shear * g3,
            shear * g4,
            shear * g5,
        )


def residual_plane(registers, carry_v):
    begin = None
    row_xy = row_yy = row_yz = None
    for jj, w, stress in registers:
        xx, yy, zz, yz, xz, xy = stress
        pxx, pxz, pxy = [load(carry_v, c, jj) for c in range(3)]
        for c, x in enumerate((xx, xz, xy)):
            carry_v[spot(c, jj)] = x
        r = [
            (xx - pxx) + (xz - prev_lane(xz)) + xy,
            (xy - pxy) + (yz - prev_lane(yz)) + yy,
            (xz - pxz) + (zz - prev_lane(zz)) + yz,
        ]
        if jj == 0:
            begin = w, r
        else:
            yield jj, w, [r[0] - row_xy, r[1] - row_yy, r[2] - row_yz]
        row_xy, row_yy, row_yz = xy, yy, yz
    rows = [pltpu.roll(x, 1, 0) for x in (row_xy, row_yy, row_yz)]
    yield 0, begin[0], [x - y for x, y in zip(begin[1], rows)]


def target_lane(m):
    return ((m >> 6) & 1) * 128 + (m & 63) * 2 + (m >> 7)


def lane_matrix(inverse):
    row = lax.broadcasted_iota(jnp.int32, (WIDE, WIDE), 0)
    column = lax.broadcasted_iota(jnp.int32, (WIDE, WIDE), 1)
    hit = (target_lane(column) == row) if inverse else (target_lane(row) == column)
    return jnp.where(hit, 1.0, 0.0).astype(jnp.bfloat16)


def permute_lanes(x, matrix, terms):
    result = None
    for t in range(terms):
        part = x.astype(jnp.bfloat16)
        moved = jnp.dot(part, matrix, preferred_element_type=jnp.float32)
        result = moved if result is None else result + moved
        if t + 1 < terms:
            x = x - part.astype(jnp.float32)
    return result


def native(plane, q):
    return pl.ds((plane // 8) * (8 * ROWS) + plane % 8 + 8 * q, 8, stride=ROWS)


def total(x):
    return jnp.sum(x, axis=(0, 1), keepdims=True)


def corner_columns(grads):
    corner = lax.broadcasted_iota(jnp.int32, (8, 128), 0)
    columns = []
    for c in range(3):
        column = jnp.full((8, 128), grads[c, 0], jnp.float32)
        for k in range(1, 8):
            column = jnp.where(corner == k, grads[c, k], column)
        columns.append(column)
    return columns


FORCE = BLOCK
SUMS = BLOCK + 4
LAME_MEAN = 120
SHEAR_MEAN = 121


def prepare_kernel(stiff_hbm, mask_hbm, halo_ref, ends_v, mask_v, sems):
    groups = stiff_hbm.shape[0] // (8 * ROWS)
    ends = [pl.ds((groups - 1) * (8 * ROWS), 8 * ROWS), pl.ds(0, 8 * ROWS)]
    copies = []
    for e in range(2):
        copies += [
            pltpu.make_async_copy(stiff_hbm.at[ends[e], :], ends_v.at[e], sems.at[2 * e]),
            pltpu.make_async_copy(mask_hbm.at[ends[e], :], mask_v.at[e], sems.at[2 * e + 1]),
        ]
    for copy in copies:
        copy.start()
    for copy in copies:
        copy.wait()
    row = 0
    for e, first in ((0, 8 - HALO), (1, 0)):
        for field in (ends_v, mask_v):
            for plane in range(first, first + HALO):
                for q in range(4):
                    x = field[e, native(plane, q), :]
                    halo_ref[row : row + 8, :] = x.astype(jnp.float32)
                    row += 8


def material_kernel(
    grads,
    rve_hbm,
    slot_hbm,
    stiff_v,
    mask_v,
    halo_ref,
    lame_ref,
    shear_ref,
    rows_ref,
    stiff_in,
    mask_in,
    rve_element,
    block_slot,
    sems,
):
    copies = [
        pltpu.make_async_copy(rve_hbm, rve_element, sems.at[0]),
        pltpu.make_async_copy(slot_hbm, block_slot, sems.at[1]),
    ]
    for copy in copies:
        copy.start()
    planes = stiff_v.shape[0] // ROWS
    half = planes // 2
    depth = half + 2 * HALO
    matrix = lane_matrix(False)

    for h in range(2):
        for at in range(depth):
            plane = at - HALO + h * half
            for q in range(4):
                if 0 <= plane < planes:
                    stiff = stiff_v[native(plane, q), :]
                    mask = mask_v[native(plane, q), :].astype(jnp.float32)
                else:
                    side, far = (0, plane + HALO) if plane < 0 else (1, plane - planes)
                    base = (side * 2 * HALO + far) * ROWS + 8 * q
                    stiff = halo_ref[base : base + 8, :]
                    mask = halo_ref[base + HALO * ROWS : base + HALO * ROWS + 8, :]
                place = (at, pl.ds(8 * q, 8), pl.ds(128 * h, 128))
                stiff_in[place] = stiff
                mask_in[place] = mask

    acc_l = acc_m = jnp.zeros((8, 128), jnp.float32)
    for first in range(0, depth, 2):
        count = min(2, depth - first)
        shape = (count * ROWS, WIDE)
        stiff = permute_lanes(stiff_in[first : first + count].reshape(shape), matrix, 2)
        mask = permute_lanes(mask_in[first : first + count].reshape(shape), matrix, 1)
        lame = lame_base * stiff
        shear = jnp.where(mask == 1.0, (shear_base * yield_ratio) * stiff, shear_base * stiff)
        lame_ref[first : first + count] = lame.reshape(count, ROWS, WIDE)
        shear_ref[first : first + count] = shear.reshape(count, ROWS, WIDE)
        for u in range(count):
            if HALO <= first + u < HALO + half:
                for jj in range(8):
                    acc_l = acc_l + load(lame_ref, first + u, jj)
                    acc_m = acc_m + load(shear_ref, first + u, jj)
    for copy in copies:
        copy.wait()
    elem = rve_element[lax.axis_index("macro")]

    scale = 1.0 / float(EDGE * EDGE * EDGE)
    lame, shear = total(acc_l) * scale, total(acc_m) * scale
    mine = corner_columns(grads)
    corner = lax.broadcasted_iota(jnp.int32, (8, 128), 0)
    lane = lax.broadcasted_iota(jnp.int32, (8, 128), 1)
    slot_of = jnp.zeros((8, 128), jnp.int32)
    for s in range(1, NEIGHBOUR_SLOTS + 1):
        slot_of = slot_of + jnp.where(lane >= 9 * s, 1, 0)
    inner = lane - 9 * slot_of
    a_of = jnp.where(inner >= 3, 1, 0) + jnp.where(inner >= 6, 1, 0)
    b_of = inner - 3 * a_of

    def by(which, x, y, z):
        return jnp.where(which == 0, x, jnp.where(which == 1, y, z))

    lame_a = lame * by(a_of, *mine)
    shear_b = shear * by(b_of, *mine)
    diagonal = jnp.where(a_of == b_of, shear, 0.0)
    rows = jnp.zeros((8, 128), jnp.float32)
    for l in range(8):
        other = [grads[c, l] for c in range(3)]
        dots = mine[0] * other[0] + mine[1] * other[1] + mine[2] * other[2]
        block = lame_a * by(b_of, *other) + shear_b * by(a_of, *other) + diagonal * dots
        slot = jnp.full((8, 128), block_slot[elem, 0, l], jnp.int32)
        for k in range(1, 8):
            slot = jnp.where(corner == k, block_slot[elem, k, l], slot)
        rows = rows + jnp.where(slot_of == slot, block, 0.0)
    rows = jnp.where(lane == LAME_MEAN, lame, rows)
    rows = jnp.where(lane == SHEAR_MEAN, shear, rows)
    rows_ref[...] = rows


def sweep_kernel(
    grads,
    rve_element,
    connectivity,
    gathered,
    lame_ref,
    shear_ref,
    rows_ref,
    w30_ref,
    w31_ref,
    w32_ref,
    strain_ref,
    strain_out,
    packet_ref,
    w10_v,
    w11_v,
    w12_v,
    w20_v,
    w21_v,
    w22_v,
    carry2_v,
    carry3_v,
):
    half = lame_ref.shape[0] - 2 * HALO
    elem = rve_element[lax.axis_index("macro")]
    nodes = [connectivity[elem, k] for k in range(8)]
    point = lax.axis_index("macro")
    moves = [[gathered[n ^ point, a] for n in nodes] for a in range(3)]

    def dot(c, a):
        result = grads[c, 0] * moves[a][0]
        for k in range(1, 8):
            result = result + grads[c, k] * moves[a][k]
        return result

    strain = [
        dot(0, 0),
        dot(1, 1),
        dot(2, 2),
        dot(2, 1) + dot(1, 2),
        dot(2, 0) + dot(0, 2),
        dot(1, 0) + dot(0, 1),
    ]
    for c in range(6):
        strain_ref[0, c] = strain[c]
        strain_out[8 * c : 8 * c + 8, :] = jnp.full((8, 128), strain[c], jnp.float32)
    w1_v = [w10_v, w11_v, w12_v]
    w2_v = [w20_v, w21_v, w22_v]
    w3_v = [w30_ref, w31_ref, w32_ref]

    strain1 = [poly2 * precond**3 * e for e in strain]
    trace1 = strain1[0] + strain1[1] + strain1[2]
    twice1 = [2.0 * strain1[c] for c in range(3)]
    ratio1 = poly1 / (poly2 * precond)
    ratio0 = poly0 / (poly2 * precond**2)

    def sweep1(at):
        for jj in range(8):
            l0, l1, l2 = differences(lame_ref, at, jj)
            m0, m1, m2 = differences(shear_ref, at, jj)
            w1_v[0][spot(at, jj)] = (
                trace1 * l0 + twice1[0] * m0 + (strain1[5] * m1 + strain1[4] * m2)
            )
            w1_v[1][spot(at, jj)] = (
                trace1 * l1 + twice1[1] * m1 + (strain1[5] * m0 + strain1[3] * m2)
            )
            w1_v[2][spot(at, jj)] = (
                trace1 * l2 + twice1[2] * m2 + (strain1[4] * m0 + strain1[3] * m1)
            )

    def sweep2(at):
        registers = plane_stress(w1_v, at, lame_ref, shear_ref, at, None)
        for jj, w, r in residual_plane(registers, carry2_v):
            for c in range(3):
                w2_v[c][spot(at, jj)] = ratio1 * w[c] + r[c]

    def sweep3(at, place):
        registers = plane_stress(w2_v, at, lame_ref, shear_ref, at, None)
        for jj, _, r in residual_plane(registers, carry3_v):
            for c in range(3):
                w3_v[c][spot(place, jj)] = ratio0 * load(w1_v[c], at, jj) + r[c]

    def by_parts(at):
        bulk, a0, a1, a2, a3, a4, a5 = (jnp.zeros((8, 128), jnp.float32),) * 7
        for jj in range(8):
            w0, w1, w2 = load3(w3_v, at - HALO, jj)
            l0, l1, l2 = differences(lame_ref, at, jj)
            m0, m1, m2 = differences(shear_ref, at, jj)
            bulk = bulk + (l0 * w0 + l1 * w1 + l2 * w2)
            a0 = a0 + m0 * w0
            a1 = a1 + m1 * w1
            a2 = a2 + m2 * w2
            a3 = a3 + (m2 * w1 + m1 * w2)
            a4 = a4 + (m2 * w0 + m0 * w2)
            a5 = a5 + (m1 * w0 + m0 * w1)
        return bulk, a0, a1, a2, a3, a4, a5

    def step(t, acc):
        at = jnp.maximum(t - 4, HALO)
        sums = by_parts(at)
        acc = [x + jnp.where(t - 4 >= HALO, y, 0.0) for x, y in zip(acc, sums)]
        at = jnp.maximum(t - 3, 0)
        sweep3(at, jnp.where(at < HALO, half, at - HALO))
        sweep2(jnp.maximum(t - 1, 0))
        sweep1(jnp.minimum(t + 1, half + 5))
        return tuple(acc)

    zero = jnp.zeros((8, 128), jnp.float32)
    acc = lax.fori_loop(0, half + 7, step, (zero,) * 7)
    scale = 1.0 / float(EDGE * EDGE * EDGE)
    bulk, *parts = [total(x) * scale for x in acc]
    rows = rows_ref[...]
    lame = rows[:1, LAME_MEAN : LAME_MEAN + 1]
    shear = rows[:1, SHEAR_MEAN : SHEAR_MEAN + 1]
    bulk = lame * (strain[0] + strain[1] + strain[2]) - bulk
    means = [bulk + 2.0 * (shear * strain[c] - parts[c]) for c in range(3)]
    means += [shear * strain[c] - parts[c] for c in range(3, 6)]

    xx, yy, zz, yz, xz, xy = means
    g0, g1, g2 = corner_columns(grads)
    lane = lax.broadcasted_iota(jnp.int32, (8, 128), 1)
    rows = jnp.where(lane == FORCE, xx * g0 + xy * g1 + xz * g2, rows)
    rows = jnp.where(lane == FORCE + 1, xy * g0 + yy * g1 + yz * g2, rows)
    rows = jnp.where(lane == FORCE + 2, xz * g0 + yz * g1 + zz * g2, rows)
    sums = jnp.zeros((8, 128), jnp.float32)
    for c in range(6):
        sums = jnp.where(lane == SUMS + c, means[c], sums)
    rows = jnp.where(lane >= SUMS, sums, rows)
    for g in range(packet_ref.shape[0] // 8):
        packet_ref[8 * g : 8 * g + 8, :] = sums
    count = lax.axis_size("macro")
    for v in range(lax.axis_size("vox")):
        for k in range(8):
            packet_ref[pl.ds(v * count + nodes[k], 1), :] = rows[k : k + 1]


def stress_kernel(
    strain_in,
    lame_ref,
    shear_ref,
    w30_ref,
    w31_ref,
    w32_ref,
    stress_ref,
    out_v,
    work_v,
    turn_v,
    sem,
):
    half = lame_ref.shape[0] - 2 * HALO
    w3_v = [w30_ref, w31_ref, w32_ref]
    strain = [strain_in[8 * c : 8 * c + 8, :] for c in range(6)]
    matrix = lane_matrix(True)
    copies = []
    for first in range(0, half, GROUP):
        slot = (first // GROUP) % 2
        for u in range(GROUP):
            at = first + u
            for jj, _, stress in plane_stress(w3_v, at, lame_ref, shear_ref, at + HALO, strain):
                for c in range(6):
                    work_v[(slot, c, u, *spot(0, jj)[1:])] = stress[c]
        for c in range(6):
            y = permute_lanes(work_v[slot, c].reshape(GROUP * ROWS, WIDE), matrix, 2)
            for u in range(GROUP):
                for q in range(4):
                    row = (u * 4 + q) * 8
                    for h in range(2):
                        s = (first + u + h * half) % 8
                        turn_v[h, c, pl.ds(s * TURN_S + q * 8 * TURN_R, 8, stride=TURN_R), :] = y[
                            row : row + 8, 128 * h : 128 * h + 128
                        ]
        done = []
        if half % 8 == 0 and (first + GROUP) % 8 == 0:
            done = [((first + GROUP) // 8 - 1 + h * (half // 8), h) for h in range(2)]
        elif half % 8 and first + GROUP == half:
            done = [(0, None)]
        for group, h in done:
            for c in range(6):
                for q in range(4):
                    for r in range(8):
                        row = group * (8 * ROWS) + (4 * r + q) * 8
                        start = (q * 8 + r) * TURN_R
                        if h is None:
                            low = turn_v[0, c, pl.ds(start, 8, stride=TURN_S), :]
                            high = turn_v[1, c, pl.ds(start, 8, stride=TURN_S), :]
                            sub = lax.broadcasted_iota(jnp.int32, (8, 128), 0)
                            out_v[c, row : row + 8, :] = jnp.where(sub < half, low, high)
                        else:
                            out_v[c, row : row + 8, :] = turn_v[
                                h, c, pl.ds(start, 8, stride=TURN_S), :
                            ]
            span = pl.ds(group * (8 * ROWS), 8 * ROWS)
            copy = pltpu.make_async_copy(
                out_v.at[:, span, :], stress_ref.at[:, span, :], sem.at[len(copies)]
            )
            copy.start()
            copies.append(copy)
    for copy in copies:
        copy.wait()


TURN_R = 3
TURN_S = TURN_R * ROWS + 1
GROUP = 4


def node_kernel(packets_ref, hom_ref, force_ref, tangent_ref):
    packets = packets_ref[...]
    count = lax.axis_size("macro")
    place = lax.broadcasted_iota(jnp.int32, packets.shape, 0)
    point = lax.axis_index("macro")
    own = place == point
    for v in range(1, lax.axis_size("vox")):
        own = own | (place == v * count + point)
    row = jnp.sum(packets, axis=0, keepdims=True)
    means = jnp.sum(jnp.where(own, packets, 0.0), axis=0, keepdims=True)
    tangent_ref[...] = row[:, :BLOCK]
    force_ref[...] = row[:, FORCE : FORCE + 3]
    hom_ref[...] = means[:, SUMS : SUMS + 6]


def gather_by_exchange(x, axis, first):
    size = lax.axis_size(axis)
    assert size & (size - 1) == 0
    while x.shape[0] < size:
        partner = [(i, i ^ x.shape[0]) for i in range(size)]
        if 2 * x.shape[0] == size:
            x = x + 0.0 * first[:1, :1]
        x = jnp.concatenate([x, lax.ppermute(x, axis, partner)], axis=0)
    return x


def on_device(
    nodal_disp,
    weighted_shape_gradients,
    rve_element,
    connectivity,
    block_slot,
    stiffness,
    yielded_mask,
):
    rve_count, planes, plane_size = stiffness.shape
    macro_size = lax.axis_size("macro")
    vox_size = lax.axis_size("vox")
    everywhere = macro_size * vox_size
    assert rve_count == 1 and nodal_disp.shape[0] == 1
    assert planes % 8 == 0 and plane_size == EDGE * EDGE

    def flat(field):
        parted = field.reshape(planes // 8, 8, ROWS, 128)
        return parted.transpose(0, 2, 1, 3).reshape(planes * ROWS, 128)

    smem = pl.BlockSpec(memory_space=pltpu.SMEM)
    vmem = pl.BlockSpec(memory_space=pltpu.VMEM)
    hbm = pl.BlockSpec(memory_space=pltpu.HBM)
    anywhere = pl.BlockSpec(memory_space=pl.ANY)
    mib = 1024 * 1024
    f32 = jnp.float32
    half = planes // 2
    depth = half + 2 * HALO
    packed = 4 * HALO * ROWS
    layer = jax.ShapeDtypeStruct((depth, ROWS, WIDE), f32)
    field = pltpu.VMEM((depth, ROWS, WIDE), f32)
    carry = pltpu.VMEM((3, ROWS, WIDE), f32)
    beyond = pltpu.VMEM((depth + 1, ROWS, WIDE), f32)
    last_layer = jax.ShapeDtypeStruct((half + 1, ROWS, WIDE), f32)

    def cost(flops, size):
        return pl.CostEstimate(
            flops=flops * planes * plane_size,
            bytes_accessed=size * planes * plane_size,
            transcendentals=0,
        )

    rims = pl.pallas_call(
        prepare_kernel,
        out_shape=jax.ShapeDtypeStruct((packed, 128), f32),
        in_specs=[hbm] * 2,
        out_specs=vmem,
        scratch_shapes=[
            pltpu.VMEM((2, 8 * ROWS, 128), f32),
            pltpu.VMEM((2, 8 * ROWS, 128), jnp.int32),
            pltpu.SemaphoreType.DMA((4,)),
        ],
        compiler_params=pltpu.CompilerParams(vmem_limit_bytes=56 * mib),
        cost_estimate=cost(10**4, 1),
        name="prepare",
    )(flat(stiffness), flat(yielded_mask))

    if vox_size == 2:
        halo = lax.ppermute(rims, "vox", [(0, 1), (1, 0)])
    else:
        forward = [(i, (i + 1) % vox_size) for i in range(vox_size)]
        backward = [(t, s) for s, t in forward]
        halo = jnp.concatenate(
            [
                lax.ppermute(rims[: packed // 2], "vox", forward),
                lax.ppermute(rims[packed // 2 :], "vox", backward),
            ],
            axis=0,
        )
    gathered = gather_by_exchange(nodal_disp, "macro", halo)

    grads = weighted_shape_gradients[0]
    lame, shear, rows = pl.pallas_call(
        material_kernel,
        out_shape=(layer, layer, jax.ShapeDtypeStruct((8, 128), f32)),
        in_specs=[smem, hbm, hbm, vmem, vmem, vmem],
        out_specs=(vmem,) * 3,
        scratch_shapes=[
            field,
            field,
            pltpu.SMEM(rve_element.shape, jnp.int32),
            pltpu.SMEM(block_slot.shape, jnp.int32),
            pltpu.SemaphoreType.DMA((2,)),
        ],
        compiler_params=pltpu.CompilerParams(vmem_limit_bytes=8 * mib),
        cost_estimate=cost(10**4, 1),
        name="material",
    )(grads, rve_element, block_slot, flat(stiffness), flat(yielded_mask), halo)

    *w3, strain, strain_rows, packet = pl.pallas_call(
        sweep_kernel,
        out_shape=(
            last_layer,
            last_layer,
            last_layer,
            jax.ShapeDtypeStruct((1, 6), f32),
            jax.ShapeDtypeStruct((48, 128), f32),
            jax.ShapeDtypeStruct((everywhere, 128), f32),
        ),
        in_specs=[smem] * 4 + [vmem] * 3,
        out_specs=(vmem, vmem, vmem, smem, vmem, vmem),
        scratch_shapes=[beyond] * 3 + [field] * 3 + [carry] * 2,
        compiler_params=pltpu.CompilerParams(vmem_limit_bytes=12 * mib),
        cost_estimate=cost(2 * 10**4, 1),
        name="sweeps",
    )(grads, rve_element, connectivity, gathered, lame, shear, rows)

    packets = lax.all_to_all(
        packet, ("vox", "macro"), split_axis=0, concat_axis=0, tiled=True
    )

    stress = pl.pallas_call(
        stress_kernel,
        out_shape=jax.ShapeDtypeStruct((6, planes * ROWS, 128), f32),
        in_specs=[vmem] * 6,
        out_specs=hbm,
        scratch_shapes=[
            pltpu.VMEM((6, planes * ROWS, 128), f32),
            pltpu.VMEM((2, 6, GROUP, ROWS, WIDE), f32),
            pltpu.VMEM((2, 6, 8 * TURN_S, 128), f32),
            pltpu.SemaphoreType.DMA((planes // 8,)),
        ],
        compiler_params=pltpu.CompilerParams(vmem_limit_bytes=16 * mib),
        cost_estimate=cost(10**4, 1),
        name="stress",
    )(strain_rows, lame, shear, *w3)
    voxel_stress = (
        stress.reshape(6, planes // 8, ROWS, 8, 128)
        .transpose(0, 1, 3, 2, 4)
        .reshape(1, 6, planes, plane_size)
    )

    homogenized, internal_node_force, tangent = pl.pallas_call(
        node_kernel,
        out_shape=(
            jax.ShapeDtypeStruct((1, 6), f32),
            jax.ShapeDtypeStruct((1, 3), f32),
            jax.ShapeDtypeStruct((1, BLOCK), f32),
        ),
        in_specs=[vmem],
        out_specs=(vmem, vmem, vmem),
        compiler_params=pltpu.CompilerParams(vmem_limit_bytes=4 * mib),
        name="nodes",
    )(packets)
    return (voxel_stress, homogenized, strain, internal_node_force, tangent)


def solution(mesh):
    in_specs = (
        P("macro", None),
        P("macro", None, None),
        P(),
        P(),
        P(),
        P("macro", "vox", None),
        P("macro", "vox", None),
    )
    out_specs = (
        P("macro", None, "vox", None),
        P("macro", None),
        P("macro", None),
        P("macro", None),
        P("macro", None),
    )
    return jax.shard_map(
        on_device, mesh=mesh, in_specs=in_specs, out_specs=out_specs, check_vma=False
    )
```

```python
import jax
import jax.numpy as jnp
from jax import lax
from jax.experimental import pallas as pl
from jax.experimental.pallas import tpu as pltpu
from jax.sharding import PartitionSpec as P

EDGE = 64
SWEEPS = 3
NEIGHBOUR_SLOTS = 12
BLOCK = NEIGHBOUR_SLOTS * 9

lame_base = 1.5
shear_base = 1.0
yield_ratio = 0.2
precond = 1.0 / 42.0
lower_bound = 0.05
upper_bound = 2.0

ROWS = EDGE * EDGE // 128
WIDE = 256
HALO = 3


def chebyshev_terms(count):
    centre = 0.5 * (upper_bound + lower_bound)
    half_width = 0.5 * (upper_bound - lower_bound)
    ratio_bound = centre / half_width
    rho_prev = 1.0 / ratio_bound
    weights = []
    for number in range(count):
        rho_next = 1.0 / (2.0 * ratio_bound - rho_prev)
        weights.append((rho_next * rho_prev, 2.0 * rho_next / half_width))
        rho_prev = rho_next
    return (centre, weights)


def sweep_polynomial():
    centre, weights = chebyshev_terms(SWEEPS - 1)
    direction = [1.0 / centre]
    result = list(direction)
    for keep, push in weights:
        applied = [1.0] + result
        direction = [
            keep * (direction[k] if k < len(direction) else 0.0) + push * applied[k]
            for k in range(len(applied))
        ]
        result = [(result[k] if k < len(result) else 0.0) + direction[k] for k in range(len(applied))]
    return result


poly0, poly1, poly2 = sweep_polynomial()


def spot(at, jj):
    half = (jj & 1) * 128
    return at, pl.ds(8 * (jj // 2), 8), pl.ds(half, 128)


def load(ref, at, jj):
    return ref[spot(at, jj)]


def load3(refs, at, jj):
    return [load(ref, at, jj) for ref in refs]


def prev_row(ref, at, jj):
    if jj > 0:
        return load(ref, at, jj - 1)
    return pltpu.roll(load(ref, at, 7), 1, 0)


def next_lane(x):
    return pltpu.roll(x, 126, 1)


def prev_lane(x):
    return pltpu.roll(x, 2, 1)


def differences(ref, lane_ref, at, jj, known):
    here = load(ref, at, jj)
    if known:
        along = load(lane_ref, at, jj)
    else:
        along = here - prev_lane(here)
        lane_ref[spot(at, jj)] = along
    return here - load(ref, at - 1, jj), here - prev_row(ref, at, jj), along


def plane_stress(w_refs, at, lame_ref, shear_ref, lame_at, strain):
    ahead = first = load3(w_refs, at, 0)
    for jj in range(8):
        w0, w1, w2 = w = ahead
        ahead = load3(w_refs, at, jj + 1) if jj < 7 else [pltpu.roll(x, 7, 0) for x in first]
        row0, row1, row2 = ahead
        n0, n1, n2 = load3(w_refs, at + 1, jj)
        lane0, lane1, lane2 = [next_lane(x) for x in w]
        lame = load(lame_ref, lame_at, jj)
        shear = load(shear_ref, lame_at, jj)
        e0 = n0 - w0
        e1 = row1 - w1
        e2 = lane2 - w2
        g3 = (lane1 + row2) - (w1 + w2)
        g4 = (lane0 + n2) - (w0 + w2)
        g5 = (row0 + n1) - (w0 + w1)
        if strain is not None:
            e0, e1, e2 = e0 + strain[0], e1 + strain[1], e2 + strain[2]
            g3, g4, g5 = g3 + strain[3], g4 + strain[4], g5 + strain[5]
        bulk = lame * (e0 + e1 + e2)
        twice = shear + shear
        yield jj, w, (
            bulk + twice * e0,
            bulk + twice * e1,
            bulk + twice * e2,
            shear * g3,
            shear * g4,
            shear * g5,
        )


def residual_plane(registers, carry_v):
    begin = None
    row_xy = row_yy = row_yz = None
    for jj, w, stress in registers:
        xx, yy, zz, yz, xz, xy = stress
        pxx, pxz, pxy = [load(carry_v, c, jj) for c in range(3)]
        for c, x in enumerate((xx, xz, xy)):
            carry_v[spot(c, jj)] = x
        r = [
            (xx - pxx) + (xz - prev_lane(xz)) + xy,
            (xy - pxy) + (yz - prev_lane(yz)) + yy,
            (xz - pxz) + (zz - prev_lane(zz)) + yz,
        ]
        if jj == 0:
            begin = w, r
        else:
            yield jj, w, [r[0] - row_xy, r[1] - row_yy, r[2] - row_yz]
        row_xy, row_yy, row_yz = xy, yy, yz
    rows = [pltpu.roll(x, 1, 0) for x in (row_xy, row_yy, row_yz)]
    yield 0, begin[0], [x - y for x, y in zip(begin[1], rows)]


def target_lane(m):
    return ((m >> 6) & 1) * 128 + (m & 63) * 2 + (m >> 7)


def lane_matrix(inverse):
    row = lax.broadcasted_iota(jnp.int32, (WIDE, WIDE), 0)
    column = lax.broadcasted_iota(jnp.int32, (WIDE, WIDE), 1)
    hit = (target_lane(column) == row) if inverse else (target_lane(row) == column)
    return jnp.where(hit, 1.0, 0.0).astype(jnp.bfloat16)


def permute_lanes(x, matrix, terms):
    result = None
    for t in range(terms):
        part = x.astype(jnp.bfloat16)
        moved = jnp.dot(part, matrix, preferred_element_type=jnp.float32)
        result = moved if result is None else result + moved
        if t + 1 < terms:
            x = x - part.astype(jnp.float32)
    return result


def native(plane, q):
    return pl.ds((plane // 8) * (8 * ROWS) + plane % 8 + 8 * q, 8, stride=ROWS)


def total(x):
    return jnp.sum(x, axis=(0, 1), keepdims=True)


def corner_columns(grads):
    corner = lax.broadcasted_iota(jnp.int32, (8, 128), 0)
    columns = []
    for c in range(3):
        column = jnp.full((8, 128), grads[c, 0], jnp.float32)
        for k in range(1, 8):
            column = jnp.where(corner == k, grads[c, k], column)
        columns.append(column)
    return columns


FORCE = BLOCK
SUMS = BLOCK + 4
LAME_MEAN = 120
SHEAR_MEAN = 121


def prepare_kernel(disp_hbm, stiff_hbm, mask_hbm, disp_ref, halo_ref, disp_v, ends_v, mask_v, sems):
    groups = stiff_hbm.shape[0] // (8 * ROWS)
    ends = [pl.ds((groups - 1) * (8 * ROWS), 8 * ROWS), pl.ds(0, 8 * ROWS)]
    copies = [pltpu.make_async_copy(disp_hbm, disp_v, sems.at[0])]
    for e in range(2):
        copies += [
            pltpu.make_async_copy(stiff_hbm.at[ends[e], :], ends_v.at[e], sems.at[1 + 2 * e]),
            pltpu.make_async_copy(mask_hbm.at[ends[e], :], mask_v.at[e], sems.at[2 + 2 * e]),
        ]
    for copy in copies:
        copy.start()
    for copy in copies:
        copy.wait()
    disp_ref[...] = jnp.broadcast_to(disp_v[...], disp_ref.shape)
    row = 0
    for e, first in ((0, 8 - HALO), (1, 0)):
        for field in (ends_v, mask_v):
            for plane in range(first, first + HALO):
                for q in range(4):
                    x = field[e, native(plane, q), :]
                    halo_ref[row : row + 8, :] = x.astype(jnp.float32)
                    row += 8


def material_kernel(
    grads,
    rve_hbm,
    slot_hbm,
    stiff_v,
    mask_v,
    halo_ref,
    lame_ref,
    shear_ref,
    rows_ref,
    stiff_in,
    mask_in,
    rve_element,
    block_slot,
    sems,
):
    copies = [
        pltpu.make_async_copy(rve_hbm, rve_element, sems.at[0]),
        pltpu.make_async_copy(slot_hbm, block_slot, sems.at[1]),
    ]
    for copy in copies:
        copy.start()
    planes = stiff_v.shape[0] // ROWS
    half = planes // 2
    depth = half + 2 * HALO
    matrix = lane_matrix(False)

    for h in range(2):
        for at in range(depth):
            plane = at - HALO + h * half
            for q in range(4):
                if 0 <= plane < planes:
                    stiff = stiff_v[native(plane, q), :]
                    mask = mask_v[native(plane, q), :].astype(jnp.float32)
                else:
                    side, far = (0, plane + HALO) if plane < 0 else (1, plane - planes)
                    base = (side * 2 * HALO + far) * ROWS + 8 * q
                    stiff = halo_ref[base : base + 8, :]
                    mask = halo_ref[base + HALO * ROWS : base + HALO * ROWS + 8, :]
                place = (at, pl.ds(8 * q, 8), pl.ds(128 * h, 128))
                stiff_in[place] = stiff
                mask_in[place] = mask

    acc_l = acc_m = jnp.zeros((8, 128), jnp.float32)
    for first in range(0, depth, 2):
        count = min(2, depth - first)
        shape = (count * ROWS, WIDE)
        stiff = permute_lanes(stiff_in[first : first + count].reshape(shape), matrix, 2)
        mask = permute_lanes(mask_in[first : first + count].reshape(shape), matrix, 1)
        lame = lame_base * stiff
        shear = jnp.where(mask == 1.0, (shear_base * yield_ratio) * stiff, shear_base * stiff)
        lame_ref[first : first + count] = lame.reshape(count, ROWS, WIDE)
        shear_ref[first : first + count] = shear.reshape(count, ROWS, WIDE)
        for u in range(count):
            if HALO <= first + u < HALO + half:
                for jj in range(8):
                    acc_l = acc_l + load(lame_ref, first + u, jj)
                    acc_m = acc_m + load(shear_ref, first + u, jj)
    for copy in copies:
        copy.wait()
    elem = rve_element[lax.axis_index("macro")]

    scale = 1.0 / float(EDGE * EDGE * EDGE)
    lame, shear = total(acc_l) * scale, total(acc_m) * scale
    mine = corner_columns(grads)
    corner = lax.broadcasted_iota(jnp.int32, (8, 128), 0)
    lane = lax.broadcasted_iota(jnp.int32, (8, 128), 1)
    slot_of = jnp.zeros((8, 128), jnp.int32)
    for s in range(1, NEIGHBOUR_SLOTS + 1):
        slot_of = slot_of + jnp.where(lane >= 9 * s, 1, 0)
    inner = lane - 9 * slot_of
    a_of = jnp.where(inner >= 3, 1, 0) + jnp.where(inner >= 6, 1, 0)
    b_of = inner - 3 * a_of

    def by(which, x, y, z):
        return jnp.where(which == 0, x, jnp.where(which == 1, y, z))

    lame_a = lame * by(a_of, *mine)
    shear_b = shear * by(b_of, *mine)
    diagonal = jnp.where(a_of == b_of, shear, 0.0)
    rows = jnp.zeros((8, 128), jnp.float32)
    for l in range(8):
        other = [grads[c, l] for c in range(3)]
        dots = mine[0] * other[0] + mine[1] * other[1] + mine[2] * other[2]
        block = lame_a * by(b_of, *other) + shear_b * by(a_of, *other) + diagonal * dots
        slot = jnp.full((8, 128), block_slot[elem, 0, l], jnp.int32)
        for k in range(1, 8):
            slot = jnp.where(corner == k, block_slot[elem, k, l], slot)
        rows = rows + jnp.where(slot_of == slot, block, 0.0)
    rows = jnp.where(lane == LAME_MEAN, lame, rows)
    rows = jnp.where(lane == SHEAR_MEAN, shear, rows)
    rows_ref[...] = rows


def sweep_kernel(
    grads,
    rve_element,
    connectivity,
    gathered,
    lame_ref,
    shear_ref,
    rows_ref,
    w30_ref,
    w31_ref,
    w32_ref,
    strain_ref,
    strain_out,
    packet_ref,
    w10_v,
    w11_v,
    w12_v,
    w20_v,
    w21_v,
    w22_v,
    dlame_v,
    dshear_v,
    carry2_v,
    carry3_v,
):
    half = lame_ref.shape[0] - 2 * HALO
    elem = rve_element[lax.axis_index("macro")]
    nodes = [connectivity[elem, k] for k in range(8)]
    moves = [[gathered[n, a] for n in nodes] for a in range(3)]

    def dot(c, a):
        result = grads[c, 0] * moves[a][0]
        for k in range(1, 8):
            result = result + grads[c, k] * moves[a][k]
        return result

    strain = [
        dot(0, 0),
        dot(1, 1),
        dot(2, 2),
        dot(2, 1) + dot(1, 2),
        dot(2, 0) + dot(0, 2),
        dot(1, 0) + dot(0, 1),
    ]
    for c in range(6):
        strain_ref[0, c] = strain[c]
        strain_out[8 * c : 8 * c + 8, :] = jnp.full((8, 128), strain[c], jnp.float32)
    w1_v = [w10_v, w11_v, w12_v]
    w2_v = [w20_v, w21_v, w22_v]
    w3_v = [w30_ref, w31_ref, w32_ref]

    strain1 = [poly2 * precond**3 * e for e in strain]
    trace1 = strain1[0] + strain1[1] + strain1[2]
    twice1 = [2.0 * strain1[c] for c in range(3)]
    ratio1 = poly1 / (poly2 * precond)
    ratio0 = poly0 / (poly2 * precond**2)

    def sweep1(at):
        for jj in range(8):
            l0, l1, l2 = differences(lame_ref, dlame_v, at, jj, False)
            m0, m1, m2 = differences(shear_ref, dshear_v, at, jj, False)
            w1_v[0][spot(at, jj)] = (
                trace1 * l0 + twice1[0] * m0 + (strain1[5] * m1 + strain1[4] * m2)
            )
            w1_v[1][spot(at, jj)] = (
                trace1 * l1 + twice1[1] * m1 + (strain1[5] * m0 + strain1[3] * m2)
            )
            w1_v[2][spot(at, jj)] = (
                trace1 * l2 + twice1[2] * m2 + (strain1[4] * m0 + strain1[3] * m1)
            )

    def sweep2(at):
        registers = plane_stress(w1_v, at, lame_ref, shear_ref, at, None)
        for jj, w, r in residual_plane(registers, carry2_v):
            for c in range(3):
                w2_v[c][spot(at, jj)] = ratio1 * w[c] + r[c]

    def sweep3(at, place):
        registers = plane_stress(w2_v, at, lame_ref, shear_ref, at, None)
        for jj, _, r in residual_plane(registers, carry3_v):
            for c in range(3):
                w3_v[c][spot(place, jj)] = ratio0 * load(w1_v[c], at, jj) + r[c]

    def by_parts(at):
        bulk, a0, a1, a2, a3, a4, a5 = (jnp.zeros((8, 128), jnp.float32),) * 7
        for jj in range(8):
            w0, w1, w2 = load3(w3_v, at - HALO, jj)
            l0, l1, l2 = differences(lame_ref, dlame_v, at, jj, True)
            m0, m1, m2 = differences(shear_ref, dshear_v, at, jj, True)
            bulk = bulk + (l0 * w0 + l1 * w1 + l2 * w2)
            a0 = a0 + m0 * w0
            a1 = a1 + m1 * w1
            a2 = a2 + m2 * w2
            a3 = a3 + (m2 * w1 + m1 * w2)
            a4 = a4 + (m2 * w0 + m0 * w2)
            a5 = a5 + (m1 * w0 + m0 * w1)
        return bulk, a0, a1, a2, a3, a4, a5

    def step(t, acc):
        at = jnp.maximum(t - 4, HALO)
        sums = by_parts(at)
        acc = [x + jnp.where(t - 4 >= HALO, y, 0.0) for x, y in zip(acc, sums)]
        at = jnp.maximum(t - 3, 0)
        sweep3(at, jnp.where(at < HALO, half, at - HALO))
        sweep2(jnp.maximum(t - 1, 0))
        sweep1(jnp.minimum(t + 1, half + 5))
        return tuple(acc)

    zero = jnp.zeros((8, 128), jnp.float32)
    acc = lax.fori_loop(0, half + 7, step, (zero,) * 7)
    scale = 1.0 / float(EDGE * EDGE * EDGE)
    bulk, *parts = [total(x) * scale for x in acc]
    rows = rows_ref[...]
    lame = rows[:1, LAME_MEAN : LAME_MEAN + 1]
    shear = rows[:1, SHEAR_MEAN : SHEAR_MEAN + 1]
    bulk = lame * (strain[0] + strain[1] + strain[2]) - bulk
    means = [bulk + 2.0 * (shear * strain[c] - parts[c]) for c in range(3)]
    means += [shear * strain[c] - parts[c] for c in range(3, 6)]

    xx, yy, zz, yz, xz, xy = means
    g0, g1, g2 = corner_columns(grads)
    lane = lax.broadcasted_iota(jnp.int32, (8, 128), 1)
    rows = jnp.where(lane == FORCE, xx * g0 + xy * g1 + xz * g2, rows)
    rows = jnp.where(lane == FORCE + 1, xy * g0 + yy * g1 + yz * g2, rows)
    rows = jnp.where(lane == FORCE + 2, xz * g0 + yz * g1 + zz * g2, rows)
    sums = jnp.zeros((8, 128), jnp.float32)
    for c in range(6):
        sums = jnp.where(lane == SUMS + c, means[c], sums)
    rows = jnp.where(lane >= SUMS, sums, rows)
    for g in range(packet_ref.shape[0] // 8):
        packet_ref[8 * g : 8 * g + 8, :] = sums
    count = lax.axis_size("macro")
    for v in range(lax.axis_size("vox")):
        for k in range(8):
            packet_ref[pl.ds(v * count + nodes[k], 1), :] = rows[k : k + 1]


def stress_kernel(
    strain_in,
    lame_ref,
    shear_ref,
    w30_ref,
    w31_ref,
    w32_ref,
    stress_ref,
    out_v,
    work_v,
    turn_v,
    sem,
):
    half = lame_ref.shape[0] - 2 * HALO
    w3_v = [w30_ref, w31_ref, w32_ref]
    strain = [strain_in[8 * c : 8 * c + 8, :] for c in range(6)]
    matrix = lane_matrix(True)
    copies = []
    for first in range(0, half, GROUP):
        slot = (first // GROUP) % 2
        for u in range(GROUP):
            at = first + u
            for jj, _, stress in plane_stress(w3_v, at, lame_ref, shear_ref, at + HALO, strain):
                for c in range(6):
                    work_v[(slot, c, u, *spot(0, jj)[1:])] = stress[c]
        for c in range(6):
            y = permute_lanes(work_v[slot, c].reshape(GROUP * ROWS, WIDE), matrix, 2)
            for u in range(GROUP):
                for q in range(4):
                    row = (u * 4 + q) * 8
                    for h in range(2):
                        s = (first + u + h * half) % 8
                        turn_v[h, c, pl.ds(s * TURN_S + q * 8 * TURN_R, 8, stride=TURN_R), :] = y[
                            row : row + 8, 128 * h : 128 * h + 128
                        ]
        done = []
        if half % 8 == 0 and (first + GROUP) % 8 == 0:
            done = [((first + GROUP) // 8 - 1 + h * (half // 8), h) for h in range(2)]
        elif half % 8 and first + GROUP == half:
            done = [(0, None)]
        for group, h in done:
            for c in range(6):
                for q in range(4):
                    for r in range(8):
                        row = group * (8 * ROWS) + (4 * r + q) * 8
                        start = (q * 8 + r) * TURN_R
                        if h is None:
                            low = turn_v[0, c, pl.ds(start, 8, stride=TURN_S), :]
                            high = turn_v[1, c, pl.ds(start, 8, stride=TURN_S), :]
                            sub = lax.broadcasted_iota(jnp.int32, (8, 128), 0)
                            out_v[c, row : row + 8, :] = jnp.where(sub < half, low, high)
                        else:
                            out_v[c, row : row + 8, :] = turn_v[
                                h, c, pl.ds(start, 8, stride=TURN_S), :
                            ]
            span = pl.ds(group * (8 * ROWS), 8 * ROWS)
            copy = pltpu.make_async_copy(
                out_v.at[:, span, :], stress_ref.at[:, span, :], sem.at[len(copies)]
            )
            copy.start()
            copies.append(copy)
    for copy in copies:
        copy.wait()


TURN_R = 3
TURN_S = TURN_R * ROWS + 1
GROUP = 4


def node_kernel(packets_ref, hom_ref, force_ref, tangent_ref):
    packets = packets_ref[...]
    count = lax.axis_size("macro")
    place = lax.broadcasted_iota(jnp.int32, packets.shape, 0)
    point = lax.axis_index("macro")
    own = place == point
    for v in range(1, lax.axis_size("vox")):
        own = own | (place == v * count + point)
    row = jnp.sum(packets, axis=0, keepdims=True)
    means = jnp.sum(jnp.where(own, packets, 0.0), axis=0, keepdims=True)
    tangent_ref[...] = row[:, :BLOCK]
    force_ref[...] = row[:, FORCE : FORCE + 3]
    hom_ref[...] = means[:, SUMS : SUMS + 6]


def on_device(
    nodal_disp,
    weighted_shape_gradients,
    rve_element,
    connectivity,
    block_slot,
    stiffness,
    yielded_mask,
):
    rve_count, planes, plane_size = stiffness.shape
    macro_size = lax.axis_size("macro")
    vox_size = lax.axis_size("vox")
    everywhere = macro_size * vox_size
    assert rve_count == 1 and nodal_disp.shape[0] == 1
    assert planes % 8 == 0 and plane_size == EDGE * EDGE

    def flat(field):
        parted = field.reshape(planes // 8, 8, ROWS, 128)
        return parted.transpose(0, 2, 1, 3).reshape(planes * ROWS, 128)

    smem = pl.BlockSpec(memory_space=pltpu.SMEM)
    vmem = pl.BlockSpec(memory_space=pltpu.VMEM)
    hbm = pl.BlockSpec(memory_space=pltpu.HBM)
    anywhere = pl.BlockSpec(memory_space=pl.ANY)
    mib = 1024 * 1024
    f32 = jnp.float32
    half = planes // 2
    depth = half + 2 * HALO
    packed = 4 * HALO * ROWS
    layer = jax.ShapeDtypeStruct((depth, ROWS, WIDE), f32)
    field = pltpu.VMEM((depth, ROWS, WIDE), f32)
    carry = pltpu.VMEM((3, ROWS, WIDE), f32)
    beyond = pltpu.VMEM((depth + 1, ROWS, WIDE), f32)
    last_layer = jax.ShapeDtypeStruct((half + 1, ROWS, WIDE), f32)

    def cost(flops, size):
        return pl.CostEstimate(
            flops=flops * planes * plane_size,
            bytes_accessed=size * planes * plane_size,
            transcendentals=0,
        )

    disp, rims = pl.pallas_call(
        prepare_kernel,
        out_shape=(
            jax.ShapeDtypeStruct((macro_size, 3), f32),
            jax.ShapeDtypeStruct((packed, 128), f32),
        ),
        in_specs=[hbm] * 3,
        out_specs=(vmem,) * 2,
        scratch_shapes=[
            pltpu.VMEM((1, 3), f32),
            pltpu.VMEM((2, 8 * ROWS, 128), f32),
            pltpu.VMEM((2, 8 * ROWS, 128), jnp.int32),
            pltpu.SemaphoreType.DMA((5,)),
        ],
        compiler_params=pltpu.CompilerParams(vmem_limit_bytes=56 * mib),
        cost_estimate=cost(10**4, 1),
        name="prepare",
    )(nodal_disp, flat(stiffness), flat(yielded_mask))

    if vox_size == 2:
        halo = lax.ppermute(rims, "vox", [(0, 1), (1, 0)])
    else:
        forward = [(i, (i + 1) % vox_size) for i in range(vox_size)]
        backward = [(t, s) for s, t in forward]
        halo = jnp.concatenate(
            [
                lax.ppermute(rims[: packed // 2], "vox", forward),
                lax.ppermute(rims[packed // 2 :], "vox", backward),
            ],
            axis=0,
        )
    gathered = lax.all_to_all(disp, "macro", split_axis=0, concat_axis=0, tiled=True)

    grads = weighted_shape_gradients[0]
    lame, shear, rows = pl.pallas_call(
        material_kernel,
        out_shape=(layer, layer, jax.ShapeDtypeStruct((8, 128), f32)),
        in_specs=[smem, hbm, hbm, vmem, vmem, vmem],
        out_specs=(vmem,) * 3,
        scratch_shapes=[
            field,
            field,
            pltpu.SMEM(rve_element.shape, jnp.int32),
            pltpu.SMEM(block_slot.shape, jnp.int32),
            pltpu.SemaphoreType.DMA((2,)),
        ],
        compiler_params=pltpu.CompilerParams(vmem_limit_bytes=8 * mib),
        cost_estimate=cost(10**4, 1),
        name="material",
    )(grads, rve_element, block_slot, flat(stiffness), flat(yielded_mask), halo)

    *w3, strain, strain_rows, packet = pl.pallas_call(
        sweep_kernel,
        out_shape=(
            last_layer,
            last_layer,
            last_layer,
            jax.ShapeDtypeStruct((1, 6), f32),
            jax.ShapeDtypeStruct((48, 128), f32),
            jax.ShapeDtypeStruct((everywhere, 128), f32),
        ),
        in_specs=[smem] * 4 + [vmem] * 3,
        out_specs=(vmem, vmem, vmem, smem, vmem, vmem),
        scratch_shapes=[beyond] * 3 + [field] * 5 + [carry] * 2,
        compiler_params=pltpu.CompilerParams(vmem_limit_bytes=12 * mib),
        cost_estimate=cost(2 * 10**4, 1),
        name="sweeps",
    )(grads, rve_element, connectivity, gathered, lame, shear, rows)

    packets = lax.all_to_all(
        packet, ("vox", "macro"), split_axis=0, concat_axis=0, tiled=True
    )

    stress = pl.pallas_call(
        stress_kernel,
        out_shape=jax.ShapeDtypeStruct((6, planes * ROWS, 128), f32),
        in_specs=[vmem] * 6,
        out_specs=hbm,
        scratch_shapes=[
            pltpu.VMEM((6, planes * ROWS, 128), f32),
            pltpu.VMEM((2, 6, GROUP, ROWS, WIDE), f32),
            pltpu.VMEM((2, 6, 8 * TURN_S, 128), f32),
            pltpu.SemaphoreType.DMA((planes // 8,)),
        ],
        compiler_params=pltpu.CompilerParams(vmem_limit_bytes=16 * mib),
        cost_estimate=cost(10**4, 1),
        name="stress",
    )(strain_rows, lame, shear, *w3)
    voxel_stress = (
        stress.reshape(6, planes // 8, ROWS, 8, 128)
        .transpose(0, 1, 3, 2, 4)
        .reshape(1, 6, planes, plane_size)
    )

    homogenized, internal_node_force, tangent = pl.pallas_call(
        node_kernel,
        out_shape=(
            jax.ShapeDtypeStruct((1, 6), f32),
            jax.ShapeDtypeStruct((1, 3), f32),
            jax.ShapeDtypeStruct((1, BLOCK), f32),
        ),
        in_specs=[vmem],
        out_specs=(vmem, vmem, vmem),
        compiler_params=pltpu.CompilerParams(vmem_limit_bytes=4 * mib),
        name="nodes",
    )(packets)
    return (voxel_stress, homogenized, strain, internal_node_force, tangent)


def solution(mesh):
    in_specs = (
        P("macro", None),
        P("macro", None, None),
        P(),
        P(),
        P(),
        P("macro", "vox", None),
        P("macro", "vox", None),
    )
    out_specs = (
        P("macro", None, "vox", None),
        P("macro", None),
        P("macro", None),
        P("macro", None),
        P("macro", None),
    )
    return jax.shard_map(
        on_device, mesh=mesh, in_specs=in_specs, out_specs=out_specs, check_vma=False
    )
```
